32 devices in a mesh: dp: 8 (over z, core), tp: 4 (over y, x).
Axes of the slice: x: 2, y: 2, z: 4, core: 2. Of those that a mesh axis runs over, the one named last changes fastest.
Arguments:
- tokens: bfloat16 [8192, 2048], P('dp'), may hold values from -6 to 6
- cotangent: bfloat16 [8192, 2048], P('dp'), may hold values from -6 to 6
- span_order: int32 [16], replicated, may hold values from 0 to 15, as said below
- w_query: bfloat16 [2048, 2048], P('dp', 'tp'), may hold values from -0.125 to 0.125
- w_keyval: bfloat16 [2048, 1024], P('dp', 'tp'), may hold values from -0.125 to 0.125
- w_output: bfloat16 [2048, 2048], P('tp', 'dp'), may hold values from -2 to 2
- w_gateup: bfloat16 [2, 2048, 8192], P(None, 'dp', 'tp'), may hold values from -0.125 to 0.125
- w_down: bfloat16 [8192, 2048], P('tp', 'dp'), may hold values from -0.0625 to 0.0625
- norm_gains: bfloat16 [2, 2048], P(None, 'dp'), may hold values from 0.5 to 1.5
- mean_query: float32 [2048, 2048], P('dp', 'tp'), may hold values from -28 to 28
- square_query: float32 [2048, 2048], P('dp', 'tp'), may hold values from 81.92 to 327.68
- mean_keyval: float32 [2048, 1024], P('dp', 'tp'), may hold values from -28 to 28
- square_keyval: float32 [2048, 1024], P('dp', 'tp'), may hold values from 409.6 to 13107.2
- mean_output: float32 [2048, 2048], P('tp', 'dp'), may hold values from -28 to 28
- square_output: float32 [2048, 2048], P('tp', 'dp'), may hold values from 81.92 to 327.68
- mean_gateup: float32 [2, 2048, 8192], P(None, 'dp', 'tp'), may hold values from -28 to 28
- square_gateup: float32 [2, 2048, 8192], P(None, 'dp', 'tp'), may hold values from 81.92 to 327.68
- mean_down: float32 [8192, 2048], P('tp', 'dp'), may hold values from -28 to 28
- square_down: float32 [8192, 2048], P('tp', 'dp'), may hold values from 81.92 to 327.68
- mean_gains: float32 [2, 2048], P(None, 'dp'), may hold values from -28 to 28
- square_gains: float32 [2, 2048], P(None, 'dp'), may hold values from 81.92 to 327.68
Outputs:
- block_output: bfloat16 [8192, 2048], P('dp')
- grad_tokens: float32 [8192, 2048], P('dp')
- grad_query: float32 [2048, 2048], P('dp', 'tp')
- moment_query: float32 [2048, 2048], P('dp', 'tp')
- spread_query: float32 [2048, 2048], P('dp', 'tp')
- update_query: float32 [2048, 2048], P('dp', 'tp')
- grad_keyval: float32 [2048, 1024], P('dp', 'tp')
- moment_keyval: float32 [2048, 1024], P('dp', 'tp')
- spread_keyval: float32 [2048, 1024], P('dp', 'tp')
- update_keyval: float32 [2048, 1024], P('dp', 'tp')
- grad_output: float32 [2048, 2048], P('tp', 'dp')
- moment_output: float32 [2048, 2048], P('tp', 'dp')
- spread_output: float32 [2048, 2048], P('tp', 'dp')
- update_output: float32 [2048, 2048], P('tp', 'dp')
- grad_gateup: float32 [2, 2048, 8192], P(None, 'dp', 'tp')
- moment_gateup: float32 [2, 2048, 8192], P(None, 'dp', 'tp')
- spread_gateup: float32 [2, 2048, 8192], P(None, 'dp', 'tp')
- update_gateup: float32 [2, 2048, 8192], P(None, 'dp', 'tp')
- grad_down: float32 [8192, 2048], P('tp', 'dp')
- moment_down: float32 [8192, 2048], P('tp', 'dp')
- spread_down: float32 [8192, 2048], P('tp', 'dp')
- update_down: float32 [8192, 2048], P('tp', 'dp')
- grad_gains: float32 [2, 2048], P(None, 'dp')
- moment_gains: float32 [2, 2048], P(None, 'dp')
- spread_gains: float32 [2, 2048], P(None, 'dp')
- update_gains: float32 [2, 2048], P(None, 'dp')
The draws below stay inside these ranges and needn't reach their ends.
Inputs may be any that keep to these rules, and one draw needn't show every extreme that they name: `span_order`: every span number occurs once; entries 2 i and 2 i + 1 are the spans held by index i of dp in every sequence, and they sum to 15.
All inputs are finite; a program needn't handle non-finite values.
Results may differ from the reference program's by a relative error of at most 0.024.
Values may be sent and summed in bfloat16 or wider, within the bound.
A program may use at most 384 MiB of HBM per device.

```python
import math
import jax
import jax.numpy as jnp
from jax import lax

D = 2048
H = 32
KV = 8
HD = 64
FF = 8192
CH = 64
SEQS = 4
MICRO = 2
STEP = 5
SPANS = 16
SEQ_LEN = 1024
TOKENS = 8192
N_DP = 8


def draw_span_order(key, part):
    half_count = SPANS // 2
    shuffled = jax.random.permutation(key, jnp.arange(half_count, dtype=jnp.int32)).astype(jnp.int32)
    mirrored = (SPANS - 1 - shuffled).astype(jnp.int32)
    return jnp.stack([shuffled, mirrored], axis=1).reshape(-1).astype(jnp.int32)


def block_levels(own_key, shape, pieces, low, largest):
    factor_of = 1.0
    for dim, parts in pieces:
        heights = jax.random.uniform(jax.random.fold_in(jax.random.fold_in(own_key, 6), dim), (parts,), jnp.float32, low / len(pieces), largest / len(pieces))
        factor_of = factor_of * jnp.repeat(jnp.exp(heights), shape[dim] // parts).reshape((-1,) + (1,) * (len(shape) - 1 - dim))
    return factor_of


def noise(own_key, extent, deviation, limit, shards=(), kind=jnp.bfloat16):
    result = deviation * jax.random.normal(own_key, extent, jnp.float32)
    if shards:
        result = result * block_levels(own_key, extent, shards, -0.22, 0.18)
    return jnp.clip(result, -limit, limit).astype(kind)


def setup_inputs(seed: int = 0) -> dict:
    key_list = jax.random.split(jax.random.key(seed), 22)
    tokens = noise(key_list[0], (TOKENS, D), 1.0, 6.0, ((0, 8),))
    cotangent = noise(key_list[1], (TOKENS, D), 1.0, 6.0, ((0, 8),))
    span_order = draw_span_order(jax.random.fold_in(key_list[21], 71), 0)
    w_query = noise(key_list[3], (D, H * HD), D ** -0.5, 0.125, ((0, 8), (1, 4)))
    w_keyval = noise(key_list[4], (D, 2 * KV * HD), D ** -0.5, 0.125, ((0, 8), (1, 4)))
    w_output = noise(key_list[5], (H * HD, D), (max(1, 4 * H * HD // SEQ_LEN)) ** -0.5, 2.0, ((0, 4), (1, 8)))
    w_gateup = noise(key_list[6], (2, D, FF), D ** -0.5, 0.125, ((1, 8), (2, 4)))
    w_down = noise(key_list[7], (FF, D), FF ** -0.5, 0.0625, ((0, 4), (1, 8)))
    norm_gains = jnp.clip(1.0 + 0.1 * jax.random.normal(key_list[8], (2, D), jnp.float32), 0.5, 1.5).astype(jnp.bfloat16)
    mean_query = noise(key_list[9], (D, H * HD), (0.05 * TOKENS ** 0.5), 28.0, ((0, 8), (1, 4)), jnp.float32)
    square_query = jnp.clip(jnp.exp(math.log(327.68) - 1.3862944 * jax.random.uniform(key_list[10], (D, H * HD), jnp.float32) ** block_levels(key_list[10], (D, H * HD), ((0, 8), (1, 4)), -0.2, 0.2)), 81.92, 327.68)
    mean_keyval = noise(key_list[11], (D, 2 * KV * HD), (0.05 * TOKENS ** 0.5), 28.0, ((0, 8), (1, 4)), jnp.float32)
    square_keyval = jnp.clip(jnp.exp(math.log(13107.2) - 3.465736 * jax.random.uniform(key_list[12], (D, 2 * KV * HD), jnp.float32) ** block_levels(key_list[12], (D, 2 * KV * HD), ((0, 8), (1, 4)), -0.2, 0.2)), 409.6, 13107.2)
    mean_output = noise(key_list[13], (H * HD, D), (0.05 * TOKENS ** 0.5), 28.0, ((0, 4), (1, 8)), jnp.float32)
    square_output = jnp.clip(jnp.exp(math.log(327.68) - 1.3862944 * jax.random.uniform(key_list[14], (H * HD, D), jnp.float32) ** block_levels(key_list[14], (H * HD, D), ((0, 4), (1, 8)), -0.2, 0.2)), 81.92, 327.68)
    mean_gateup = noise(key_list[15], (2, D, FF), (0.05 * TOKENS ** 0.5), 28.0, ((1, 8), (2, 4)), jnp.float32)
    square_gateup = jnp.clip(jnp.exp(math.log(327.68) - 1.3862944 * jax.random.uniform(key_list[16], (2, D, FF), jnp.float32) ** block_levels(key_list[16], (2, D, FF), ((1, 8), (2, 4)), -0.2, 0.2)), 81.92, 327.68)
    mean_down = noise(key_list[17], (FF, D), (0.05 * TOKENS ** 0.5), 28.0, ((0, 4), (1, 8)), jnp.float32)
    square_down = jnp.clip(jnp.exp(math.log(327.68) - 1.3862944 * jax.random.uniform(key_list[18], (FF, D), jnp.float32) ** block_levels(key_list[18], (FF, D), ((0, 4), (1, 8)), -0.2, 0.2)), 81.92, 327.68)
    mean_gains = noise(key_list[19], (2, D), (0.05 * TOKENS ** 0.5), 28.0, ((1, 8),), jnp.float32)
    square_gains = jnp.clip(jnp.exp(math.log(327.68) - 1.3862944 * jax.random.uniform(key_list[20], (2, D), jnp.float32) ** block_levels(key_list[20], (2, D), ((1, 8),), -0.2, 0.2)), 81.92, 327.68)
    return {"tokens": tokens, "cotangent": cotangent, "span_order": span_order, "w_query": w_query, "w_keyval": w_keyval, "w_output": w_output, "w_gateup": w_gateup, "w_down": w_down, "norm_gains": norm_gains, "mean_query": mean_query, "square_query": square_query, "mean_keyval": mean_keyval, "square_keyval": square_keyval, "mean_output": mean_output, "square_output": square_output, "mean_gateup": mean_gateup, "square_gateup": square_gateup, "mean_down": mean_down, "square_down": square_down, "mean_gains": mean_gains, "square_gains": square_gains}


norm_eps = 1e-05
rope_base = 500000.0
beta_one = 0.9
beta_two = 0.95
learn_rate = 0.01
weight_decay = 0.1
adam_eps = 1e-08
masked_score = -1e+30

@jax.custom_vjp
def low(v):
    return lax.optimization_barrier(v.astype(jnp.bfloat16)).astype(jnp.float32)

@jax.custom_vjp
def low_back(v):
    return v

def low_keep(v):
    return (low(v), None)

def low_pass(kept, grad):
    return (grad,)

def back_keep(v):
    return (v, None)

def back_low(kept, grad):
    return (low(grad),)
low.defvjp(low_keep, low_pass)
low_back.defvjp(back_keep, back_low)

def product(left_side, right_side):
    return jnp.dot(left_side, right_side, precision=lax.Precision.HIGHEST, preferred_element_type=jnp.float32)

def rotate(values, positions):
    half_size = HD // 2
    frequencies = rope_base ** (-(jnp.arange(half_size, dtype=jnp.float32) * 2.0 / HD))
    angles = positions.astype(jnp.float32)[:, None] * frequencies[None, :]
    cosine_table = jnp.concatenate([jnp.cos(angles), jnp.cos(angles)], axis=-1)[:, None, :]
    sine_table = jnp.concatenate([jnp.sin(angles), jnp.sin(angles)], axis=-1)[:, None, :]
    turned = jnp.concatenate([-values[..., half_size:], values[..., :half_size]], axis=-1)
    return values * cosine_table + turned * sine_table

def normalize(source):
    return source * lax.rsqrt(lax.optimization_barrier(jnp.mean(source * source, axis=-1, keepdims=True)) + norm_eps)

def attend_block(query_block, key_block, value_block, positions):
    scores = jnp.einsum('gqd,td->gqt', query_block, key_block, precision=lax.Precision.HIGHEST, preferred_element_type=jnp.float32) * HD ** (-0.5)
    scores = low_back(scores)
    causal = positions[None, :] <= positions[:, None]
    scores = jnp.where(causal[None], scores, masked_score)
    row_max = lax.optimization_barrier(jnp.max(scores, axis=-1, keepdims=True))
    exponent = jnp.exp(scores - row_max)
    attention = exponent / lax.optimization_barrier(jnp.sum(exponent, axis=-1, keepdims=True))
    return jnp.einsum('gqt,td->gqd', low(attention), value_block, precision=lax.Precision.HIGHEST, preferred_element_type=jnp.float32)

def forward(block_in, weights, positions):
    w_query, w_keyval, w_output, w_gateup, w_down, norm_gains = weights
    row_count = block_in.shape[0]
    group_size = H // KV
    row_pos = jnp.tile(positions, SEQS)
    attn_in = low(normalize(block_in) * norm_gains[0])
    queries = low_back(product(attn_in, w_query)).reshape(row_count, H, HD)
    keyvals = low_back(product(attn_in, w_keyval)).reshape(row_count, KV, 2, HD)
    query_low = low(rotate(queries, row_pos))
    key_low = low(rotate(keyvals[:, :, 0], row_pos))
    value_low = low(keyvals[:, :, 1])
    query_items = query_low.reshape(SEQS, SEQ_LEN, KV, group_size, HD).transpose(0, 2, 3, 1, 4).reshape(SEQS * KV, group_size, SEQ_LEN, HD)
    key_items = key_low.reshape(SEQS, SEQ_LEN, KV, HD).transpose(0, 2, 1, 3).reshape(SEQS * KV, SEQ_LEN, HD)
    value_items = value_low.reshape(SEQS, SEQ_LEN, KV, HD).transpose(0, 2, 1, 3).reshape(SEQS * KV, SEQ_LEN, HD)

    def one_item(block_item):
        return attend_block(block_item[0], block_item[1], block_item[2], positions)
    attended = lax.map(jax.checkpoint(one_item), (query_items, key_items, value_items))
    attended = attended.reshape(SEQS, KV, group_size, SEQ_LEN, HD).transpose(0, 3, 1, 2, 4).reshape(row_count, H * HD)
    attended = low(low_back(attended))
    middle = block_in + low_back(product(attended, w_output))
    mlp_input = low(normalize(middle) * norm_gains[1])
    gate_proj = low_back(product(mlp_input, w_gateup[0]))
    up_proj = low_back(product(mlp_input, w_gateup[1]))
    hidden = low(gate_proj * jax.nn.sigmoid(gate_proj) * up_proj)
    return middle + low_back(product(hidden, w_down))

def adam_update(gradient, old_mean, square, weight, decay_factor):
    moment = beta_one * old_mean + (1.0 - beta_one) * gradient
    spread = beta_two * square + (1.0 - beta_two) * gradient * gradient
    change = -learn_rate * (moment / (1.0 - beta_one ** STEP) / (jnp.sqrt(spread / (1.0 - beta_two ** STEP)) + adam_eps) + decay_factor * weight)
    return (moment, spread, change)

def reference(tokens, cotangent, span_order, w_query, w_keyval, w_output, w_gateup, w_down, norm_gains, mean_query, square_query, mean_keyval, square_keyval, mean_output, square_output, mean_gateup, square_gateup, mean_down, square_down, mean_gains, square_gains):
    positions = (span_order[:, None] * CH + jnp.arange(CH, dtype=jnp.int32)[None, :]).reshape(-1).astype(jnp.int32)

    def to_sequences(source):
        return source.astype(jnp.float32).reshape(N_DP, MICRO, SEQS, 2 * CH, D).transpose(1, 2, 0, 3, 4).reshape(MICRO, SEQS * SEQ_LEN, D)

    def from_sequences(source):
        return source.reshape(MICRO, SEQS, N_DP, 2 * CH, D).transpose(2, 0, 1, 3, 4).reshape(TOKENS, D)
    params = (w_query.astype(jnp.float32), w_keyval.astype(jnp.float32), w_output.astype(jnp.float32), w_gateup.astype(jnp.float32), w_down.astype(jnp.float32), norm_gains.astype(jnp.float32))

    def one_batch(totals, batch_pair):

        def forward_one(block_in, *weights):
            return forward(block_in, weights, positions)
        outputs, pullback = jax.vjp(forward_one, batch_pair[0], *params)
        gradients = pullback(batch_pair[1])
        summed = tuple((totals[index] + gradients[index + 1] for index in range(6)))
        return (summed, (outputs, gradients[0]))
    initial = tuple((jnp.zeros_like(weight) for weight in params))
    totals, stacked = lax.scan(one_batch, initial, (to_sequences(tokens), to_sequences(cotangent)))
    block_output = from_sequences(stacked[0]).astype(jnp.bfloat16)
    grad_tokens = from_sequences(stacked[1])
    grad_query, grad_keyval, grad_output, grad_gateup, grad_down, grad_gains = totals
    moment_query, spread_query, update_query = adam_update(grad_query, mean_query, square_query, params[0], weight_decay)
    moment_keyval, spread_keyval, update_keyval = adam_update(grad_keyval, mean_keyval, square_keyval, params[1], weight_decay)
    moment_output, spread_output, update_output = adam_update(grad_output, mean_output, square_output, params[2], weight_decay)
    moment_gateup, spread_gateup, update_gateup = adam_update(grad_gateup, mean_gateup, square_gateup, params[3], weight_decay)
    moment_down, spread_down, update_down = adam_update(grad_down, mean_down, square_down, params[4], weight_decay)
    moment_gains, spread_gains, update_gains = adam_update(grad_gains, mean_gains, square_gains, params[5], 0.0)
    return (block_output, grad_tokens, grad_query, moment_query, spread_query, update_query, grad_keyval, moment_keyval, spread_keyval, update_keyval, grad_output, moment_output, spread_output, update_output, grad_gateup, moment_gateup, spread_gateup, update_gateup, grad_down, moment_down, spread_down, update_down, grad_gains, moment_gains, spread_gains, update_gains)
```

```python
import functools

import jax
import jax.numpy as jnp
from jax import lax
from jax.experimental import pallas as pl
from jax.experimental.pallas import tpu as pltpu
from jax.sharding import PartitionSpec as P

HD = 64
CH = 64
SEQS = 4
MICRO = 2
STEP = 5
CHUNKS = 2

norm_eps = 1e-05
rope_base = 500000.0
beta_one = 0.9
beta_two = 0.95
learn_rate = 0.01
weight_decay = 0.1
adam_eps = 1e-08
masked_score = -1e30

F32 = jnp.float32
BF16 = jnp.bfloat16
VMEM_LIMIT = 60 * 1024 * 1024


def lane_tables(positions, kinds):
    half_size = HD // 2
    frequencies = rope_base ** (-(jnp.arange(half_size, dtype=F32) * 2.0 / HD))
    angles = positions.astype(F32)[:, None] * frequencies[None, :]
    cos_half, sin_half = jnp.cos(angles), jnp.sin(angles)
    cos_head = jnp.concatenate([cos_half, cos_half], axis=-1)
    sin_head = jnp.concatenate([-sin_half, sin_half], axis=-1)
    ones, zeros = jnp.ones_like(cos_head), jnp.zeros_like(cos_head)
    cos_all, sin_all = [], []
    for kind in kinds:
        cos_all.append(cos_head if kind else ones)
        sin_all.append(sin_head if kind else zeros)
    return jnp.concatenate(cos_all, axis=-1), jnp.concatenate(sin_all, axis=-1)


def half_turn(values):
    width = values.shape[-1]
    axis = values.ndim - 1
    lane = lax.broadcasted_iota(jnp.int32, values.shape, axis)
    ahead = pltpu.roll(values, width - HD // 2, axis)
    behind = pltpu.roll(values, HD // 2, axis)
    return jnp.where(lane % HD < HD // 2, ahead, behind)


def mean_square_scale(values):
    return lax.rsqrt(jnp.mean(values * values, axis=-1, keepdims=True) + norm_eps)


def project_kernel(x_ref, gain_ref, w_ref, cos_ref, sin_ref, a_ref, qkv_ref):
    x = x_ref[...].astype(F32)
    a = (x * mean_square_scale(x) * gain_ref[...].astype(F32)).astype(BF16)
    a_ref[...] = a
    t = jnp.dot(a, w_ref[...], preferred_element_type=F32)
    qkv_ref[...] = (t * cos_ref[...] + half_turn(t) * sin_ref[...]).astype(BF16)


def project(x, gain, weight, cos_t, sin_t):
    rows, depth = x.shape
    width = weight.shape[1]
    block = cos_t.shape[0]
    return pl.pallas_call(
        project_kernel,
        grid=(rows // block,),
        in_specs=[
            pl.BlockSpec((block, depth), lambda i: (i, 0)),
            pl.BlockSpec((1, depth), lambda i: (0, 0)),
            pl.BlockSpec((depth, width), lambda i: (0, 0)),
            pl.BlockSpec((block, width), lambda i: (0, 0)),
            pl.BlockSpec((block, width), lambda i: (0, 0)),
        ],
        out_specs=[
            pl.BlockSpec((block, depth), lambda i: (i, 0)),
            pl.BlockSpec((block, width), lambda i: (i, 0)),
        ],
        out_shape=[
            jax.ShapeDtypeStruct((rows, depth), BF16),
            jax.ShapeDtypeStruct((rows, width), BF16),
        ],
        compiler_params=pltpu.CompilerParams(vmem_limit_bytes=VMEM_LIMIT),
        cost_estimate=pl.CostEstimate(
            flops=2 * rows * depth * width, bytes_accessed=4 * rows * depth, transcendentals=0
        ),
        name="project",
    )(x, gain, weight, cos_t, sin_t)


def stack_heads(block, group, upper):
    lane = lax.broadcasted_iota(jnp.int32, (block.shape[0], 2 * HD), 1)
    keep = (lane >= HD) if upper else (lane < HD)
    parts = []
    for head in range(group):
        pair = block[:, (head // 2) * 2 * HD : (head // 2 + 1) * 2 * HD].astype(F32)
        if (head % 2 == 1) != upper:
            pair = pltpu.roll(pair, HD, 1)
        parts.append(jnp.where(keep, pair, 0.0).astype(BF16))
    return jnp.concatenate(parts, axis=0)


def unstack_heads(stacked, group, upper):
    rows = stacked.shape[0] // group
    lane = lax.broadcasted_iota(jnp.int32, (rows, 2 * HD), 1)
    pairs = []
    for pair in range(group // 2):
        even = stacked[(2 * pair) * rows : (2 * pair + 1) * rows]
        odd = stacked[(2 * pair + 1) * rows : (2 * pair + 2) * rows]
        if upper:
            even = pltpu.roll(even, HD, 1)
        else:
            odd = pltpu.roll(odd, HD, 1)
        pairs.append(jnp.where(lane < HD, even, odd))
    return jnp.concatenate(pairs, axis=1)


def scores_and_probs(q_pad, keys, qpos, kpos, group):
    scores = (
        lax.dot_general(q_pad, keys, (((1,), (1,)), ((), ())), preferred_element_type=F32)
        * HD ** (-0.5)
    )
    rows = qpos.shape[0]
    blocked = kpos > qpos
    masked = [
        jnp.where(blocked, masked_score, scores[h * rows : (h + 1) * rows]) for h in range(group)
    ]
    scores = jnp.concatenate(masked, axis=0)
    exponent = jnp.exp(scores - jnp.max(scores, axis=-1, keepdims=True))
    return exponent * (1.0 / jnp.sum(exponent, axis=-1, keepdims=True))


def attend_kernel(group, qpos_ref, kpos_ref, q_ref, kv_ref, o_ref):
    keyvals = kv_ref[...].reshape(-1, 2 * HD)
    q_pad = stack_heads(q_ref[...].reshape(-1, group * HD), group, False)
    probs = scores_and_probs(q_pad, keyvals, qpos_ref[...], kpos_ref[...], group)
    out = jnp.dot(probs.astype(BF16), keyvals, preferred_element_type=F32)
    o_ref[...] = unstack_heads(out, group, True).astype(BF16).reshape(o_ref.shape)


def attend_back_kernel(
    group, qpos_ref, kpos_ref, cos_ref, sin_ref, q_ref, do_ref, kv_ref, dq_ref, dkv_ref
):
    keyvals = kv_ref[...].reshape(-1, 2 * HD)
    q_pad = stack_heads(q_ref[...].reshape(-1, group * HD), group, False)
    do_pad = stack_heads(do_ref[...].reshape(-1, group * HD), group, True)
    probs = scores_and_probs(q_pad, keyvals, qpos_ref[...], kpos_ref[...], group)
    d_probs = lax.dot_general(
        do_pad, keyvals, (((1,), (1,)), ((), ())), preferred_element_type=F32
    )
    d_scores = probs * (d_probs - jnp.sum(d_probs * probs, axis=-1, keepdims=True))
    ds_low = d_scores.astype(BF16) * HD ** (-0.5)
    dq = jnp.dot(ds_low, keyvals, preferred_element_type=F32)
    dq = unstack_heads(dq, group, False)
    dq = dq * cos_ref[...] + half_turn(dq * sin_ref[...])
    dq_ref[...] = dq.astype(BF16).reshape(dq_ref.shape)
    contract = (((0,), (0,)), ((), ()))
    d_keyvals = lax.dot_general(
        ds_low, q_pad, contract, preferred_element_type=F32
    ) + lax.dot_general(probs.astype(BF16), do_pad, contract, preferred_element_type=F32)
    dkv_ref[...] = d_keyvals.astype(BF16).reshape(dkv_ref.shape)


def attention_specs(qkv_heads, n_dp, span_rows, group):
    q_spec = pl.BlockSpec((1, 1, span_rows, group * HD), lambda m, s, h: (m, s, 0, h))
    kv_spec = pl.BlockSpec(
        (n_dp, 1, 1, span_rows, 2 * HD), lambda m, s, h: (0, m, s, 0, h)
    )
    pos_q = pl.BlockSpec((span_rows, 1), lambda m, s, h: (0, 0))
    pos_k = pl.BlockSpec((1, n_dp * span_rows), lambda m, s, h: (0, 0))
    return q_spec, kv_spec, pos_q, pos_k


def attend(qpos, kpos, q, kv, group):
    micro, seqs, span_rows, width = q.shape
    n_dp, heads = kv.shape[0], width // (group * HD)
    q_spec, kv_spec, pos_q, pos_k = attention_specs(heads, n_dp, span_rows, group)
    return pl.pallas_call(
        functools.partial(attend_kernel, group),
        grid=(micro, seqs, heads),
        in_specs=[pos_q, pos_k, q_spec, kv_spec],
        out_specs=q_spec,
        out_shape=jax.ShapeDtypeStruct(q.shape, BF16),
        compiler_params=pltpu.CompilerParams(vmem_limit_bytes=VMEM_LIMIT),
        cost_estimate=pl.CostEstimate(
            flops=16 * micro * seqs * span_rows * width * n_dp * span_rows,
            bytes_accessed=4 * q.size + 2 * kv.size,
            transcendentals=0,
        ),
        name="attend",
    )(qpos, kpos, q, kv)


def attend_back(qpos, kpos, cos_q, sin_q, q, d_out, kv, group):
    micro, seqs, span_rows, width = q.shape
    n_dp, heads = kv.shape[0], width // (group * HD)
    q_spec, kv_spec, pos_q, pos_k = attention_specs(heads, n_dp, span_rows, group)
    table = pl.BlockSpec((span_rows, group * HD), lambda m, s, h: (0, 0))
    return pl.pallas_call(
        functools.partial(attend_back_kernel, group),
        grid=(micro, seqs, heads),
        in_specs=[pos_q, pos_k, table, table, q_spec, q_spec, kv_spec],
        out_specs=[q_spec, kv_spec],
        out_shape=[
            jax.ShapeDtypeStruct(q.shape, BF16),
            jax.ShapeDtypeStruct(kv.shape, BF16),
        ],
        compiler_params=pltpu.CompilerParams(vmem_limit_bytes=VMEM_LIMIT),
        cost_estimate=pl.CostEstimate(
            flops=40 * micro * seqs * span_rows * width * n_dp * span_rows,
            bytes_accessed=6 * q.size + 4 * kv.size,
            transcendentals=0,
        ),
        name="attend_back",
    )(qpos, kpos, cos_q, sin_q, q, d_out, kv)


def norm_back(d_normed, normed, scale):
    return scale * (d_normed - normed * jnp.mean(d_normed * normed, axis=-1, keepdims=True))


def adam_update(gradient, old_mean, square, weight, decay_factor):
    moment = beta_one * old_mean + (1.0 - beta_one) * gradient
    spread = beta_two * square + (1.0 - beta_two) * gradient * gradient
    change = -learn_rate * (
        moment / (1.0 - beta_one**STEP) / (jnp.sqrt(spread / (1.0 - beta_two**STEP)) + adam_eps)
        + decay_factor * weight
    )
    return (moment, spread, change)


def dot(left, right):
    return jnp.dot(left, right, preferred_element_type=F32)


def dot_nt(left, right):
    return lax.dot_general(left, right, (((1,), (1,)), ((), ())), preferred_element_type=F32)


def dot_tn(left, right):
    return lax.dot_general(left, right, (((0,), (0,)), ((), ())), preferred_element_type=F32)


def per_device(
    n_dp,
    n_tp,
    tokens,
    cotangent,
    span_order,
    w_query,
    w_keyval,
    w_output,
    w_gateup,
    w_down,
    norm_gains,
    mean_query,
    square_query,
    mean_keyval,
    square_keyval,
    mean_output,
    square_output,
    mean_gateup,
    square_gateup,
    mean_down,
    square_down,
    mean_gains,
    square_gains,
):
    depth = tokens.shape[1]
    span_rows = 2 * CH
    block_rows = SEQS * span_rows // n_tp
    parts = span_rows // min(span_rows, block_rows)
    q_width = w_query.shape[1]
    kv_width = w_keyval.shape[1]
    hidden_width = w_down.shape[0]
    own_depth = w_query.shape[0]
    group = q_width // HD // (kv_width // (2 * HD))
    device = lax.axis_index("dp")
    rank = lax.axis_index("tp")

    def swap(value, k):
        return lax.ppermute(value, "tp", [(i, i ^ k) for i in range(n_tp)])

    def reorder(value):
        return jnp.concatenate(
            [lax.dynamic_slice_in_dim(value, rank ^ k, 1, axis=1) for k in range(n_tp)], axis=1
        )

    def gather_rows(own):
        return jnp.stack([own] + [swap(own, k) for k in range(1, n_tp)], axis=1)

    def exchange(blocks):
        return [blocks[0]] + [swap(blocks[k], k) for k in range(1, n_tp)]

    def scatter_sum(partial):
        got = exchange([partial[:, k].astype(BF16) for k in range(n_tp)])
        total = partial[:, 0].astype(F32)
        for k in range(1, n_tp):
            total = total + got[k].astype(F32)
        return total

    qkv_full = lax.all_gather(
        jnp.concatenate([w_query, w_keyval], axis=1), "dp", axis=0, tiled=True
    )
    gains_full = lax.all_gather(norm_gains, "dp", axis=1, tiled=True)
    out_t_full = lax.all_gather(w_output.T, "dp", axis=0, tiled=True)

    offsets = jnp.arange(CH, dtype=jnp.int32)
    all_pos = (span_order[:, None] * CH + offsets[None, :]).reshape(n_dp, parts, -1)
    all_pos = jnp.stack([all_pos[:, (rank % parts) ^ p] for p in range(parts)], axis=1)
    own_pos = lax.dynamic_slice_in_dim(all_pos, device, 1).reshape(-1)
    all_pos = all_pos.reshape(-1)
    qpos, kpos = own_pos[:, None], all_pos[None, :]
    kv_kinds = [True, False] * (kv_width // (2 * HD))
    cos_t, sin_t = lane_tables(own_pos, [True] * (q_width // HD) + kv_kinds)

    x = reorder(tokens.reshape(MICRO, n_tp, block_rows, depth))
    seed = reorder(cotangent.reshape(MICRO, n_tp, block_rows, depth))
    rows = MICRO * SEQS * span_rows
    gain_one, gain_two = gains_full[0:1], gains_full[1:2]
    attn_in, qkv = project(x.reshape(rows, depth), gain_one, qkv_full, cos_t, sin_t)
    qkv = qkv.reshape(MICRO, SEQS, span_rows, q_width + kv_width)
    q, kv = qkv[..., :q_width], qkv[..., q_width:]
    kv_all = lax.all_gather(kv, "dp", axis=0, tiled=False)

    chunk = hidden_width // CHUNKS
    w_down_t = w_down.T
    mlp_full = []
    for c in range(CHUNKS):
        cols = slice(c * chunk, (c + 1) * chunk)
        shard = jnp.concatenate(
            [w_gateup[0][:, cols], w_gateup[1][:, cols], w_down_t[:, cols]], axis=1
        )
        mlp_full.append(lax.all_gather(shard, "dp", axis=0, tiled=True))

    attended = attend(qpos, kpos, q, kv_all, group)
    by_block = (MICRO, n_tp, block_rows, -1)

    out_t_all = [out_t_full] + [swap(out_t_full, k) for k in range(1, n_tp)]
    attended_blocks = attended.reshape(by_block)
    heads_in = exchange([attended_blocks[:, k] for k in range(n_tp)])
    own_rows = MICRO * block_rows
    x_own = x[:, 0].reshape(own_rows, depth).astype(F32)
    seed_own = seed[:, 0].reshape(own_rows, depth).astype(F32)
    middle = x_own
    for k in range(n_tp):
        middle = middle + dot_nt(heads_in[k].reshape(own_rows, q_width), out_t_all[k])
    scale_two = mean_square_scale(middle)
    normed_two = middle * scale_two
    u_own = (normed_two * gain_two.astype(F32)).astype(BF16)
    u = gather_rows(u_own.reshape(MICRO, block_rows, depth)).reshape(rows, depth)
    g = seed.reshape(rows, depth)

    y_part = None
    du_part = None
    mlp_grads = []
    for c in range(CHUNKS):
        weights = mlp_full[c]
        gate_proj = dot(u, weights[:, :chunk])
        up_proj = dot(u, weights[:, chunk : 2 * chunk])
        d_hidden = dot(g, weights[:, 2 * chunk :])
        sigmoid_gate = jax.nn.sigmoid(gate_proj)
        silu_gate = gate_proj * sigmoid_gate
        hidden = (silu_gate * up_proj).astype(BF16)
        d_gate = (
            d_hidden * up_proj * sigmoid_gate * (1.0 + gate_proj * (1.0 - sigmoid_gate))
        ).astype(BF16)
        d_up = (d_hidden * silu_gate).astype(BF16)
        d_both = jnp.concatenate([d_gate, d_up], axis=1)
        du_term = dot_nt(d_both, weights[:, : 2 * chunk])
        y_term = dot_nt(hidden, weights[:, 2 * chunk :])
        du_part = du_term if du_part is None else du_part + du_term
        y_part = y_term if y_part is None else y_part + y_term
        grads = jnp.concatenate(
            [dot_tn(u, d_both).astype(BF16), dot_tn(g, hidden).astype(BF16)], axis=1
        )
        mlp_grads.append(lax.psum_scatter(grads, "dp", scatter_dimension=0, tiled=True))

    d_mixed = scatter_sum(du_part.reshape(by_block)).reshape(own_rows, depth)
    gain_grad_two = jnp.sum(d_mixed * normed_two, axis=0)
    d_middle = seed_own + norm_back(d_mixed * gain_two.astype(F32), normed_two, scale_two)
    d_mid_low = d_middle.astype(BF16)
    do_rows = [
        dot(d_mid_low, out_t_all[k]).astype(BF16).reshape(MICRO, block_rows, q_width)
        for k in range(n_tp)
    ]
    d_attend = jnp.stack(exchange(do_rows), axis=1).reshape(q.shape)
    cos_q, sin_q = cos_t[:, : group * HD], sin_t[:, : group * HD]
    d_query_low, d_kv_part = attend_back(qpos, kpos, cos_q, sin_q, q, d_attend, kv_all, group)
    own_grad = lax.psum_scatter(d_kv_part, "dp", scatter_dimension=0, tiled=False).astype(F32)

    block_own = middle + scatter_sum(y_part.reshape(by_block)).reshape(own_rows, depth)
    out_rows = gather_rows(block_own.astype(BF16).reshape(MICRO, block_rows, depth))
    block_output = reorder(out_rows).reshape(rows, depth)
    d_mid_rows = gather_rows(d_mid_low.reshape(MICRO, block_rows, depth)).reshape(rows, depth)
    out_grad_t = dot_tn(d_mid_rows, attended.reshape(rows, q_width)).astype(BF16)

    cos_k, sin_k = cos_t[:, q_width:], sin_t[:, q_width:]
    scaled = own_grad * sin_k
    lane = jnp.arange(kv_width)
    turned = jnp.where(
        lane % HD < HD // 2,
        jnp.roll(scaled, -(HD // 2), axis=-1),
        jnp.roll(scaled, HD // 2, axis=-1),
    )
    d_kv_low = (own_grad * cos_k + turned).astype(BF16)
    d_qkv = jnp.concatenate([d_query_low, d_kv_low], axis=-1)
    qkv_all = [qkv_full] + [swap(qkv_full, k) for k in range(1, n_tp)]
    d_blocks = d_qkv.reshape(by_block)
    d_heads = exchange([d_blocks[:, k] for k in range(n_tp)])
    d_act = None
    for k in range(n_tp):
        term = dot_nt(d_heads[k].reshape(own_rows, q_width + kv_width), qkv_all[k])
        d_act = term if d_act is None else d_act + term
    scale_one = mean_square_scale(x_own)
    normed_one = x_own * scale_one
    gain_grad_one = jnp.sum(d_act * normed_one, axis=0)
    tokens_own = d_middle + norm_back(d_act * gain_one.astype(F32), normed_one, scale_one)
    tokens_rows = gather_rows(tokens_own.astype(BF16).reshape(MICRO, block_rows, depth))
    grad_tokens = reorder(tokens_rows).reshape(rows, depth).astype(F32)

    qkv_grad = dot_tn(attn_in, d_qkv.reshape(rows, q_width + kv_width)).astype(BF16)
    gain_cols = jnp.stack([gain_grad_one, gain_grad_two], axis=1)
    gain_cols = jnp.pad(gain_cols, ((0, 0), (0, 126))).astype(BF16)
    attn_grads = lax.psum_scatter(
        jnp.concatenate([qkv_grad, out_grad_t, gain_cols], axis=1),
        "dp",
        scatter_dimension=0,
        tiled=True,
    )
    gain_part = attn_grads[:, 2 * q_width + kv_width :]
    gain_sum = gain_part.astype(F32)
    for k in range(1, n_tp):
        gain_sum = gain_sum + swap(gain_part, k).astype(F32)

    grad_query = attn_grads[:, :q_width].astype(F32)
    grad_keyval = attn_grads[:, q_width : q_width + kv_width].astype(F32)
    grad_output = attn_grads[:, q_width + kv_width : 2 * q_width + kv_width].astype(F32).T
    grad_gains = gain_sum[:, :2].T
    grad_gateup = jnp.stack(
        [
            jnp.concatenate([part[:, i * chunk : (i + 1) * chunk] for part in mlp_grads], axis=1)
            for i in range(2)
        ]
    ).astype(F32)
    grad_down = jnp.concatenate([part[:, 2 * chunk :] for part in mlp_grads], axis=1).astype(F32).T

    def with_update(gradient, old_mean, square, weight, decay):
        return (gradient,) + adam_update(gradient, old_mean, square, weight.astype(F32), decay)

    return (
        (block_output, grad_tokens)
        + with_update(grad_query, mean_query, square_query, w_query, weight_decay)
        + with_update(grad_keyval, mean_keyval, square_keyval, w_keyval, weight_decay)
        + with_update(grad_output, mean_output, square_output, w_output, weight_decay)
        + with_update(grad_gateup, mean_gateup, square_gateup, w_gateup, weight_decay)
        + with_update(grad_down, mean_down, square_down, w_down, weight_decay)
        + with_update(grad_gains, mean_gains, square_gains, norm_gains, 0.0)
    )


def solution(mesh):
    rows_first = P("dp", "tp")
    cols_last = P("tp", "dp")
    stacked = P(None, "dp", "tp")
    gains = P(None, "dp")
    token_rows = P("dp", None)
    placed = (
        (token_rows, token_rows, P())
        + (rows_first, rows_first, cols_last, stacked, cols_last, gains)
        + (rows_first,) * 4
        + (cols_last,) * 2
        + (stacked,) * 2
        + (cols_last,) * 2
        + (gains,) * 2
    )
    results = (
        (token_rows, token_rows)
        + (rows_first,) * 8
        + (cols_last,) * 4
        + (stacked,) * 4
        + (cols_last,) * 4
        + (gains,) * 4
    )
    return jax.shard_map(
        functools.partial(per_device, mesh.shape["dp"], mesh.shape["tp"]),
        mesh=mesh,
        in_specs=placed,
        out_specs=results,
        check_vma=False,
    )
```

```python
import functools

import jax
import jax.numpy as jnp
from jax import lax
from jax.experimental import pallas as pl
from jax.experimental.pallas import tpu as pltpu
from jax.sharding import PartitionSpec as P

HD = 64
CH = 64
SEQS = 4
MICRO = 2
STEP = 5
CHUNKS = 2
SUB = 512

norm_eps = 1e-05
rope_base = 500000.0
beta_one = 0.9
beta_two = 0.95
learn_rate = 0.01
weight_decay = 0.1
adam_eps = 1e-08
masked_score = -1e30

F32 = jnp.float32
BF16 = jnp.bfloat16
VMEM_LIMIT = 60 * 1024 * 1024
HINT = 20


def hint(flops, bytes_accessed, transcendentals):
    return pl.CostEstimate(
        flops=flops // HINT, bytes_accessed=bytes_accessed // HINT, transcendentals=transcendentals
    )


def lane_tables(positions, kinds):
    half_size = HD // 2
    frequencies = rope_base ** (-(jnp.arange(half_size, dtype=F32) * 2.0 / HD))
    angles = positions.astype(F32)[:, None] * frequencies[None, :]
    cos_half, sin_half = jnp.cos(angles), jnp.sin(angles)
    cos_head = jnp.concatenate([cos_half, cos_half], axis=-1)
    sin_head = jnp.concatenate([-sin_half, sin_half], axis=-1)
    ones, zeros = jnp.ones_like(cos_head), jnp.zeros_like(cos_head)
    cos_all, sin_all = [], []
    for kind in kinds:
        cos_all.append(cos_head if kind else ones)
        sin_all.append(sin_head if kind else zeros)
    return jnp.concatenate(cos_all, axis=-1), jnp.concatenate(sin_all, axis=-1)


def half_turn(values):
    width = values.shape[-1]
    axis = values.ndim - 1
    lane = lax.broadcasted_iota(jnp.int32, values.shape, axis)
    ahead = pltpu.roll(values, width - HD // 2, axis)
    behind = pltpu.roll(values, HD // 2, axis)
    return jnp.where(lane % HD < HD // 2, ahead, behind)


def mean_square_scale(values):
    return lax.rsqrt(jnp.mean(values * values, axis=-1, keepdims=True) + norm_eps)


def project_kernel(x_ref, gain_ref, w_ref, cos_ref, sin_ref, a_ref, qkv_ref):
    x = x_ref[...].astype(F32)
    a = (x * mean_square_scale(x) * gain_ref[...].astype(F32)).astype(BF16)
    a_ref[...] = a
    t = jnp.dot(a, w_ref[...], preferred_element_type=F32)
    qkv_ref[...] = (t * cos_ref[...] + half_turn(t) * sin_ref[...]).astype(BF16)


def project(x, gain, weight, cos_t, sin_t):
    rows, depth = x.shape
    width = weight.shape[1]
    block = cos_t.shape[0]
    return pl.pallas_call(
        project_kernel,
        grid=(rows // block,),
        in_specs=[
            pl.BlockSpec((block, depth), lambda i: (i, 0)),
            pl.BlockSpec((1, depth), lambda i: (0, 0)),
            pl.BlockSpec((depth, width), lambda i: (0, 0)),
            pl.BlockSpec((block, width), lambda i: (0, 0)),
            pl.BlockSpec((block, width), lambda i: (0, 0)),
        ],
        out_specs=[
            pl.BlockSpec((block, depth), lambda i: (i, 0)),
            pl.BlockSpec((block, width), lambda i: (i, 0)),
        ],
        out_shape=[
            jax.ShapeDtypeStruct((rows, depth), BF16),
            jax.ShapeDtypeStruct((rows, width), BF16),
        ],
        compiler_params=pltpu.CompilerParams(vmem_limit_bytes=VMEM_LIMIT),
        cost_estimate=hint(
            flops=2 * rows * depth * width, bytes_accessed=4 * rows * depth, transcendentals=0
        ),
        name="project",
    )(x, gain, weight, cos_t, sin_t)


def stack_heads(block, group, upper):
    lane = lax.broadcasted_iota(jnp.int32, (block.shape[0], 2 * HD), 1)
    keep = (lane >= HD) if upper else (lane < HD)
    parts = []
    for head in range(group):
        pair = block[:, (head // 2) * 2 * HD : (head // 2 + 1) * 2 * HD].astype(F32)
        if (head % 2 == 1) != upper:
            pair = pltpu.roll(pair, HD, 1)
        parts.append(jnp.where(keep, pair, 0.0).astype(BF16))
    return jnp.concatenate(parts, axis=0)


def unstack_heads(stacked, group, upper):
    rows = stacked.shape[0] // group
    lane = lax.broadcasted_iota(jnp.int32, (rows, 2 * HD), 1)
    pairs = []
    for pair in range(group // 2):
        even = stacked[(2 * pair) * rows : (2 * pair + 1) * rows]
        odd = stacked[(2 * pair + 1) * rows : (2 * pair + 2) * rows]
        if upper:
            even = pltpu.roll(even, HD, 1)
        else:
            odd = pltpu.roll(odd, HD, 1)
        pairs.append(jnp.where(lane < HD, even, odd))
    return jnp.concatenate(pairs, axis=1)


def scores_and_probs(q_pad, keys, qpos, kpos, group):
    scores = (
        lax.dot_general(q_pad, keys, (((1,), (1,)), ((), ())), preferred_element_type=F32)
        * HD ** (-0.5)
    )
    rows = qpos.shape[0]
    blocked = kpos > qpos
    masked = [
        jnp.where(blocked, masked_score, scores[h * rows : (h + 1) * rows]) for h in range(group)
    ]
    scores = jnp.concatenate(masked, axis=0)
    exponent = jnp.exp(scores - jnp.max(scores, axis=-1, keepdims=True))
    return exponent * (1.0 / jnp.sum(exponent, axis=-1, keepdims=True))


def attend_kernel(group, qpos_ref, kpos_ref, q_ref, kv_ref, o_ref):
    keyvals = kv_ref[...].reshape(-1, 2 * HD)
    q_pad = stack_heads(q_ref[...].reshape(-1, group * HD), group, False)
    probs = scores_and_probs(q_pad, keyvals, qpos_ref[...], kpos_ref[...], group)
    out = jnp.dot(probs.astype(BF16), keyvals, preferred_element_type=F32)
    o_ref[...] = unstack_heads(out, group, True).astype(BF16).reshape(o_ref.shape)


def attend_back_kernel(
    group, qpos_ref, kpos_ref, cos_ref, sin_ref, q_ref, do_ref, kv_ref, dq_ref, dkv_ref
):
    keyvals = kv_ref[...].reshape(-1, 2 * HD)
    q_pad = stack_heads(q_ref[...].reshape(-1, group * HD), group, False)
    do_pad = stack_heads(do_ref[...].reshape(-1, group * HD), group, True)
    probs = scores_and_probs(q_pad, keyvals, qpos_ref[...], kpos_ref[...], group)
    d_probs = lax.dot_general(
        do_pad, keyvals, (((1,), (1,)), ((), ())), preferred_element_type=F32
    )
    d_scores = probs * (d_probs - jnp.sum(d_probs * probs, axis=-1, keepdims=True))
    ds_low = d_scores.astype(BF16) * HD ** (-0.5)
    dq = jnp.dot(ds_low, keyvals, preferred_element_type=F32)
    dq = unstack_heads(dq, group, False)
    dq = dq * cos_ref[...] + half_turn(dq * sin_ref[...])
    dq_ref[...] = dq.astype(BF16).reshape(dq_ref.shape)
    contract = (((0,), (0,)), ((), ()))
    d_keyvals = lax.dot_general(
        ds_low, q_pad, contract, preferred_element_type=F32
    ) + lax.dot_general(probs.astype(BF16), do_pad, contract, preferred_element_type=F32)
    dkv_ref[...] = d_keyvals.astype(BF16).reshape(dkv_ref.shape)


def attention_specs(qkv_heads, n_dp, span_rows, group):
    q_spec = pl.BlockSpec((1, 1, span_rows, group * HD), lambda m, s, h: (m, s, 0, h))
    kv_spec = pl.BlockSpec(
        (n_dp, 1, 1, span_rows, 2 * HD), lambda m, s, h: (0, m, s, 0, h)
    )
    pos_q = pl.BlockSpec((span_rows, 1), lambda m, s, h: (0, 0))
    pos_k = pl.BlockSpec((1, n_dp * span_rows), lambda m, s, h: (0, 0))
    return q_spec, kv_spec, pos_q, pos_k


def attend(qpos, kpos, q, kv, group):
    micro, seqs, span_rows, width = q.shape
    n_dp, heads = kv.shape[0], width // (group * HD)
    q_spec, kv_spec, pos_q, pos_k = attention_specs(heads, n_dp, span_rows, group)
    return pl.pallas_call(
        functools.partial(attend_kernel, group),
        grid=(micro, seqs, heads),
        in_specs=[pos_q, pos_k, q_spec, kv_spec],
        out_specs=q_spec,
        out_shape=jax.ShapeDtypeStruct(q.shape, BF16),
        compiler_params=pltpu.CompilerParams(vmem_limit_bytes=VMEM_LIMIT),
        cost_estimate=hint(
            flops=16 * micro * seqs * span_rows * width * n_dp * span_rows,
            bytes_accessed=4 * q.size + 2 * kv.size,
            transcendentals=0,
        ),
        name="attend",
    )(qpos, kpos, q, kv)


def attend_back(qpos, kpos, cos_q, sin_q, q, d_out, kv, group):
    micro, seqs, span_rows, width = q.shape
    n_dp, heads = kv.shape[0], width // (group * HD)
    q_spec, kv_spec, pos_q, pos_k = attention_specs(heads, n_dp, span_rows, group)
    table = pl.BlockSpec((span_rows, group * HD), lambda m, s, h: (0, 0))
    return pl.pallas_call(
        functools.partial(attend_back_kernel, group),
        grid=(micro, seqs, heads),
        in_specs=[pos_q, pos_k, table, table, q_spec, q_spec, kv_spec],
        out_specs=[q_spec, kv_spec],
        out_shape=[
            jax.ShapeDtypeStruct(q.shape, BF16),
            jax.ShapeDtypeStruct(kv.shape, BF16),
        ],
        compiler_params=pltpu.CompilerParams(vmem_limit_bytes=VMEM_LIMIT),
        cost_estimate=hint(
            flops=40 * micro * seqs * span_rows * width * n_dp * span_rows,
            bytes_accessed=6 * q.size + 4 * kv.size,
            transcendentals=0,
        ),
        name="attend_back",
    )(qpos, kpos, cos_q, sin_q, q, d_out, kv)


def norm_back(d_normed, normed, scale):
    return scale * (d_normed - normed * jnp.mean(d_normed * normed, axis=-1, keepdims=True))


def adam_update(gradient, old_mean, square, weight, decay_factor):
    moment = beta_one * old_mean + (1.0 - beta_one) * gradient
    spread = beta_two * square + (1.0 - beta_two) * gradient * gradient
    change = -learn_rate * (
        moment / (1.0 - beta_one**STEP) / (jnp.sqrt(spread / (1.0 - beta_two**STEP)) + adam_eps)
        + decay_factor * weight
    )
    return (moment, spread, change)


def dot(left, right):
    return jnp.dot(left, right, preferred_element_type=F32)


def dot_nt(left, right):
    return lax.dot_general(left, right, (((1,), (1,)), ((), ())), preferred_element_type=F32)


def dot_tn(left, right):
    return lax.dot_general(left, right, (((0,), (0,)), ((), ())), preferred_element_type=F32)


def gated_kernel(last, steps, u_ref, g_ref, w_ref, *refs):
    if last:
        y_old, du_old, hid_ref, dgu_ref, y_out, du_out, y_sum, du_sum, y_low, du_low, sem = refs
    else:
        hid_ref, dgu_ref, y_out, du_out, y_sum, du_sum, y_low, du_low, sem = refs
    step = pl.program_id(0)
    depth = w_ref.shape[0]
    sub = hid_ref.shape[1]
    cols = min(512, depth)

    @pl.when(step == 0)
    def _():
        y_sum[...] = jnp.zeros_like(y_sum)
        du_sum[...] = jnp.zeros_like(du_sum)
        if last:
            pltpu.make_async_copy(y_old, y_low, sem.at[0]).start()
            pltpu.make_async_copy(du_old, du_low, sem.at[1]).start()

    gate_proj = dot(u_ref[...], w_ref[:, :sub])
    up_proj = dot(u_ref[...], w_ref[:, sub : 2 * sub])
    sigmoid_gate = jax.nn.sigmoid(gate_proj)
    silu_gate = gate_proj * sigmoid_gate
    hid_ref[...] = (silu_gate * up_proj).astype(BF16)
    d_hidden = dot(g_ref[...], w_ref[:, 2 * sub :])
    d_gate = d_hidden * up_proj * sigmoid_gate * (1.0 + gate_proj * (1.0 - sigmoid_gate))
    dgu_ref[:, :sub] = d_gate.astype(BF16)
    dgu_ref[:, sub:] = (d_hidden * silu_gate).astype(BF16)
    for start in range(0, depth, cols):
        part = slice(start, start + cols)
        du_sum[:, part] += dot_nt(dgu_ref[...], w_ref[part, : 2 * sub])
        y_sum[:, part] += dot_nt(hid_ref[...], w_ref[part, 2 * sub :])

    @pl.when(step == steps - 1)
    def _():
        copy_y = pltpu.make_async_copy(y_low, y_out, sem.at[0])
        copy_du = pltpu.make_async_copy(du_low, du_out, sem.at[1])
        if last:
            pltpu.make_async_copy(y_old, y_low, sem.at[0]).wait()
            pltpu.make_async_copy(du_old, du_low, sem.at[1]).wait()
            du_low[...] = (du_sum[...] + du_low[...].astype(F32)).astype(BF16)
            copy_du.start()
            y_low[...] = (y_sum[...] + y_low[...].astype(F32)).astype(BF16)
        else:
            du_low[...] = du_sum[...].astype(BF16)
            copy_du.start()
            y_low[...] = y_sum[...].astype(BF16)
        copy_y.start()
        copy_du.wait()
        copy_y.wait()


def feed_forward(u, g, weights, sub, sums):
    rows, depth = u.shape
    steps = weights.shape[1] // (3 * sub)
    last = sums is not None
    whole = functools.partial(pl.BlockSpec, pipeline_mode=pl.Buffered(1))
    anywhere = pl.BlockSpec(memory_space=pl.ANY)
    return pl.pallas_call(
        functools.partial(gated_kernel, last, steps),
        grid=(steps,),
        in_specs=[
            whole((rows, depth), lambda j: (0, 0)),
            whole((rows, depth), lambda j: (0, 0)),
            pl.BlockSpec((depth, 3 * sub), lambda j: (0, j)),
        ]
        + ([anywhere, anywhere] if last else []),
        out_specs=[
            pl.BlockSpec((rows, sub), lambda j: (0, j)),
            pl.BlockSpec((rows, 2 * sub), lambda j: (0, j)),
            anywhere,
            anywhere,
        ],
        out_shape=[
            jax.ShapeDtypeStruct((rows, steps * sub), BF16),
            jax.ShapeDtypeStruct((rows, 2 * steps * sub), BF16),
            jax.ShapeDtypeStruct((rows, depth), BF16),
            jax.ShapeDtypeStruct((rows, depth), BF16),
        ],
        scratch_shapes=[
            pltpu.VMEM((rows, depth), F32),
            pltpu.VMEM((rows, depth), F32),
            pltpu.VMEM((rows, depth), BF16),
            pltpu.VMEM((rows, depth), BF16),
            pltpu.SemaphoreType.DMA((2,)),
        ],
        compiler_params=pltpu.CompilerParams(vmem_limit_bytes=VMEM_LIMIT),
        cost_estimate=hint(
            flops=12 * rows * depth * steps * sub,
            bytes_accessed=2 * weights.size + 8 * rows * depth,
            transcendentals=0,
        ),
        name="feed_forward",
    )(u, g, weights, *(sums if last else ()))


def outer_kernel(batches, sub, steps, half, core_ref, *refs):
    u_refs, g_refs = refs[:batches], refs[batches : 2 * batches]
    hid_refs, dgu_refs = refs[2 * batches : 3 * batches], refs[3 * batches : 4 * batches]
    outs = refs[4 * batches :]

    def products(out_ref):
        for j in range(steps):
            both = slice(2 * j * sub, 2 * (j + 1) * sub)
            one = slice(j * sub, (j + 1) * sub)
            total = dot_tn(u_refs[0][...], dgu_refs[0][:, both])
            for m in range(1, batches):
                total += dot_tn(u_refs[m][...], dgu_refs[m][:, both])
            out_ref[0, :, 3 * j * sub : 3 * j * sub + 2 * sub] = total.astype(BF16)
            total = dot_tn(g_refs[0][...], hid_refs[0][:, one])
            for m in range(1, batches):
                total += dot_tn(g_refs[m][...], hid_refs[m][:, one])
            out_ref[0, :, 3 * j * sub + 2 * sub : 3 * (j + 1) * sub] = total.astype(BF16)

    if len(outs) == 1:
        products(outs[0])
    else:

        @pl.when(pl.program_id(0) < half)
        def _():
            products(outs[0])

        @pl.when(pl.program_id(0) >= half)
        def _():
            products(outs[1])


def outer_products(core, us, gs, hids, dgus, own, sub, split):
    batches = len(us)
    rows, depth = us[0].shape
    n_dp = depth // own
    half = n_dp // 2
    width = hids[0].shape[1]
    steps = width // sub
    if split:

        def place(i, core_ref):
            mine = jnp.where(i < half, 1 - core_ref[0], core_ref[0])
            return (i % half) * 2 + mine

        out_specs = [
            pl.BlockSpec((1, own, 3 * width), lambda i, r: (jnp.minimum(i, half - 1), 0, 0)),
            pl.BlockSpec((1, own, 3 * width), lambda i, r: (jnp.maximum(i - half, 0), 0, 0)),
        ]
        out_shape = [jax.ShapeDtypeStruct((half, own, 3 * width), BF16)] * 2
    else:

        def place(i, core_ref):
            return i

        out_specs = [pl.BlockSpec((1, own, 3 * width), lambda i, r: (i, 0, 0))]
        out_shape = [jax.ShapeDtypeStruct((n_dp, own, 3 * width), BF16)]
    whole = functools.partial(pl.BlockSpec, pipeline_mode=pl.Buffered(1))
    column = pl.BlockSpec((rows, own), lambda i, r: (0, place(i, r)))
    return pl.pallas_call(
        functools.partial(outer_kernel, batches, sub, steps, half),
        grid_spec=pltpu.PrefetchScalarGridSpec(
            num_scalar_prefetch=1,
            grid=(n_dp,),
            in_specs=[column] * (2 * batches)
            + [whole((rows, width), lambda i, r: (0, 0))] * batches
            + [whole((rows, 2 * width), lambda i, r: (0, 0))] * batches,
            out_specs=out_specs,
        ),
        out_shape=out_shape,
        compiler_params=pltpu.CompilerParams(vmem_limit_bytes=VMEM_LIMIT),
        cost_estimate=hint(
            flops=6 * rows * batches * depth * width,
            bytes_accessed=6 * depth * width,
            transcendentals=0,
        ),
        name="outer_products",
    )(core, *us, *gs, *hids, *dgus)


def step_kernel(turned, decay, steps, chunks, *refs):
    grads = refs[:chunks]
    mean_ref, square_ref, weight_ref, grad_ref, moment_ref, spread_ref, update_ref = refs[chunks:]
    place = pl.program_id(1)
    for c in range(chunks):

        @pl.when(place // steps == c)
        def _(c=c):
            gradient = grads[c][...].astype(F32)
            if turned:
                gradient = gradient.T
            gradient = gradient.reshape(grad_ref.shape)
            moment, spread, change = adam_update(
                gradient, mean_ref[...], square_ref[...], weight_ref[...].astype(F32), decay
            )
            grad_ref[...] = gradient
            moment_ref[...] = moment
            spread_ref[...] = spread
            update_ref[...] = change


def step_from_chunks(grads, old_mean, square, weight, sub, offset, turned, decay):
    chunks, own = len(grads), grads[0].shape[0]
    steps = grads[0].shape[1] // (3 * sub)

    def grad_spec(c):
        def index(i, p):
            j = jnp.clip(p - c * steps, 0, steps - 1)
            return (0, 3 * j + i + offset)

        return pl.BlockSpec((own, sub), index)

    if turned:
        lead, spec = 1, pl.BlockSpec((sub, own), lambda i, p: (p, 0))
    else:
        lead, spec = old_mean.shape[0], pl.BlockSpec((1, own, sub), lambda i, p: (i, 0, p))
    return tuple(
        pl.pallas_call(
            functools.partial(step_kernel, turned, decay, steps, chunks),
            grid=(lead, chunks * steps),
            in_specs=[grad_spec(c) for c in range(chunks)] + [spec] * 3,
            out_specs=[spec] * 4,
            out_shape=[jax.ShapeDtypeStruct(old_mean.shape, F32)] * 4,
            compiler_params=pltpu.CompilerParams(vmem_limit_bytes=VMEM_LIMIT),
            cost_estimate=hint(
                flops=20 * old_mean.size, bytes_accessed=28 * old_mean.size, transcendentals=0
            ),
            name="weight_step",
        )(*grads, old_mean, square, weight)
    )


def per_device(
    n_dp,
    n_tp,
    tokens,
    cotangent,
    span_order,
    w_query,
    w_keyval,
    w_output,
    w_gateup,
    w_down,
    norm_gains,
    mean_query,
    square_query,
    mean_keyval,
    square_keyval,
    mean_output,
    square_output,
    mean_gateup,
    square_gateup,
    mean_down,
    square_down,
    mean_gains,
    square_gains,
):
    depth = tokens.shape[1]
    span_rows = 2 * CH
    block_rows = SEQS * span_rows // n_tp
    parts = span_rows // min(span_rows, block_rows)
    q_width = w_query.shape[1]
    kv_width = w_keyval.shape[1]
    hidden_width = w_down.shape[0]
    own_depth = w_query.shape[0]
    group = q_width // HD // (kv_width // (2 * HD))
    device = lax.axis_index("dp")
    rank = lax.axis_index("tp")
    line = n_dp // 2
    place, core = device // 2, device % 2

    def swap(value, k):
        return lax.ppermute(value, "tp", [(i, i ^ k) for i in range(n_tp)])

    def reorder(value):
        return jnp.concatenate(
            [lax.dynamic_slice_in_dim(value, rank ^ k, 1, axis=1) for k in range(n_tp)], axis=1
        )

    def gather_blocks(own):
        half = own.shape[0] // 2
        got = [own, swap(own, 1), swap(own, 2)]
        got.append(jnp.concatenate([swap(got[1][:half], 2), swap(got[2][half:], 1)], axis=0))
        return got + [swap(own, k) for k in range(4, n_tp)]

    def exchange(blocks):
        return [blocks[0]] + [swap(blocks[k], k) for k in range(1, n_tp)]

    def total_of(parts):
        total = parts[0].astype(F32)
        for part in parts[1:]:
            total = total + part.astype(F32)
        return total

    def gather_pair(owns):
        got = [owns, [swap(own, 1) for own in owns], [swap(own, 2) for own in owns]]
        got.append([swap(got[1][0], 2)] + [swap(own, 1) for own in got[2][1:]])
        return got + [[swap(own, k) for own in owns] for k in range(4, n_tp)]

    def scatter_pair(blocks):
        first = swap(blocks[0][3], 1)
        seconds = [swap(blocks[m][3], 2) for m in range(1, MICRO)]
        to_two = total_of([blocks[0][2], first]).astype(BF16)
        to_one = [total_of([blocks[m][1], seconds[m - 1]]).astype(BF16) for m in range(1, MICRO)]
        yield [to_two] + to_one
        totals = []
        for m in range(MICRO):
            one = blocks[m][1] if m == 0 else to_one[m - 1]
            two = to_two if m == 0 else blocks[m][2]
            far = [swap(blocks[m][k], k) for k in range(4, n_tp)]
            totals.append(total_of([blocks[m][0], swap(one, 1), swap(two, 2)] + far))
        yield totals

    def line_sum(other, own):
        met = lax.ppermute(other, "dp", [(i, i ^ 1) for i in range(n_dp)])
        yield [met]

        def share(index):
            index = jnp.clip(index, 0, line - 1)
            return lax.dynamic_index_in_dim(own, index, 0, False).astype(
                F32
            ) + lax.dynamic_index_in_dim(met, index, 0, False).astype(F32)

        sends = []
        for far in range(1, line):
            for way in (far, -far):
                sends.append((way, share(place + way).astype(BF16)))
        yield [value for _, value in sends]
        total = share(place)
        for far in range(1, line):
            arrived = []
            for way, value in sends:
                if abs(way) == far:
                    pairs = [
                        (i, i + 2 * way) for i in range(n_dp) if 0 <= i + 2 * way < n_dp
                    ]
                    arrived.append(lax.ppermute(value, "dp", pairs))
            if far <= 3:
                yield arrived
            for value in arrived:
                total = total + value.astype(F32)
        yield [total]

    def my_half(value):
        return lax.dynamic_slice_in_dim(value, core * (depth // 2), depth // 2, axis=0)

    def swap_cores(value):
        return lax.ppermute(value, "dp", [(i, i ^ 1) for i in range(n_dp)])

    def both_halves(near, far):
        return jnp.where(
            core == 0,
            jnp.concatenate([near, far], axis=1),
            jnp.concatenate([far, near], axis=1),
        )

    def after(value, *earlier):
        return lax.optimization_barrier((value,) + earlier)[0]

    qkv_full = lax.all_gather(
        jnp.concatenate([w_query, w_keyval], axis=1), "dp", axis=0, tiled=True
    )
    gains_full = lax.all_gather(norm_gains, "dp", axis=1, tiled=True)
    out_t_full = lax.all_gather(w_output.T, "dp", axis=0, tiled=True)

    offsets = jnp.arange(CH, dtype=jnp.int32)
    all_pos = (span_order[:, None] * CH + offsets[None, :]).reshape(n_dp, parts, -1)
    all_pos = jnp.stack([all_pos[:, (rank % parts) ^ p] for p in range(parts)], axis=1)
    own_pos = lax.dynamic_slice_in_dim(all_pos, device, 1).reshape(-1)
    all_pos = all_pos.reshape(-1)
    qpos, kpos = own_pos[:, None], all_pos[None, :]
    kv_kinds = [True, False] * (kv_width // (2 * HD))
    cos_t, sin_t = lane_tables(own_pos, [True] * (q_width // HD) + kv_kinds)

    x = reorder(tokens.reshape(MICRO, n_tp, block_rows, depth))
    seed = reorder(cotangent.reshape(MICRO, n_tp, block_rows, depth))
    batch_rows = SEQS * span_rows
    rows = MICRO * batch_rows
    gain_one, gain_two = gains_full[0:1], gains_full[1:2]
    attn_in, qkv = project(x.reshape(rows, depth), gain_one, qkv_full, cos_t, sin_t)
    qkv = qkv.reshape(MICRO, SEQS, span_rows, q_width + kv_width)
    q, kv = qkv[..., :q_width], qkv[..., q_width:]
    kv_all = lax.all_gather(kv, "dp", axis=0, tiled=False)

    sub = min(SUB, hidden_width // CHUNKS)
    chunk = hidden_width // CHUNKS
    w_down_t = w_down.T
    mlp_full = []
    for c in range(CHUNKS):
        pieces = []
        for start in range(c * chunk, (c + 1) * chunk, sub):
            cols = slice(start, start + sub)
            pieces += [w_gateup[0][:, cols], w_gateup[1][:, cols], w_down_t[:, cols]]
        shard = jnp.concatenate(pieces, axis=1)
        mlp_full.append(lax.all_gather(shard, "dp", axis=0, tiled=True))

    attended = attend(qpos, kpos, q, kv_all, group)
    attended_blocks = attended.reshape(MICRO, n_tp, block_rows, q_width)
    out_near = my_half(out_t_full)
    out_near = jnp.concatenate([out_near] + [swap(out_near, k) for k in range(1, n_tp)], axis=1)
    out_far = swap_cores(out_near)
    heads_in = exchange([attended_blocks[:, k] for k in range(n_tp)])
    own_rows = MICRO * block_rows
    x_own = x[:, 0].reshape(own_rows, depth).astype(F32)
    heads_cat = jnp.concatenate([v.reshape(own_rows, q_width) for v in heads_in], axis=1)
    middle = x_own + both_halves(dot_nt(heads_cat, out_near), dot_nt(heads_cat, out_far))
    scale_two = mean_square_scale(middle)
    normed_two = middle * scale_two
    u_own = (normed_two * gain_two.astype(F32)).astype(BF16)
    batches = range(MICRO)
    gathered = [g.reshape(MICRO, block_rows, depth) for g in gather_blocks(u_own)]
    u = [jnp.concatenate([gathered[k][m] for k in range(n_tp)], axis=0) for m in batches]
    g = [seed[m].reshape(batch_rows, depth) for m in batches]

    qkv_half = after(my_half(qkv_full), u[0])
    quarter = depth // 4
    qkv_quarters = [qkv_half[:quarter], qkv_half[quarter:]]
    qkv_moves = [(k, i) for i in range(2) for k in range(1, min(n_tp, 3))]
    qkv_moves = [qkv_moves[:2], qkv_moves[2:]] + [
        [(k, i) for k in range(3, n_tp)] for i in range(2)
    ]
    qkv_got = {}

    def move_qkv():
        if not qkv_moves:
            return []
        now = qkv_moves.pop(0)
        for k, i in now:
            qkv_got[k, i] = swap(qkv_quarters[i], k)
        return [qkv_got[move] for move in now]

    def blocks_of(value):
        return [value[k * block_rows : (k + 1) * block_rows] for k in range(n_tp)]

    def own_part(value, m):
        return value[m * block_rows : (m + 1) * block_rows]

    core_index = core.astype(jnp.int32).reshape(1)
    gain_two_f = gain_two.astype(F32)
    gain_one_f = gain_one.astype(F32)
    cos_q, sin_q = cos_t[:, : group * HD], sin_t[:, : group * HD]
    cos_k, sin_k = cos_t[:, q_width:], sin_t[:, q_width:]
    gain_grads = [0.0, 0.0]
    sums = [None] * MICRO

    def expand(c, m, *earlier):
        hid, dgu, y_low, du_low = feed_forward(
            after(u[m], *earlier), g[m], mlp_full[c], sub, sums[m]
        )
        sums[m] = (y_low, du_low)
        return hid, dgu

    def close(hids, dgus, *earlier):
        (grads,) = outer_products(
            core_index, [after(u[0], *earlier)] + u[1:], g, hids, dgus, own_depth, sub, False
        )
        return grads, lax.psum_scatter(grads, "dp", scatter_dimension=0, tiled=False)

    chunk_grads = []
    earlier = []
    for c in range(CHUNKS - 1):
        hids, dgus = [], []
        for m in batches:
            hid, dgu = expand(c, m, *earlier)
            earlier = [hid] + move_qkv()
            hids.append(hid)
            dgus.append(dgu)
        grads, owned = close(hids, dgus, *earlier)
        earlier = [grads] + move_qkv()
        chunk_grads.append(owned)

    d_middles, d_mid_lows, d_attends, all_rows = [], [], [], []
    hids, dgus = [], []
    for m in batches:
        hid, dgu = expand(CHUNKS - 1, m, *earlier)
        earlier = [hid] + move_qkv()
        hids.append(hid)
        dgus.append(dgu)
    qkv_near = [qkv_half] + [
        jnp.concatenate([qkv_got[k, i] for i in range(2)], axis=0) for k in range(1, n_tp)
    ]
    qkv_near = after(jnp.concatenate(qkv_near, axis=1), *earlier)
    qkv_far = swap_cores(qkv_near)
    for m in batches:
        if m == 1:
            grads, owned = close(hids, dgus, all_rows[0], qkv_near)
            chunk_grads.append(owned)
            earlier = [grads, qkv_far]
        got = exchange(blocks_of(sums[m][1]))
        d_mixed = total_of([after(got[0], *(earlier if m else []))] + got[1:])
        normed = own_part(normed_two, m)
        gain_grads[1] = gain_grads[1] + jnp.sum(d_mixed * normed, axis=0)
        d_middle = seed[m, 0].astype(F32) + norm_back(
            d_mixed * gain_two_f, normed, own_part(scale_two, m)
        )
        d_mid_low = d_middle.astype(BF16)
        near, far = (
            lax.dynamic_slice_in_dim(d_mid_low, side * (depth // 2), depth // 2, axis=1)
            for side in (core, 1 - core)
        )
        do_rows = (dot(near, out_near) + dot(far, out_far)).astype(BF16)
        all_rows.append(do_rows)
        do_blocks = [do_rows[:, k * q_width : (k + 1) * q_width] for k in range(n_tp)]
        d_attends.append(jnp.concatenate(exchange(do_blocks), axis=0).reshape((1,) + q.shape[1:]))
        d_middles.append(d_middle)
        d_mid_lows.append(d_mid_low)

    y_stages = scatter_pair([blocks_of(after(sums[m][0], d_attends[-1])) for m in batches])
    y_sends = next(y_stages)
    d_queries, kv_stages = [], []
    for m in batches:
        waits = [all_rows[-1]] if m == 0 else y_sends
        d_query_low, d_kv_part = attend_back(
            qpos,
            kpos,
            cos_q,
            sin_q,
            q[m : m + 1],
            after(d_attends[m], *waits),
            kv_all[:, m : m + 1],
            group,
        )
        d_queries.append(d_query_low[0])
        by_core = d_kv_part.reshape((line, 2) + d_kv_part.shape[2:])
        kv_stages.append(
            line_sum(
                lax.dynamic_index_in_dim(by_core, 1 - core, 1, False),
                lax.dynamic_index_in_dim(by_core, core, 1, False),
            )
        )
    blocks_own = [own_part(middle, m) + total for m, total in enumerate(next(y_stages))]
    d_mid_rows = gather_pair([after(v, d_attends[-1]) for v in d_mid_lows])
    d_mid_rows = jnp.concatenate(
        [d_mid_rows[k][m] for m in batches for k in range(n_tp)], axis=0
    )
    out_rows = gather_pair([value.astype(BF16) for value in blocks_own])

    block_output = jnp.zeros((MICRO, n_tp, block_rows, depth), BF16)
    grad_tokens = jnp.zeros((MICRO, n_tp, block_rows, depth), F32)

    def placed(buffer, m, blocks):
        for k in range(n_tp):
            piece = blocks[k].astype(buffer.dtype)[None, None]
            buffer = lax.dynamic_update_slice(buffer, piece, (m, rank ^ k, 0, 0))
        return buffer

    lane = jnp.arange(kv_width)
    d_qkvs = []
    for m in batches:
        block_output = placed(block_output, m, [out_rows[k][m] for k in range(n_tp)])
        own_grad = list(kv_stages[m])[-1][0]
        own_grad = after(own_grad, *(blocks_own if m == 0 else []))
        scaled = own_grad * sin_k
        turned = jnp.where(
            lane % HD < HD // 2,
            jnp.roll(scaled, -(HD // 2), axis=-1),
            jnp.roll(scaled, HD // 2, axis=-1),
        )
        d_kv_low = (own_grad * cos_k + turned).astype(BF16)
        d_qkv = jnp.concatenate([d_queries[m], d_kv_low], axis=-1)
        d_qkv = d_qkv.reshape(batch_rows, q_width + kv_width)
        d_qkvs.append(d_qkv)
        d_heads = exchange(blocks_of(d_qkv))
        heads_cat = jnp.concatenate(d_heads, axis=1)
        d_act = both_halves(dot_nt(heads_cat, qkv_near), dot_nt(heads_cat, qkv_far))
        x_part = own_part(x_own, m)
        scale_one = mean_square_scale(x_part)
        normed_one = x_part * scale_one
        gain_grads[0] = gain_grads[0] + jnp.sum(d_act * normed_one, axis=0)
        tokens_own = d_middles[m] + norm_back(d_act * gain_one_f, normed_one, scale_one)
        tokens_low = tokens_own.astype(BF16)
        grad_tokens = placed(
            grad_tokens, m, [tokens_low] + [swap(tokens_low, k) for k in range(1, n_tp)]
        )
    mlp_grads = [v.reshape(own_depth, -1) for v in chunk_grads]
    block_output = block_output.reshape(rows, depth)
    grad_tokens = grad_tokens.reshape(rows, depth)

    out_grad_t = dot_tn(d_mid_rows, attended.reshape(rows, q_width)).astype(BF16)
    qkv_grad = dot_tn(attn_in, jnp.concatenate(d_qkvs, axis=0)).astype(BF16)
    gain_cols = jnp.stack(gain_grads, axis=1)
    gain_cols = jnp.pad(gain_cols, ((0, 0), (0, 126))).astype(BF16)
    attn_grads = lax.psum_scatter(
        after(jnp.concatenate([qkv_grad, out_grad_t, gain_cols], axis=1), *chunk_grads),
        "dp",
        scatter_dimension=0,
        tiled=True,
    )
    gain_part = attn_grads[:, 2 * q_width + kv_width :]
    gain_sum = gain_part.astype(F32)
    for k in range(1, n_tp):
        gain_sum = gain_sum + swap(gain_part, k).astype(F32)

    grad_query = attn_grads[:, :q_width].astype(F32)
    grad_keyval = attn_grads[:, q_width : q_width + kv_width].astype(F32)
    grad_output = attn_grads[:, q_width + kv_width : 2 * q_width + kv_width].astype(F32).T
    grad_gains = gain_sum[:, :2].T
    def with_update(gradient, old_mean, square, weight, decay):
        return (gradient,) + adam_update(gradient, old_mean, square, weight.astype(F32), decay)

    return (
        (block_output, grad_tokens)
        + with_update(grad_query, mean_query, square_query, w_query, weight_decay)
        + with_update(grad_keyval, mean_keyval, square_keyval, w_keyval, weight_decay)
        + with_update(grad_output, mean_output, square_output, w_output, weight_decay)
        + step_from_chunks(
            mlp_grads, mean_gateup, square_gateup, w_gateup, sub, 0, False, weight_decay
        )
        + step_from_chunks(mlp_grads, mean_down, square_down, w_down, sub, 2, True, weight_decay)
        + with_update(grad_gains, mean_gains, square_gains, norm_gains, 0.0)
    )


def solution(mesh):
    rows_first = P("dp", "tp")
    cols_last = P("tp", "dp")
    stacked = P(None, "dp", "tp")
    gains = P(None, "dp")
    token_rows = P("dp", None)
    placed = (
        (token_rows, token_rows, P())
        + (rows_first, rows_first, cols_last, stacked, cols_last, gains)
        + (rows_first,) * 4
        + (cols_last,) * 2
        + (stacked,) * 2
        + (cols_last,) * 2
        + (gains,) * 2
    )
    results = (
        (token_rows, token_rows)
        + (rows_first,) * 8
        + (cols_last,) * 4
        + (stacked,) * 4
        + (cols_last,) * 4
        + (gains,) * 4
    )
    return jax.shard_map(
        functools.partial(per_device, mesh.shape["dp"], mesh.shape["tp"]),
        mesh=mesh,
        in_specs=placed,
        out_specs=results,
        check_vma=False,
    )
```

```python
import functools

import jax
import jax.numpy as jnp
from jax import lax
from jax.experimental import pallas as pl
from jax.experimental.pallas import tpu as pltpu
from jax.sharding import PartitionSpec as P

HD = 64
CH = 64
SEQS = 4
MICRO = 2
STEP = 5
CHUNKS = 2
SUB = 512

norm_eps = 1e-05
rope_base = 500000.0
beta_one = 0.9
beta_two = 0.95
learn_rate = 0.01
weight_decay = 0.1
adam_eps = 1e-08
masked_score = -1e30

F32 = jnp.float32
BF16 = jnp.bfloat16
VMEM_LIMIT = 60 * 1024 * 1024
HINT = 20


def hint(flops, bytes_accessed, transcendentals):
    return pl.CostEstimate(
        flops=flops // HINT, bytes_accessed=bytes_accessed // HINT, transcendentals=transcendentals
    )


def lane_tables(positions, kinds):
    half_size = HD // 2
    frequencies = rope_base ** (-(jnp.arange(half_size, dtype=F32) * 2.0 / HD))
    angles = positions.astype(F32)[:, None] * frequencies[None, :]
    cos_half, sin_half = jnp.cos(angles), jnp.sin(angles)
    cos_head = jnp.concatenate([cos_half, cos_half], axis=-1)
    sin_head = jnp.concatenate([-sin_half, sin_half], axis=-1)
    ones, zeros = jnp.ones_like(cos_head), jnp.zeros_like(cos_head)
    cos_all, sin_all = [], []
    for kind in kinds:
        cos_all.append(cos_head if kind else ones)
        sin_all.append(sin_head if kind else zeros)
    return jnp.concatenate(cos_all, axis=-1), jnp.concatenate(sin_all, axis=-1)


def half_turn(values):
    width = values.shape[-1]
    axis = values.ndim - 1
    lane = lax.broadcasted_iota(jnp.int32, values.shape, axis)
    ahead = pltpu.roll(values, width - HD // 2, axis)
    behind = pltpu.roll(values, HD // 2, axis)
    return jnp.where(lane % HD < HD // 2, ahead, behind)


def mean_square_scale(values):
    return lax.rsqrt(jnp.mean(values * values, axis=-1, keepdims=True) + norm_eps)


def project_kernel(x_ref, gain_ref, w_ref, cos_ref, sin_ref, a_ref, qkv_ref):
    x = x_ref[...].astype(F32)
    a = (x * mean_square_scale(x) * gain_ref[...].astype(F32)).astype(BF16)
    a_ref[...] = a
    t = jnp.dot(a, w_ref[...], preferred_element_type=F32)
    qkv_ref[...] = (t * cos_ref[...] + half_turn(t) * sin_ref[...]).astype(BF16)


def project(x, gain, weight, cos_t, sin_t):
    rows, depth = x.shape
    width = weight.shape[1]
    block = cos_t.shape[0]
    return pl.pallas_call(
        project_kernel,
        grid=(rows // block,),
        in_specs=[
            pl.BlockSpec((block, depth), lambda i: (i, 0)),
            pl.BlockSpec((1, depth), lambda i: (0, 0)),
            pl.BlockSpec((depth, width), lambda i: (0, 0)),
            pl.BlockSpec((block, width), lambda i: (0, 0)),
            pl.BlockSpec((block, width), lambda i: (0, 0)),
        ],
        out_specs=[
            pl.BlockSpec((block, depth), lambda i: (i, 0)),
            pl.BlockSpec((block, width), lambda i: (i, 0)),
        ],
        out_shape=[
            jax.ShapeDtypeStruct((rows, depth), BF16),
            jax.ShapeDtypeStruct((rows, width), BF16),
        ],
        compiler_params=pltpu.CompilerParams(vmem_limit_bytes=VMEM_LIMIT),
        cost_estimate=hint(
            flops=2 * rows * depth * width, bytes_accessed=4 * rows * depth, transcendentals=0
        ),
        name="project",
    )(x, gain, weight, cos_t, sin_t)


def stack_heads(block, group, upper):
    lane = lax.broadcasted_iota(jnp.int32, (block.shape[0], 2 * HD), 1)
    keep = (lane >= HD) if upper else (lane < HD)
    parts = []
    for head in range(group):
        pair = block[:, (head // 2) * 2 * HD : (head // 2 + 1) * 2 * HD].astype(F32)
        if (head % 2 == 1) != upper:
            pair = pltpu.roll(pair, HD, 1)
        parts.append(jnp.where(keep, pair, 0.0).astype(BF16))
    return jnp.concatenate(parts, axis=0)


def unstack_heads(stacked, group, upper):
    rows = stacked.shape[0] // group
    lane = lax.broadcasted_iota(jnp.int32, (rows, 2 * HD), 1)
    pairs = []
    for pair in range(group // 2):
        even = stacked[(2 * pair) * rows : (2 * pair + 1) * rows]
        odd = stacked[(2 * pair + 1) * rows : (2 * pair + 2) * rows]
        if upper:
            even = pltpu.roll(even, HD, 1)
        else:
            odd = pltpu.roll(odd, HD, 1)
        pairs.append(jnp.where(lane < HD, even, odd))
    return jnp.concatenate(pairs, axis=1)


def scores_and_probs(q_pad, keys, qpos, kpos, group):
    scores = (
        lax.dot_general(q_pad, keys, (((1,), (1,)), ((), ())), preferred_element_type=F32)
        * HD ** (-0.5)
    )
    rows = qpos.shape[0]
    blocked = kpos > qpos
    masked = [
        jnp.where(blocked, masked_score, scores[h * rows : (h + 1) * rows]) for h in range(group)
    ]
    scores = jnp.concatenate(masked, axis=0)
    exponent = jnp.exp(scores - jnp.max(scores, axis=-1, keepdims=True))
    return exponent * (1.0 / jnp.sum(exponent, axis=-1, keepdims=True))


def attend_kernel(group, qpos_ref, kpos_ref, q_ref, kv_ref, o_ref):
    keyvals = kv_ref[...].reshape(-1, 2 * HD)
    q_pad = stack_heads(q_ref[...].reshape(-1, group * HD), group, False)
    probs = scores_and_probs(q_pad, keyvals, qpos_ref[...], kpos_ref[...], group)
    out = jnp.dot(probs.astype(BF16), keyvals, preferred_element_type=F32)
    o_ref[...] = unstack_heads(out, group, True).astype(BF16).reshape(o_ref.shape)


def attend_back_kernel(
    group, qpos_ref, kpos_ref, cos_ref, sin_ref, q_ref, do_ref, kv_ref, dq_ref, dkv_ref
):
    keyvals = kv_ref[...].reshape(-1, 2 * HD)
    q_pad = stack_heads(q_ref[...].reshape(-1, group * HD), group, False)
    do_pad = stack_heads(do_ref[...].reshape(-1, group * HD), group, True)
    probs = scores_and_probs(q_pad, keyvals, qpos_ref[...], kpos_ref[...], group)
    d_probs = lax.dot_general(
        do_pad, keyvals, (((1,), (1,)), ((), ())), preferred_element_type=F32
    )
    d_scores = probs * (d_probs - jnp.sum(d_probs * probs, axis=-1, keepdims=True))
    ds_low = d_scores.astype(BF16) * HD ** (-0.5)
    dq = jnp.dot(ds_low, keyvals, preferred_element_type=F32)
    dq = unstack_heads(dq, group, False)
    dq = dq * cos_ref[...] + half_turn(dq * sin_ref[...])
    dq_ref[...] = dq.astype(BF16).reshape(dq_ref.shape)
    contract = (((0,), (0,)), ((), ()))
    d_keyvals = lax.dot_general(
        ds_low, q_pad, contract, preferred_element_type=F32
    ) + lax.dot_general(probs.astype(BF16), do_pad, contract, preferred_element_type=F32)
    dkv_ref[...] = d_keyvals.astype(BF16).reshape(dkv_ref.shape)


def attention_specs(qkv_heads, n_dp, span_rows, group):
    q_spec = pl.BlockSpec((1, 1, span_rows, group * HD), lambda m, s, h: (m, s, 0, h))
    kv_spec = pl.BlockSpec(
        (n_dp, 1, 1, span_rows, 2 * HD), lambda m, s, h: (0, m, s, 0, h)
    )
    pos_q = pl.BlockSpec((span_rows, 1), lambda m, s, h: (0, 0))
    pos_k = pl.BlockSpec((1, n_dp * span_rows), lambda m, s, h: (0, 0))
    return q_spec, kv_spec, pos_q, pos_k


def attend(qpos, kpos, q, kv, group):
    micro, seqs, span_rows, width = q.shape
    n_dp, heads = kv.shape[0], width // (group * HD)
    q_spec, kv_spec, pos_q, pos_k = attention_specs(heads, n_dp, span_rows, group)
    return pl.pallas_call(
        functools.partial(attend_kernel, group),
        grid=(micro, seqs, heads),
        in_specs=[pos_q, pos_k, q_spec, kv_spec],
        out_specs=q_spec,
        out_shape=jax.ShapeDtypeStruct(q.shape, BF16),
        compiler_params=pltpu.CompilerParams(vmem_limit_bytes=VMEM_LIMIT),
        cost_estimate=hint(
            flops=16 * micro * seqs * span_rows * width * n_dp * span_rows,
            bytes_accessed=4 * q.size + 2 * kv.size,
            transcendentals=0,
        ),
        name="attend",
    )(qpos, kpos, q, kv)


def attend_back(qpos, kpos, cos_q, sin_q, q, d_out, kv, group):
    micro, seqs, span_rows, width = q.shape
    n_dp, heads = kv.shape[0], width // (group * HD)
    q_spec, kv_spec, pos_q, pos_k = attention_specs(heads, n_dp, span_rows, group)
    table = pl.BlockSpec((span_rows, group * HD), lambda m, s, h: (0, 0))
    return pl.pallas_call(
        functools.partial(attend_back_kernel, group),
        grid=(micro, seqs, heads),
        in_specs=[pos_q, pos_k, table, table, q_spec, q_spec, kv_spec],
        out_specs=[q_spec, kv_spec],
        out_shape=[
            jax.ShapeDtypeStruct(q.shape, BF16),
            jax.ShapeDtypeStruct(kv.shape, BF16),
        ],
        compiler_params=pltpu.CompilerParams(vmem_limit_bytes=VMEM_LIMIT),
        cost_estimate=hint(
            flops=40 * micro * seqs * span_rows * width * n_dp * span_rows,
            bytes_accessed=6 * q.size + 4 * kv.size,
            transcendentals=0,
        ),
        name="attend_back",
    )(qpos, kpos, cos_q, sin_q, q, d_out, kv)


def norm_back(d_normed, normed, scale):
    return scale * (d_normed - normed * jnp.mean(d_normed * normed, axis=-1, keepdims=True))


def adam_update(gradient, old_mean, square, weight, decay_factor):
    moment = beta_one * old_mean + (1.0 - beta_one) * gradient
    spread = beta_two * square + (1.0 - beta_two) * gradient * gradient
    change = -learn_rate * (
        moment / (1.0 - beta_one**STEP) / (jnp.sqrt(spread / (1.0 - beta_two**STEP)) + adam_eps)
        + decay_factor * weight
    )
    return (moment, spread, change)


def dot(left, right):
    return jnp.dot(left, right, preferred_element_type=F32)


def dot_nt(left, right):
    return lax.dot_general(left, right, (((1,), (1,)), ((), ())), preferred_element_type=F32)


def dot_tn(left, right):
    return lax.dot_general(left, right, (((0,), (0,)), ((), ())), preferred_element_type=F32)


def gated_kernel(last, steps, u_ref, g_ref, w_ref, *refs):
    if last:
        y_old, du_old, hid_ref, dgu_ref, y_out, du_out, y_sum, du_sum, y_low, du_low, sem = refs
    else:
        hid_ref, dgu_ref, y_out, du_out, y_sum, du_sum, y_low, du_low, sem = refs
    step = pl.program_id(0)
    depth = w_ref.shape[0]
    sub = hid_ref.shape[1]
    cols = min(512, depth)

    @pl.when(step == 0)
    def _():
        y_sum[...] = jnp.zeros_like(y_sum)
        du_sum[...] = jnp.zeros_like(du_sum)
        if last:
            pltpu.make_async_copy(y_old, y_low, sem.at[0]).start()
            pltpu.make_async_copy(du_old, du_low, sem.at[1]).start()

    gate_proj = dot(u_ref[...], w_ref[:, :sub])
    up_proj = dot(u_ref[...], w_ref[:, sub : 2 * sub])
    sigmoid_gate = jax.nn.sigmoid(gate_proj)
    silu_gate = gate_proj * sigmoid_gate
    hid_ref[...] = (silu_gate * up_proj).astype(BF16)
    d_hidden = dot(g_ref[...], w_ref[:, 2 * sub :])
    d_gate = d_hidden * up_proj * sigmoid_gate * (1.0 + gate_proj * (1.0 - sigmoid_gate))
    dgu_ref[:, :sub] = d_gate.astype(BF16)
    dgu_ref[:, sub:] = (d_hidden * silu_gate).astype(BF16)
    for start in range(0, depth, cols):
        part = slice(start, start + cols)
        du_sum[:, part] += dot_nt(dgu_ref[...], w_ref[part, : 2 * sub])
        y_sum[:, part] += dot_nt(hid_ref[...], w_ref[part, 2 * sub :])

    @pl.when(step == steps - 1)
    def _():
        copy_y = pltpu.make_async_copy(y_low, y_out, sem.at[0])
        copy_du = pltpu.make_async_copy(du_low, du_out, sem.at[1])
        if last:
            pltpu.make_async_copy(y_old, y_low, sem.at[0]).wait()
            pltpu.make_async_copy(du_old, du_low, sem.at[1]).wait()
            du_low[...] = (du_sum[...] + du_low[...].astype(F32)).astype(BF16)
            copy_du.start()
            y_low[...] = (y_sum[...] + y_low[...].astype(F32)).astype(BF16)
        else:
            du_low[...] = du_sum[...].astype(BF16)
            copy_du.start()
            y_low[...] = y_sum[...].astype(BF16)
        copy_y.start()
        copy_du.wait()
        copy_y.wait()


def feed_forward(u, g, weights, sub, sums):
    rows, depth = u.shape
    steps = weights.shape[1] // (3 * sub)
    last = sums is not None
    whole = functools.partial(pl.BlockSpec, pipeline_mode=pl.Buffered(1))
    anywhere = pl.BlockSpec(memory_space=pl.ANY)
    return pl.pallas_call(
        functools.partial(gated_kernel, last, steps),
        grid=(steps,),
        in_specs=[
            whole((rows, depth), lambda j: (0, 0)),
            whole((rows, depth), lambda j: (0, 0)),
            pl.BlockSpec((depth, 3 * sub), lambda j: (0, j)),
        ]
        + ([anywhere, anywhere] if last else []),
        out_specs=[
            pl.BlockSpec((rows, sub), lambda j: (0, j)),
            pl.BlockSpec((rows, 2 * sub), lambda j: (0, j)),
            anywhere,
            anywhere,
        ],
        out_shape=[
            jax.ShapeDtypeStruct((rows, steps * sub), BF16),
            jax.ShapeDtypeStruct((rows, 2 * steps * sub), BF16),
            jax.ShapeDtypeStruct((rows, depth), BF16),
            jax.ShapeDtypeStruct((rows, depth), BF16),
        ],
        scratch_shapes=[
            pltpu.VMEM((rows, depth), F32),
            pltpu.VMEM((rows, depth), F32),
            pltpu.VMEM((rows, depth), BF16),
            pltpu.VMEM((rows, depth), BF16),
            pltpu.SemaphoreType.DMA((2,)),
        ],
        compiler_params=pltpu.CompilerParams(vmem_limit_bytes=VMEM_LIMIT),
        cost_estimate=hint(
            flops=12 * rows * depth * steps * sub,
            bytes_accessed=2 * weights.size + 8 * rows * depth,
            transcendentals=0,
        ),
        name="feed_forward",
    )(u, g, weights, *(sums if last else ()))


def outer_kernel(batches, sub, steps, half, core_ref, *refs):
    u_refs, g_refs = refs[:batches], refs[batches : 2 * batches]
    hid_refs, dgu_refs = refs[2 * batches : 3 * batches], refs[3 * batches : 4 * batches]
    outs = refs[4 * batches :]

    def products(out_ref):
        for j in range(steps):
            both = slice(2 * j * sub, 2 * (j + 1) * sub)
            one = slice(j * sub, (j + 1) * sub)
            total = dot_tn(u_refs[0][...], dgu_refs[0][:, both])
            for m in range(1, batches):
                total += dot_tn(u_refs[m][...], dgu_refs[m][:, both])
            out_ref[0, :, 3 * j * sub : 3 * j * sub + 2 * sub] = total.astype(BF16)
            total = dot_tn(g_refs[0][...], hid_refs[0][:, one])
            for m in range(1, batches):
                total += dot_tn(g_refs[m][...], hid_refs[m][:, one])
            out_ref[0, :, 3 * j * sub + 2 * sub : 3 * (j + 1) * sub] = total.astype(BF16)

    if len(outs) == 1:
        products(outs[0])
    else:

        @pl.when(pl.program_id(0) < half)
        def _():
            products(outs[0])

        @pl.when(pl.program_id(0) >= half)
        def _():
            products(outs[1])


def outer_products(core, us, gs, hids, dgus, own, sub, split):
    batches = len(us)
    rows, depth = us[0].shape
    n_dp = depth // own
    half = n_dp // 2
    width = hids[0].shape[1]
    steps = width // sub
    if split:

        def place(i, core_ref):
            mine = jnp.where(i < half, 1 - core_ref[0], core_ref[0])
            return (i % half) * 2 + mine

        out_specs = [
            pl.BlockSpec((1, own, 3 * width), lambda i, r: (jnp.minimum(i, half - 1), 0, 0)),
            pl.BlockSpec((1, own, 3 * width), lambda i, r: (jnp.maximum(i - half, 0), 0, 0)),
        ]
        out_shape = [jax.ShapeDtypeStruct((half, own, 3 * width), BF16)] * 2
    else:

        def place(i, core_ref):
            return i

        out_specs = [pl.BlockSpec((1, own, 3 * width), lambda i, r: (i, 0, 0))]
        out_shape = [jax.ShapeDtypeStruct((n_dp, own, 3 * width), BF16)]
    whole = functools.partial(pl.BlockSpec, pipeline_mode=pl.Buffered(1))
    column = pl.BlockSpec((rows, own), lambda i, r: (0, place(i, r)))
    return pl.pallas_call(
        functools.partial(outer_kernel, batches, sub, steps, half),
        grid_spec=pltpu.PrefetchScalarGridSpec(
            num_scalar_prefetch=1,
            grid=(n_dp,),
            in_specs=[column] * (2 * batches)
            + [whole((rows, width), lambda i, r: (0, 0))] * batches
            + [whole((rows, 2 * width), lambda i, r: (0, 0))] * batches,
            out_specs=out_specs,
        ),
        out_shape=out_shape,
        compiler_params=pltpu.CompilerParams(vmem_limit_bytes=VMEM_LIMIT),
        cost_estimate=hint(
            flops=6 * rows * batches * depth * width,
            bytes_accessed=6 * depth * width,
            transcendentals=0,
        ),
        name="outer_products",
    )(core, *us, *gs, *hids, *dgus)


def step_kernel(turned, decay, steps, chunks, *refs):
    grads = refs[:chunks]
    mean_ref, square_ref, weight_ref, grad_ref, moment_ref, spread_ref, update_ref = refs[chunks:]
    place = pl.program_id(1)
    for c in range(chunks):

        @pl.when(place // steps == c)
        def _(c=c):
            gradient = grads[c][...].astype(F32)
            if turned:
                gradient = gradient.T
            gradient = gradient.reshape(grad_ref.shape)
            moment, spread, change = adam_update(
                gradient, mean_ref[...], square_ref[...], weight_ref[...].astype(F32), decay
            )
            grad_ref[...] = gradient
            moment_ref[...] = moment
            spread_ref[...] = spread
            update_ref[...] = change


def step_from_chunks(grads, old_mean, square, weight, sub, offset, turned, decay):
    chunks, own = len(grads), grads[0].shape[0]
    steps = grads[0].shape[1] // (3 * sub)

    def grad_spec(c):
        def index(i, p):
            j = jnp.clip(p - c * steps, 0, steps - 1)
            return (0, 3 * j + i + offset)

        return pl.BlockSpec((own, sub), index)

    if turned:
        lead, spec = 1, pl.BlockSpec((sub, own), lambda i, p: (p, 0))
    else:
        lead, spec = old_mean.shape[0], pl.BlockSpec((1, own, sub), lambda i, p: (i, 0, p))
    return tuple(
        pl.pallas_call(
            functools.partial(step_kernel, turned, decay, steps, chunks),
            grid=(lead, chunks * steps),
            in_specs=[grad_spec(c) for c in range(chunks)] + [spec] * 3,
            out_specs=[spec] * 4,
            out_shape=[jax.ShapeDtypeStruct(old_mean.shape, F32)] * 4,
            compiler_params=pltpu.CompilerParams(vmem_limit_bytes=VMEM_LIMIT),
            cost_estimate=hint(
                flops=20 * old_mean.size, bytes_accessed=28 * old_mean.size, transcendentals=0
            ),
            name="weight_step",
        )(*grads, old_mean, square, weight)
    )


def paired(index, k):
    bit = 1
    while bit <= k:
        if k & bit:
            index = index + bit - 2 * bit * ((index // bit) % 2)
        bit *= 2
    return index


def tail_kernel(n_dp, n_tp, group, *refs):
    (
        du_refs,
        y_refs,
        seed_ref,
        middle_ref,
        x_ref,
        gains_ref,
        out_refs,
        qkv_refs,
        q_ref,
        kv_ref,
        qpos_ref,
        kpos_ref,
        cos_ref,
        sin_ref,
        d_qkv_ref,
        mid_rows,
        out_rows,
        tok_rows,
        gain_ref,
    ) = (refs[0:2], refs[2:4]) + refs[4:8] + (refs[8:10], refs[10:12]) + refs[12:23]
    (
        weights,
        du_got,
        y_got,
        own_mid,
        mid_low,
        block_low,
        tok_low,
        do_send,
        do_got,
        shares,
        met,
        z_send,
        z_got,
        heads_got,
        local_sem,
        du_s,
        du_r,
        y_s,
        y_r,
        mid_s,
        mid_r,
        block_s,
        block_r,
        tok_s,
        tok_r,
        do_s,
        do_r,
        core_s,
        core_r,
        z_s,
        z_r,
        heads_s,
        heads_r,
    ) = refs[23:]
    line = n_dp // 2
    batches = range(MICRO)
    others = range(1, n_tp)
    dp, tp = lax.axis_index("dp"), lax.axis_index("tp")
    place, core = dp // 2, dp % 2
    depth = middle_ref.shape[1]
    rows = mid_low.shape[1]
    seq_rows = q_ref.shape[2]
    q_width = q_ref.shape[3]
    kv_width = kv_ref.shape[4]
    width = q_width + kv_width
    half = depth // 2

    def rank(k):
        return (dp, paired(tp, k))

    def spot(k):
        return (paired(place, k) * 2 + core, tp)

    other_core = (place * 2 + 1 - core, tp)

    def remote(src, dst, send, recv, device):
        return pltpu.make_async_remote_copy(
            src_ref=src,
            dst_ref=dst,
            send_sem=send,
            recv_sem=recv,
            device_id=device,
            device_id_type=pl.DeviceIdType.MESH,
        )

    def block(k):
        return pl.ds(k * rows, rows)

    du_moves = [
        [
            remote(
                du_refs[m].at[block(k)], du_got.at[m, k], du_s.at[m, k], du_r.at[m, k], rank(k)
            )
            for k in others
        ]
        for m in batches
    ]
    y_moves = [
        [
            remote(y_refs[m].at[block(k)], y_got.at[m, k], y_s.at[m, k], y_r.at[m, k], rank(k))
            for k in others
        ]
        for m in batches
    ]

    def row_moves(low, got, send, recv):
        return [
            [
                remote(low.at[m], got.at[m, k], send.at[m, k], recv.at[m, k], rank(k))
                for k in others
            ]
            for m in batches
        ]

    mid_moves = row_moves(mid_low, mid_rows, mid_s, mid_r)
    block_moves = row_moves(block_low, out_rows, block_s, block_r)
    tok_moves = row_moves(tok_low, tok_rows, tok_s, tok_r)
    do_moves = [
        [
            remote(
                do_send.at[m, k], do_got.at[m, block(k)], do_s.at[m, k], do_r.at[m, k], rank(k)
            )
            for k in others
        ]
        for m in batches
    ]
    core_moves = [
        remote(shares.at[m, 1 - core], met.at[m], core_s.at[m], core_r.at[m], other_core)
        for m in batches
    ]
    z_moves = [
        [
            remote(z_send.at[m, k], z_got.at[m, k], z_s.at[m, k], z_r.at[m, k], spot(k))
            for k in range(1, line)
        ]
        for m in batches
    ]
    heads_moves = [
        [
            remote(
                d_qkv_ref.at[m, block(k)],
                heads_got.at[m, k],
                heads_s.at[m, k],
                heads_r.at[m, k],
                rank(k),
            )
            for k in others
        ]
        for m in batches
    ]

    def start(moves):
        for move in moves:
            move.start()

    def arrive(moves):
        for move in moves:
            move.wait_recv()

    def sent(moves):
        for move in moves:
            move.wait_send()

    own_copies = [
        pltpu.make_async_copy(ref.at[pl.ds(0, rows)], got.at[m, 0], local_sem.at[i, m])
        for i, (pair, got) in enumerate(((du_refs, du_got), (y_refs, y_got)))
        for m, ref in enumerate(pair)
    ]
    load_out = [
        pltpu.make_async_copy(
            ref, weights.at[side, :, pl.ds(0, n_tp * q_width)], local_sem.at[6, side]
        )
        for side, ref in enumerate(out_refs)
    ]
    load_qkv = [
        pltpu.make_async_copy(ref, weights.at[side], local_sem.at[2, side])
        for side, ref in enumerate(qkv_refs)
    ]
    keep = [
        [
            pltpu.make_async_copy(low.at[m], got.at[m, 0], local_sem.at[3 + i, m])
            for m in batches
        ]
        for i, (low, got) in enumerate(
            ((mid_low, mid_rows), (block_low, out_rows), (tok_low, tok_rows))
        )
    ]

    barrier = pltpu.get_barrier_semaphore()
    peers = [rank(k) for k in others] + [other_core] + [spot(k) for k in range(1, line)]
    for peer in peers:
        pl.semaphore_signal(barrier, inc=1, device_id=peer, device_id_type=pl.DeviceIdType.MESH)
    pl.semaphore_wait(barrier, len(peers))

    for moves in du_moves:
        start(moves)
    start(own_copies)
    start(load_out)
    gain_one = gains_ref[0:1, :].astype(F32)
    gain_two = gains_ref[1:2, :].astype(F32)
    gain_ref[...] = jnp.zeros_like(gain_ref)

    def total_of(got, m):
        total = got[m, 0].astype(F32)
        for k in others:
            total = total + got[m, k].astype(F32)
        return total

    for copy in own_copies:
        copy.wait()
    for m in batches:
        part = slice(m * rows, (m + 1) * rows)
        arrive(du_moves[m])
        d_mixed = total_of(du_got, m)
        middle = middle_ref[part, :]
        scale = mean_square_scale(middle)
        normed = middle * scale
        gain_ref[1:2, :] += jnp.sum(d_mixed * normed, axis=0, keepdims=True)
        d_middle = seed_ref[part, :].astype(F32) + norm_back(d_mixed * gain_two, normed, scale)
        own_mid[m] = d_middle
        mid_low[m] = d_middle.astype(BF16)
        if m == 0:
            for copy in load_out:
                copy.wait()
        near_cols = pl.ds(pl.multiple_of(core * half, half), half)
        far_cols = pl.ds(pl.multiple_of((1 - core) * half, half), half)
        near, far = mid_low[m, :, near_cols], mid_low[m, :, far_cols]
        for k in range(n_tp):
            lanes = slice(k * q_width, (k + 1) * q_width)
            rows_out = (dot(near, weights[0, :, lanes]) + dot(far, weights[1, :, lanes])).astype(
                BF16
            )
            if k == 0:
                do_got[m, 0:rows, :] = rows_out
            else:
                do_send[m, k] = rows_out
        start(do_moves[m])
    start(load_qkv)
    for m in batches:
        start(mid_moves[m])
        keep[0][m].start()
        start(y_moves[m])

    def attend_back_seq(m, s):
        seq = pl.ds(s * seq_rows, seq_rows)
        for h in range(kv_width // (2 * HD)):
            pair = slice(h * 2 * HD, (h + 1) * 2 * HD)
            keyvals = kv_ref[:, m, s, :, pair].reshape(-1, 2 * HD)
            grads = None
            for part in range(group // 2):
                lanes = slice((h * group + 2 * part) * HD, (h * group + 2 * part + 2) * HD)
                q_pad = stack_heads(q_ref[m, s, :, lanes], 2, False)
                do_pad = stack_heads(do_got[m, seq, lanes], 2, True)
                probs = scores_and_probs(q_pad, keyvals, qpos_ref[...], kpos_ref[...], 2)
                d_probs = dot_nt(do_pad, keyvals)
                d_scores = probs * (d_probs - jnp.sum(d_probs * probs, axis=-1, keepdims=True))
                ds_low = d_scores.astype(BF16) * HD ** (-0.5)
                dq = unstack_heads(dot(ds_low, keyvals), 2, False)
                cos_q, sin_q = cos_ref[:, 0 : 2 * HD], sin_ref[:, 0 : 2 * HD]
                dq = dq * cos_q + half_turn(dq * sin_q)
                d_qkv_ref[m, seq, lanes] = dq.astype(BF16)
                term = dot_tn(ds_low, q_pad) + dot_tn(probs.astype(BF16), do_pad)
                grads = term if grads is None else grads + term
            grads = grads.astype(BF16)
            for i in range(n_dp):
                shares[m, i % 2, i // 2, seq, pair] = grads[i * seq_rows : (i + 1) * seq_rows]

    def attend_back_range(m, low, high):
        @pl.loop(low, high)
        def _(s):
            attend_back_seq(m, s)

    def send_along(m):
        arrive([core_moves[m]])
        for k in range(1, line):
            there = paired(place, k)
            z_send[m, k] = (
                shares[m, core, there].astype(F32) + met[m, there].astype(F32)
            ).astype(BF16)
        start(z_moves[m])

    def close_keys(m):
        arrive(z_moves[m])
        total = shares[m, core, place].astype(F32) + met[m, place].astype(F32)
        for k in range(1, line):
            total = total + z_got[m, k].astype(F32)
        cos_k, sin_k = cos_ref[:, q_width:], sin_ref[:, q_width:]
        for s in range(SEQS):
            seq = slice(s * seq_rows, (s + 1) * seq_rows)
            grad = total[seq]
            d_qkv_ref[m, seq, q_width:] = (grad * cos_k + half_turn(grad * sin_k)).astype(BF16)
        start(heads_moves[m])

    def close_block(m):
        arrive(y_moves[m])
        part = slice(m * rows, (m + 1) * rows)
        block_low[m] = (middle_ref[part, :] + total_of(y_got, m)).astype(BF16)
        start(block_moves[m])
        keep[1][m].start()

    def close_tokens(m):
        arrive(heads_moves[m])
        part = slice(m * rows, (m + 1) * rows)
        heads = [d_qkv_ref[m, 0:rows, :]] + [heads_got[m, k] for k in others]
        sides = []
        for side in range(2):
            total = dot_nt(heads[0], weights[side, :, 0:width])
            for k in others:
                total = total + dot_nt(heads[k], weights[side, :, k * width : (k + 1) * width])
            sides.append(total)
        d_act = jnp.where(
            core == 0,
            jnp.concatenate(sides, axis=1),
            jnp.concatenate(sides[::-1], axis=1),
        )
        x_part = x_ref[part, :].astype(F32)
        scale = mean_square_scale(x_part)
        normed = x_part * scale
        gain_ref[0:1, :] += jnp.sum(d_act * normed, axis=0, keepdims=True)
        tok_low[m] = (own_mid[m] + norm_back(d_act * gain_one, normed, scale)).astype(BF16)
        start(tok_moves[m])
        keep[2][m].start()

    arrive(do_moves[0])
    attend_back_range(0, 0, SEQS)
    core_moves[0].start()
    arrive(do_moves[1])
    attend_back_range(1, 0, SEQS // 2)
    send_along(0)
    attend_back_range(1, SEQS // 2, SEQS)
    core_moves[1].start()
    for copy in load_qkv:
        copy.wait()
    close_keys(0)
    send_along(1)
    close_tokens(0)
    close_block(0)
    close_keys(1)
    close_tokens(1)
    close_block(1)
    for m in batches:
        for moves in (mid_moves[m], block_moves[m], tok_moves[m]):
            arrive(moves)
            sent(moves)
        for moves in (du_moves[m], y_moves[m], do_moves[m], [core_moves[m]], z_moves[m]):
            sent(moves)
        sent(heads_moves[m])
        for copies in keep:
            copies[m].wait()


def tail(
    n_dp, n_tp, group, sums, seed, middle, x, gains, out_w, qkv_w, q, kv, qpos, kpos, cos, sin
):
    own_rows, depth = middle.shape
    rows = own_rows // MICRO
    batch_rows = n_tp * rows
    line = n_dp // 2
    q_width, kv_width = q.shape[3], kv.shape[4]
    width = q_width + kv_width
    anywhere = pl.BlockSpec(memory_space=pl.ANY)
    vmem = pl.BlockSpec(memory_space=pltpu.VMEM)
    dma = pltpu.SemaphoreType.DMA
    gathered = jax.ShapeDtypeStruct((MICRO, n_tp, rows, depth), BF16)
    return pl.pallas_call(
        functools.partial(tail_kernel, n_dp, n_tp, group),
        in_specs=[anywhere] * 4 + [vmem] * 4 + [anywhere] * 4 + [vmem] * 6,
        out_specs=[vmem] + [anywhere] * 3 + [vmem],
        out_shape=[
            jax.ShapeDtypeStruct((MICRO, batch_rows, width), BF16),
            gathered,
            gathered,
            gathered,
            jax.ShapeDtypeStruct((2, depth), F32),
        ],
        scratch_shapes=[
            pltpu.VMEM((2, depth // 2, n_tp * width), BF16),
            pltpu.VMEM((MICRO, n_tp, rows, depth), BF16),
            pltpu.VMEM((MICRO, n_tp, rows, depth), BF16),
            pltpu.VMEM((MICRO, rows, depth), F32),
            pltpu.VMEM((MICRO, rows, depth), BF16),
            pltpu.VMEM((MICRO, rows, depth), BF16),
            pltpu.VMEM((MICRO, rows, depth), BF16),
            pltpu.VMEM((MICRO, n_tp, rows, q_width), BF16),
            pltpu.VMEM((MICRO, batch_rows, q_width), BF16),
            pltpu.VMEM((MICRO, 2, line, batch_rows, kv_width), BF16),
            pltpu.VMEM((MICRO, line, batch_rows, kv_width), BF16),
            pltpu.VMEM((MICRO, line, batch_rows, kv_width), BF16),
            pltpu.VMEM((MICRO, line, batch_rows, kv_width), BF16),
            pltpu.VMEM((MICRO, n_tp, rows, width), BF16),
            dma((7, 2)),
        ]
        + [dma((MICRO, n_tp))] * 12
        + [dma((MICRO,))] * 2
        + [dma((MICRO, line))] * 2
        + [dma((MICRO, n_tp))] * 2,
        compiler_params=pltpu.CompilerParams(
            collective_id=0, has_side_effects=True, vmem_limit_bytes=VMEM_LIMIT
        ),
        cost_estimate=hint(
            flops=10**10,
            bytes_accessed=10**8,
            transcendentals=0,
        ),
        name="tail",
    )(
        sums[0][1],
        sums[1][1],
        sums[0][0],
        sums[1][0],
        seed,
        middle,
        x,
        gains,
        *out_w,
        *qkv_w,
        q,
        kv,
        qpos,
        kpos,
        cos,
        sin,
    )


def spread_kernel(rank_ref, out_ref, tok_ref, block_ref, grad_ref):
    block_ref[...] = out_ref[...]
    grad_ref[...] = tok_ref[...].astype(F32)


def spread(rank, out_rows, tok_rows):
    micro, n_tp, rows, depth = out_rows.shape
    here = pl.BlockSpec((1, 1, rows, depth), lambda m, k, r: (m, k, 0, 0))
    there = pl.BlockSpec((1, 1, rows, depth), lambda m, k, r: (m, r[0] ^ k, 0, 0))
    return pl.pallas_call(
        spread_kernel,
        grid_spec=pltpu.PrefetchScalarGridSpec(
            num_scalar_prefetch=1,
            grid=(micro, n_tp),
            in_specs=[here, here],
            out_specs=[there, there],
        ),
        out_shape=[
            jax.ShapeDtypeStruct(out_rows.shape, BF16),
            jax.ShapeDtypeStruct(out_rows.shape, F32),
        ],
        compiler_params=pltpu.CompilerParams(vmem_limit_bytes=VMEM_LIMIT),
        name="spread",
    )(rank, out_rows, tok_rows)


def per_device(
    n_dp,
    n_tp,
    tokens,
    cotangent,
    span_order,
    w_query,
    w_keyval,
    w_output,
    w_gateup,
    w_down,
    norm_gains,
    mean_query,
    square_query,
    mean_keyval,
    square_keyval,
    mean_output,
    square_output,
    mean_gateup,
    square_gateup,
    mean_down,
    square_down,
    mean_gains,
    square_gains,
):
    depth = tokens.shape[1]
    span_rows = 2 * CH
    block_rows = SEQS * span_rows // n_tp
    parts = span_rows // min(span_rows, block_rows)
    q_width = w_query.shape[1]
    kv_width = w_keyval.shape[1]
    hidden_width = w_down.shape[0]
    own_depth = w_query.shape[0]
    group = q_width // HD // (kv_width // (2 * HD))
    device = lax.axis_index("dp")
    rank = lax.axis_index("tp")
    line = n_dp // 2
    place, core = device // 2, device % 2

    def swap(value, k):
        return lax.ppermute(value, "tp", [(i, i ^ k) for i in range(n_tp)])

    def reorder(value):
        return jnp.concatenate(
            [lax.dynamic_slice_in_dim(value, rank ^ k, 1, axis=1) for k in range(n_tp)], axis=1
        )

    def gather_blocks(own):
        half = own.shape[0] // 2
        got = [own, swap(own, 1), swap(own, 2)]
        got.append(jnp.concatenate([swap(got[1][:half], 2), swap(got[2][half:], 1)], axis=0))
        return got + [swap(own, k) for k in range(4, n_tp)]

    def exchange(blocks):
        return [blocks[0]] + [swap(blocks[k], k) for k in range(1, n_tp)]

    def total_of(parts):
        total = parts[0].astype(F32)
        for part in parts[1:]:
            total = total + part.astype(F32)
        return total

    def gather_pair(owns):
        got = [owns, [swap(own, 1) for own in owns], [swap(own, 2) for own in owns]]
        got.append([swap(got[1][0], 2)] + [swap(own, 1) for own in got[2][1:]])
        return got + [[swap(own, k) for own in owns] for k in range(4, n_tp)]

    def scatter_pair(blocks):
        first = swap(blocks[0][3], 1)
        seconds = [swap(blocks[m][3], 2) for m in range(1, MICRO)]
        to_two = total_of([blocks[0][2], first]).astype(BF16)
        to_one = [total_of([blocks[m][1], seconds[m - 1]]).astype(BF16) for m in range(1, MICRO)]
        yield [to_two] + to_one
        totals = []
        for m in range(MICRO):
            one = blocks[m][1] if m == 0 else to_one[m - 1]
            two = to_two if m == 0 else blocks[m][2]
            far = [swap(blocks[m][k], k) for k in range(4, n_tp)]
            totals.append(total_of([blocks[m][0], swap(one, 1), swap(two, 2)] + far))
        yield totals

    def line_sum(other, own):
        met = lax.ppermute(other, "dp", [(i, i ^ 1) for i in range(n_dp)])
        yield [met]

        def share(index):
            index = jnp.clip(index, 0, line - 1)
            return lax.dynamic_index_in_dim(own, index, 0, False).astype(
                F32
            ) + lax.dynamic_index_in_dim(met, index, 0, False).astype(F32)

        sends = []
        for far in range(1, line):
            for way in (far, -far):
                sends.append((way, share(place + way).astype(BF16)))
        yield [value for _, value in sends]
        total = share(place)
        for far in range(1, line):
            arrived = []
            for way, value in sends:
                if abs(way) == far:
                    pairs = [
                        (i, i + 2 * way) for i in range(n_dp) if 0 <= i + 2 * way < n_dp
                    ]
                    arrived.append(lax.ppermute(value, "dp", pairs))
            if far <= 3:
                yield arrived
            for value in arrived:
                total = total + value.astype(F32)
        yield [total]

    def my_half(value):
        return lax.dynamic_slice_in_dim(value, core * (depth // 2), depth // 2, axis=0)

    def swap_cores(value):
        return lax.ppermute(value, "dp", [(i, i ^ 1) for i in range(n_dp)])

    def both_halves(near, far):
        return jnp.where(
            core == 0,
            jnp.concatenate([near, far], axis=1),
            jnp.concatenate([far, near], axis=1),
        )

    def after(value, *earlier):
        return lax.optimization_barrier((value,) + earlier)[0]

    qkv_full = lax.all_gather(
        jnp.concatenate([w_query, w_keyval], axis=1), "dp", axis=0, tiled=True
    )
    gains_full = lax.all_gather(norm_gains, "dp", axis=1, tiled=True)
    out_t_full = lax.all_gather(w_output.T, "dp", axis=0, tiled=True)

    offsets = jnp.arange(CH, dtype=jnp.int32)
    all_pos = (span_order[:, None] * CH + offsets[None, :]).reshape(n_dp, parts, -1)
    all_pos = jnp.stack([all_pos[:, (rank % parts) ^ p] for p in range(parts)], axis=1)
    own_pos = lax.dynamic_slice_in_dim(all_pos, device, 1).reshape(-1)
    all_pos = all_pos.reshape(-1)
    qpos, kpos = own_pos[:, None], all_pos[None, :]
    kv_kinds = [True, False] * (kv_width // (2 * HD))
    cos_t, sin_t = lane_tables(own_pos, [True] * (q_width // HD) + kv_kinds)

    x = reorder(tokens.reshape(MICRO, n_tp, block_rows, depth))
    seed = reorder(cotangent.reshape(MICRO, n_tp, block_rows, depth))
    batch_rows = SEQS * span_rows
    rows = MICRO * batch_rows
    gain_one, gain_two = gains_full[0:1], gains_full[1:2]
    attn_in, qkv = project(x.reshape(rows, depth), gain_one, qkv_full, cos_t, sin_t)
    qkv = qkv.reshape(MICRO, SEQS, span_rows, q_width + kv_width)
    q, kv = qkv[..., :q_width], qkv[..., q_width:]
    kv_all = lax.all_gather(kv, "dp", axis=0, tiled=False)

    sub = min(SUB, hidden_width // CHUNKS)
    chunk = hidden_width // CHUNKS
    w_down_t = w_down.T
    mlp_full = []
    for c in range(CHUNKS):
        pieces = []
        for start in range(c * chunk, (c + 1) * chunk, sub):
            cols = slice(start, start + sub)
            pieces += [w_gateup[0][:, cols], w_gateup[1][:, cols], w_down_t[:, cols]]
        shard = jnp.concatenate(pieces, axis=1)
        mlp_full.append(lax.all_gather(shard, "dp", axis=0, tiled=True))

    attended = attend(qpos, kpos, q, kv_all, group)
    attended_blocks = attended.reshape(MICRO, n_tp, block_rows, q_width)
    out_near = my_half(out_t_full)
    out_near = jnp.concatenate([out_near] + [swap(out_near, k) for k in range(1, n_tp)], axis=1)
    out_far = swap_cores(out_near)
    heads_in = exchange([attended_blocks[:, k] for k in range(n_tp)])
    own_rows = MICRO * block_rows
    x_own = x[:, 0].reshape(own_rows, depth).astype(F32)
    heads_cat = jnp.concatenate([v.reshape(own_rows, q_width) for v in heads_in], axis=1)
    middle = x_own + both_halves(dot_nt(heads_cat, out_near), dot_nt(heads_cat, out_far))
    scale_two = mean_square_scale(middle)
    normed_two = middle * scale_two
    u_own = (normed_two * gain_two.astype(F32)).astype(BF16)
    batches = range(MICRO)
    gathered = [g.reshape(MICRO, block_rows, depth) for g in gather_blocks(u_own)]
    u = [jnp.concatenate([gathered[k][m] for k in range(n_tp)], axis=0) for m in batches]
    g = [seed[m].reshape(batch_rows, depth) for m in batches]

    qkv_half = after(my_half(qkv_full), u[0])
    quarter = depth // 4
    qkv_width = q_width + kv_width
    qkv_near = jnp.zeros((depth // 2, n_tp * qkv_width), BF16)
    qkv_near = lax.dynamic_update_slice(qkv_near, qkv_half, (0, 0))
    qkv_moves = [(k, i) for i in range(2) for k in range(1, min(n_tp, 3))]
    qkv_moves = [qkv_moves[:2], qkv_moves[2:]] + [
        [(k, i) for k in range(3, n_tp)] for i in range(2)
    ]

    def move_qkv(buffer):
        for k, i in qkv_moves.pop(0) if qkv_moves else []:
            got = swap(qkv_half[i * quarter : (i + 1) * quarter], k)
            buffer = lax.dynamic_update_slice(buffer, got, (i * quarter, k * qkv_width))
        return buffer

    def blocks_of(value):
        return [value[k * block_rows : (k + 1) * block_rows] for k in range(n_tp)]

    def own_part(value, m):
        return value[m * block_rows : (m + 1) * block_rows]

    core_index = core.astype(jnp.int32).reshape(1)
    gain_two_f = gain_two.astype(F32)
    gain_one_f = gain_one.astype(F32)
    cos_q, sin_q = cos_t[:, : group * HD], sin_t[:, : group * HD]
    cos_k, sin_k = cos_t[:, q_width:], sin_t[:, q_width:]
    gain_grads = [0.0, 0.0]
    sums = [None] * MICRO

    def expand(c, m, *earlier):
        hid, dgu, y_low, du_low = feed_forward(
            after(u[m], *earlier), g[m], mlp_full[c], sub, sums[m]
        )
        sums[m] = (y_low, du_low)
        return hid, dgu

    def close(hids, dgus, *earlier):
        (grads,) = outer_products(
            core_index, [after(u[0], *earlier)] + u[1:], g, hids, dgus, own_depth, sub, False
        )
        return grads, lax.psum_scatter(grads, "dp", scatter_dimension=0, tiled=False)

    chunk_grads = []
    earlier = []
    for c in range(CHUNKS - 1):
        hids, dgus = [], []
        for m in batches:
            hid, dgu = expand(c, m, *earlier)
            qkv_near = move_qkv(qkv_near)
            earlier = [hid, qkv_near]
            hids.append(hid)
            dgus.append(dgu)
        grads, owned = close(hids, dgus, *earlier)
        qkv_near = move_qkv(qkv_near)
        earlier = [grads, qkv_near]
        chunk_grads.append(owned)

    d_middles, d_mid_lows, d_attends, all_rows = [], [], [], []
    hids, dgus = [], []
    for m in batches:
        hid, dgu = expand(CHUNKS - 1, m, *earlier)
        qkv_near = move_qkv(qkv_near)
        earlier = [hid, qkv_near]
        if m == 0:
            qkv_far = swap_cores(qkv_near)
        hids.append(hid)
        dgus.append(dgu)
    grads, owned = close(hids, dgus, *earlier, qkv_far)
    chunk_grads.append(owned)
    tail_sums = [after(sums[0], grads)] + sums[1:]
    d_qkv, mid_rows, out_rows, tok_rows, gain_part = tail(
        n_dp,
        n_tp,
        group,
        tail_sums,
        seed[:, 0].reshape(own_rows, depth),
        middle,
        x[:, 0].reshape(own_rows, depth),
        gains_full,
        (out_near, out_far),
        (qkv_near, qkv_far),
        q,
        kv_all,
        qpos,
        kpos,
        cos_t,
        sin_t,
    )
    block_output, grad_tokens = spread(rank.astype(jnp.int32).reshape(1), out_rows, tok_rows)
    block_output = block_output.reshape(rows, depth)
    grad_tokens = grad_tokens.reshape(rows, depth)
    d_mid_rows = mid_rows.reshape(rows, depth)
    d_qkvs = [d_qkv.reshape(rows, q_width + kv_width)]
    gain_grads = [gain_part[0], gain_part[1]]

    out_grad_t = dot_tn(d_mid_rows, attended.reshape(rows, q_width)).astype(BF16)
    mlp_grads = [v.reshape(own_depth, -1) for v in chunk_grads]
    qkv_grad = dot_tn(attn_in, jnp.concatenate(d_qkvs, axis=0)).astype(BF16)
    gain_cols = jnp.stack(gain_grads, axis=1)
    gain_cols = jnp.pad(gain_cols, ((0, 0), (0, 126))).astype(BF16)
    attn_grads = lax.psum_scatter(
        after(jnp.concatenate([qkv_grad, out_grad_t, gain_cols], axis=1), *chunk_grads),
        "dp",
        scatter_dimension=0,
        tiled=True,
    )
    gain_part = attn_grads[:, 2 * q_width + kv_width :]
    gain_sum = gain_part.astype(F32)
    for k in range(1, n_tp):
        gain_sum = gain_sum + swap(gain_part, k).astype(F32)

    grad_query = attn_grads[:, :q_width].astype(F32)
    grad_keyval = attn_grads[:, q_width : q_width + kv_width].astype(F32)
    grad_output = attn_grads[:, q_width + kv_width : 2 * q_width + kv_width].astype(F32).T
    grad_gains = gain_sum[:, :2].T
    def with_update(gradient, old_mean, square, weight, decay):
        return (gradient,) + adam_update(gradient, old_mean, square, weight.astype(F32), decay)

    return (
        (block_output, grad_tokens)
        + with_update(grad_query, mean_query, square_query, w_query, weight_decay)
        + with_update(grad_keyval, mean_keyval, square_keyval, w_keyval, weight_decay)
        + with_update(grad_output, mean_output, square_output, w_output, weight_decay)
        + step_from_chunks(
            mlp_grads, mean_gateup, square_gateup, w_gateup, sub, 0, False, weight_decay
        )
        + step_from_chunks(mlp_grads, mean_down, square_down, w_down, sub, 2, True, weight_decay)
        + with_update(grad_gains, mean_gains, square_gains, norm_gains, 0.0)
    )


def solution(mesh):
    rows_first = P("dp", "tp")
    cols_last = P("tp", "dp")
    stacked = P(None, "dp", "tp")
    gains = P(None, "dp")
    token_rows = P("dp", None)
    placed = (
        (token_rows, token_rows, P())
        + (rows_first, rows_first, cols_last, stacked, cols_last, gains)
        + (rows_first,) * 4
        + (cols_last,) * 2
        + (stacked,) * 2
        + (cols_last,) * 2
        + (gains,) * 2
    )
    results = (
        (token_rows, token_rows)
        + (rows_first,) * 8
        + (cols_last,) * 4
        + (stacked,) * 4
        + (cols_last,) * 4
        + (gains,) * 4
    )
    return jax.shard_map(
        functools.partial(per_device, mesh.shape["dp"], mesh.shape["tp"]),
        mesh=mesh,
        in_specs=placed,
        out_specs=results,
        check_vma=False,
    )
```

```python
import functools

import jax
import jax.numpy as jnp
from jax import lax
from jax.experimental import pallas as pl
from jax.experimental.pallas import tpu as pltpu
from jax.sharding import PartitionSpec as P

HD = 64
CH = 64
SEQS = 4
MICRO = 2
STEP = 5
CHUNKS = 2
SUB = 512

norm_eps = 1e-05
rope_base = 500000.0
beta_one = 0.9
beta_two = 0.95
learn_rate = 0.01
weight_decay = 0.1
adam_eps = 1e-08
masked_score = -1e30

F32 = jnp.float32
BF16 = jnp.bfloat16
VMEM_LIMIT = 60 * 1024 * 1024
HINT = 20


def hint(flops, bytes_accessed, transcendentals):
    return pl.CostEstimate(
        flops=flops // HINT, bytes_accessed=bytes_accessed // HINT, transcendentals=transcendentals
    )


def lane_tables(positions, kinds):
    half_size = HD // 2
    frequencies = rope_base ** (-(jnp.arange(half_size, dtype=F32) * 2.0 / HD))
    angles = positions.astype(F32)[:, None] * frequencies[None, :]
    cos_half, sin_half = jnp.cos(angles), jnp.sin(angles)
    cos_head = jnp.concatenate([cos_half, cos_half], axis=-1)
    sin_head = jnp.concatenate([-sin_half, sin_half], axis=-1)
    ones, zeros = jnp.ones_like(cos_head), jnp.zeros_like(cos_head)
    cos_all, sin_all = [], []
    for kind in kinds:
        cos_all.append(cos_head if kind else ones)
        sin_all.append(sin_head if kind else zeros)
    return jnp.concatenate(cos_all, axis=-1), jnp.concatenate(sin_all, axis=-1)


def half_turn(values):
    width = values.shape[-1]
    axis = values.ndim - 1
    lane = lax.broadcasted_iota(jnp.int32, values.shape, axis)
    ahead = pltpu.roll(values, width - HD // 2, axis)
    behind = pltpu.roll(values, HD // 2, axis)
    return jnp.where(lane % HD < HD // 2, ahead, behind)


def mean_square_scale(values):
    return lax.rsqrt(jnp.mean(values * values, axis=-1, keepdims=True) + norm_eps)


def project_kernel(x_ref, gain_ref, w_ref, cos_ref, sin_ref, a_ref, qkv_ref):
    x = x_ref[...].astype(F32)
    a = (x * mean_square_scale(x) * gain_ref[...].astype(F32)).astype(BF16)
    a_ref[...] = a
    t = jnp.dot(a, w_ref[...], preferred_element_type=F32)
    qkv_ref[...] = (t * cos_ref[...] + half_turn(t) * sin_ref[...]).astype(BF16)


def project(x, gain, weight, cos_t, sin_t):
    rows, depth = x.shape
    width = weight.shape[1]
    block = cos_t.shape[0]
    return pl.pallas_call(
        project_kernel,
        grid=(rows // block,),
        in_specs=[
            pl.BlockSpec((block, depth), lambda i: (i, 0)),
            pl.BlockSpec((1, depth), lambda i: (0, 0)),
            pl.BlockSpec((depth, width), lambda i: (0, 0)),
            pl.BlockSpec((block, width), lambda i: (0, 0)),
            pl.BlockSpec((block, width), lambda i: (0, 0)),
        ],
        out_specs=[
            pl.BlockSpec((block, depth), lambda i: (i, 0)),
            pl.BlockSpec((block, width), lambda i: (i, 0)),
        ],
        out_shape=[
            jax.ShapeDtypeStruct((rows, depth), BF16),
            jax.ShapeDtypeStruct((rows, width), BF16),
        ],
        compiler_params=pltpu.CompilerParams(vmem_limit_bytes=VMEM_LIMIT),
        cost_estimate=hint(
            flops=2 * rows * depth * width, bytes_accessed=4 * rows * depth, transcendentals=0
        ),
        name="project",
    )(x, gain, weight, cos_t, sin_t)


def stack_heads(block, group, upper):
    lane = lax.broadcasted_iota(jnp.int32, (block.shape[0], 2 * HD), 1)
    keep = (lane >= HD) if upper else (lane < HD)
    parts = []
    for head in range(group):
        pair = block[:, (head // 2) * 2 * HD : (head // 2 + 1) * 2 * HD].astype(F32)
        if (head % 2 == 1) != upper:
            pair = pltpu.roll(pair, HD, 1)
        parts.append(jnp.where(keep, pair, 0.0).astype(BF16))
    return jnp.concatenate(parts, axis=0)


def unstack_heads(stacked, group, upper):
    rows = stacked.shape[0] // group
    lane = lax.broadcasted_iota(jnp.int32, (rows, 2 * HD), 1)
    pairs = []
    for pair in range(group // 2):
        even = stacked[(2 * pair) * rows : (2 * pair + 1) * rows]
        odd = stacked[(2 * pair + 1) * rows : (2 * pair + 2) * rows]
        if upper:
            even = pltpu.roll(even, HD, 1)
        else:
            odd = pltpu.roll(odd, HD, 1)
        pairs.append(jnp.where(lane < HD, even, odd))
    return jnp.concatenate(pairs, axis=1)


def scores_and_probs(q_pad, keys, qpos, kpos, group):
    scores = (
        lax.dot_general(q_pad, keys, (((1,), (1,)), ((), ())), preferred_element_type=F32)
        * HD ** (-0.5)
    )
    rows = qpos.shape[0]
    blocked = kpos > qpos
    masked = [
        jnp.where(blocked, masked_score, scores[h * rows : (h + 1) * rows]) for h in range(group)
    ]
    scores = jnp.concatenate(masked, axis=0)
    exponent = jnp.exp(scores - jnp.max(scores, axis=-1, keepdims=True))
    return exponent * (1.0 / jnp.sum(exponent, axis=-1, keepdims=True))


def attend_kernel(group, qpos_ref, kpos_ref, q_ref, kv_ref, o_ref):
    keyvals = kv_ref[...].reshape(-1, 2 * HD)
    q_pad = stack_heads(q_ref[...].reshape(-1, group * HD), group, False)
    probs = scores_and_probs(q_pad, keyvals, qpos_ref[...], kpos_ref[...], group)
    out = jnp.dot(probs.astype(BF16), keyvals, preferred_element_type=F32)
    o_ref[...] = unstack_heads(out, group, True).astype(BF16).reshape(o_ref.shape)


def attend_back_kernel(
    group, qpos_ref, kpos_ref, cos_ref, sin_ref, q_ref, do_ref, kv_ref, dq_ref, dkv_ref
):
    keyvals = kv_ref[...].reshape(-1, 2 * HD)
    q_pad = stack_heads(q_ref[...].reshape(-1, group * HD), group, False)
    do_pad = stack_heads(do_ref[...].reshape(-1, group * HD), group, True)
    probs = scores_and_probs(q_pad, keyvals, qpos_ref[...], kpos_ref[...], group)
    d_probs = lax.dot_general(
        do_pad, keyvals, (((1,), (1,)), ((), ())), preferred_element_type=F32
    )
    d_scores = probs * (d_probs - jnp.sum(d_probs * probs, axis=-1, keepdims=True))
    ds_low = d_scores.astype(BF16) * HD ** (-0.5)
    dq = jnp.dot(ds_low, keyvals, preferred_element_type=F32)
    dq = unstack_heads(dq, group, False)
    dq = dq * cos_ref[...] + half_turn(dq * sin_ref[...])
    dq_ref[...] = dq.astype(BF16).reshape(dq_ref.shape)
    contract = (((0,), (0,)), ((), ()))
    d_keyvals = lax.dot_general(
        ds_low, q_pad, contract, preferred_element_type=F32
    ) + lax.dot_general(probs.astype(BF16), do_pad, contract, preferred_element_type=F32)
    dkv_ref[...] = d_keyvals.astype(BF16).reshape(dkv_ref.shape)


def attention_specs(qkv_heads, n_dp, span_rows, group):
    q_spec = pl.BlockSpec((1, 1, span_rows, group * HD), lambda m, s, h: (m, s, 0, h))
    kv_spec = pl.BlockSpec(
        (n_dp, 1, 1, span_rows, 2 * HD), lambda m, s, h: (0, m, s, 0, h)
    )
    pos_q = pl.BlockSpec((span_rows, 1), lambda m, s, h: (0, 0))
    pos_k = pl.BlockSpec((1, n_dp * span_rows), lambda m, s, h: (0, 0))
    return q_spec, kv_spec, pos_q, pos_k


def attend(qpos, kpos, q, kv, group):
    micro, seqs, span_rows, width = q.shape
    n_dp, heads = kv.shape[0], width // (group * HD)
    q_spec, kv_spec, pos_q, pos_k = attention_specs(heads, n_dp, span_rows, group)
    return pl.pallas_call(
        functools.partial(attend_kernel, group),
        grid=(micro, seqs, heads),
        in_specs=[pos_q, pos_k, q_spec, kv_spec],
        out_specs=q_spec,
        out_shape=jax.ShapeDtypeStruct(q.shape, BF16),
        compiler_params=pltpu.CompilerParams(vmem_limit_bytes=VMEM_LIMIT),
        cost_estimate=hint(
            flops=16 * micro * seqs * span_rows * width * n_dp * span_rows,
            bytes_accessed=4 * q.size + 2 * kv.size,
            transcendentals=0,
        ),
        name="attend",
    )(qpos, kpos, q, kv)


def attend_back(qpos, kpos, cos_q, sin_q, q, d_out, kv, group):
    micro, seqs, span_rows, width = q.shape
    n_dp, heads = kv.shape[0], width // (group * HD)
    q_spec, kv_spec, pos_q, pos_k = attention_specs(heads, n_dp, span_rows, group)
    table = pl.BlockSpec((span_rows, group * HD), lambda m, s, h: (0, 0))
    return pl.pallas_call(
        functools.partial(attend_back_kernel, group),
        grid=(micro, seqs, heads),
        in_specs=[pos_q, pos_k, table, table, q_spec, q_spec, kv_spec],
        out_specs=[q_spec, kv_spec],
        out_shape=[
            jax.ShapeDtypeStruct(q.shape, BF16),
            jax.ShapeDtypeStruct(kv.shape, BF16),
        ],
        compiler_params=pltpu.CompilerParams(vmem_limit_bytes=VMEM_LIMIT),
        cost_estimate=hint(
            flops=40 * micro * seqs * span_rows * width * n_dp * span_rows,
            bytes_accessed=6 * q.size + 4 * kv.size,
            transcendentals=0,
        ),
        name="attend_back",
    )(qpos, kpos, cos_q, sin_q, q, d_out, kv)


def norm_back(d_normed, normed, scale):
    return scale * (d_normed - normed * jnp.mean(d_normed * normed, axis=-1, keepdims=True))


def adam_update(gradient, old_mean, square, weight, decay_factor):
    moment = beta_one * old_mean + (1.0 - beta_one) * gradient
    spread = beta_two * square + (1.0 - beta_two) * gradient * gradient
    change = -learn_rate * (
        moment / (1.0 - beta_one**STEP) / (jnp.sqrt(spread / (1.0 - beta_two**STEP)) + adam_eps)
        + decay_factor * weight
    )
    return (moment, spread, change)


def dot(left, right):
    return jnp.dot(left, right, preferred_element_type=F32)


def dot_nt(left, right):
    return lax.dot_general(left, right, (((1,), (1,)), ((), ())), preferred_element_type=F32)


def dot_tn(left, right):
    return lax.dot_general(left, right, (((0,), (0,)), ((), ())), preferred_element_type=F32)


def paired(index, k):
    bit = 1
    while bit <= k:
        if k & bit:
            index = index + bit - 2 * bit * ((index // bit) % 2)
        bit *= 2
    return index


def remote(src, dst, send, recv, device):
    return pltpu.make_async_remote_copy(
        src_ref=src,
        dst_ref=dst,
        send_sem=send,
        recv_sem=recv,
        device_id=device,
        device_id_type=pl.DeviceIdType.MESH,
    )


def meet(peers):
    barrier = pltpu.get_barrier_semaphore()
    for peer in peers:
        pl.semaphore_signal(barrier, inc=1, device_id=peer, device_id_type=pl.DeviceIdType.MESH)
    pl.semaphore_wait(barrier, len(peers))


def start(moves):
    for move in moves:
        move.start()


def arrive(moves):
    for move in moves:
        move.wait_recv()


def sent(moves):
    for move in moves:
        move.wait_send()


def row_moves(remote, rank, n_tp, low, got, send, recv):
    first = [
        [
            remote(low.at[m], got.at[m, k], send.at[m, k], recv.at[m, k], rank(k))
            for k in range(1, n_tp)
            if k != 3
        ]
        for m in range(MICRO)
    ]
    relay = [
        remote(got.at[m, 1 + m], got.at[m, 3], send.at[m, 3], recv.at[m, 3], rank(2 - m))
        for m in range(MICRO)
    ]
    return first, relay


def relay_rows(first, relay):
    for m in range(MICRO):
        first[m][m].wait_recv()
        relay[m].start()


def close_rows(first, relay):
    for m in range(MICRO):
        for i, move in enumerate(first[m]):
            if i != m:
                move.wait_recv()
            move.wait_send()
        relay[m].wait_recv()
        relay[m].wait_send()


def carried(n_tp, src, got, send, recv):
    dp, tp = lax.axis_index("dp"), lax.axis_index("tp")
    rows = got.shape[1]
    return [
        remote(
            src.at[pl.ds(k * rows, rows)],
            got.at[k],
            send.at[k],
            recv.at[k],
            (dp, paired(tp, k)),
        )
        for k in range(1, n_tp)
    ]


def carry_start(n_tp, *move):
    dp, tp = lax.axis_index("dp"), lax.axis_index("tp")
    meet([(dp, paired(tp, k)) for k in range(1, n_tp)])
    start(carried(n_tp, *move))


def carry_end(n_tp, *move):
    moves = carried(n_tp, *move)
    arrive(moves)
    sent(moves)


def gated_kernel(n_tp, last, steps, u_ref, g_ref, w_ref, *refs):
    refs = list(refs)
    move = None
    if n_tp:
        send, recv = refs[-2:]
        src, got = refs.pop(2), refs[6]
        move = (src, got, send, recv)
        refs = refs[:6] + refs[7:-2]
    if last:
        y_old, du_old = refs[:2]
        refs = refs[2:]
    hid_ref, dgu_ref, y_out, du_out, y_sum, du_sum, y_low, du_low, sem = refs
    step = pl.program_id(0)
    depth = w_ref.shape[0]
    sub = hid_ref.shape[1]
    cols = min(512, depth)

    @pl.when(step == 0)
    def _():
        if move:
            carry_start(n_tp, *move)
        y_sum[...] = jnp.zeros_like(y_sum)
        du_sum[...] = jnp.zeros_like(du_sum)
        if last:
            pltpu.make_async_copy(y_old, y_low, sem.at[0]).start()
            pltpu.make_async_copy(du_old, du_low, sem.at[1]).start()

    gate_proj = dot(u_ref[...], w_ref[:, :sub])
    up_proj = dot(u_ref[...], w_ref[:, sub : 2 * sub])
    sigmoid_gate = jax.nn.sigmoid(gate_proj)
    silu_gate = gate_proj * sigmoid_gate
    hid_ref[...] = (silu_gate * up_proj).astype(BF16)
    d_hidden = dot(g_ref[...], w_ref[:, 2 * sub :])
    d_gate = d_hidden * up_proj * sigmoid_gate * (1.0 + gate_proj * (1.0 - sigmoid_gate))
    dgu_ref[:, :sub] = d_gate.astype(BF16)
    dgu_ref[:, sub:] = (d_hidden * silu_gate).astype(BF16)
    for start in range(0, depth, cols):
        part = slice(start, start + cols)
        du_sum[:, part] += dot_nt(dgu_ref[...], w_ref[part, : 2 * sub])
        y_sum[:, part] += dot_nt(hid_ref[...], w_ref[part, 2 * sub :])

    @pl.when(step == steps - 1)
    def _():
        copy_y = pltpu.make_async_copy(y_low, y_out, sem.at[0])
        copy_du = pltpu.make_async_copy(du_low, du_out, sem.at[1])
        if last:
            pltpu.make_async_copy(y_old, y_low, sem.at[0]).wait()
            pltpu.make_async_copy(du_old, du_low, sem.at[1]).wait()
            du_low[...] = (du_sum[...] + du_low[...].astype(F32)).astype(BF16)
            copy_du.start()
            y_low[...] = (y_sum[...] + y_low[...].astype(F32)).astype(BF16)
        else:
            du_low[...] = du_sum[...].astype(BF16)
            copy_du.start()
            y_low[...] = y_sum[...].astype(BF16)
        copy_y.start()
        copy_du.wait()
        copy_y.wait()
        if move:
            carry_end(n_tp, *move)


def carrier_params(n_tp, collective_id):
    if not n_tp:
        return pltpu.CompilerParams(vmem_limit_bytes=VMEM_LIMIT)
    return pltpu.CompilerParams(
        collective_id=collective_id, has_side_effects=True, vmem_limit_bytes=VMEM_LIMIT
    )


def feed_forward(u, g, weights, sub, sums, n_tp=0, carry=None):
    rows, depth = u.shape
    steps = weights.shape[1] // (3 * sub)
    last = sums is not None
    whole = functools.partial(pl.BlockSpec, pipeline_mode=pl.Buffered(1))
    anywhere = pl.BlockSpec(memory_space=pl.ANY)
    return pl.pallas_call(
        functools.partial(gated_kernel, n_tp, last, steps),
        grid=(steps,),
        in_specs=[
            whole((rows, depth), lambda j: (0, 0)),
            whole((rows, depth), lambda j: (0, 0)),
            pl.BlockSpec((depth, 3 * sub), lambda j: (0, j)),
        ]
        + ([anywhere, anywhere] if last else [])
        + ([anywhere] if n_tp else []),
        out_specs=[
            pl.BlockSpec((rows, sub), lambda j: (0, j)),
            pl.BlockSpec((rows, 2 * sub), lambda j: (0, j)),
            anywhere,
            anywhere,
        ]
        + ([anywhere] if n_tp else []),
        out_shape=[
            jax.ShapeDtypeStruct((rows, steps * sub), BF16),
            jax.ShapeDtypeStruct((rows, 2 * steps * sub), BF16),
            jax.ShapeDtypeStruct((rows, depth), BF16),
            jax.ShapeDtypeStruct((rows, depth), BF16),
        ]
        + ([jax.ShapeDtypeStruct((n_tp, rows // n_tp, depth), BF16)] if n_tp else []),
        scratch_shapes=[
            pltpu.VMEM((rows, depth), F32),
            pltpu.VMEM((rows, depth), F32),
            pltpu.VMEM((rows, depth), BF16),
            pltpu.VMEM((rows, depth), BF16),
            pltpu.SemaphoreType.DMA((2,)),
        ]
        + ([pltpu.SemaphoreType.DMA((n_tp,))] * 2 if n_tp else []),
        compiler_params=carrier_params(n_tp, 3),
        cost_estimate=hint(
            flops=12 * rows * depth * steps * sub,
            bytes_accessed=2 * weights.size + 8 * rows * depth,
            transcendentals=0,
        ),
        name="feed_forward",
    )(u, g, weights, *(sums if last else ()), *([carry] if n_tp else []))


def outer_kernel(n_tp, batches, sub, steps, *refs):
    u_refs, g_refs = refs[:batches], refs[batches : 2 * batches]
    hid_refs, dgu_refs = refs[2 * batches : 3 * batches], refs[3 * batches : 4 * batches]
    refs = refs[4 * batches :]
    move = None
    if n_tp:
        src, out_ref, got, send, recv = refs
        move = (src, got, send, recv)

        @pl.when(pl.program_id(0) == 0)
        def _():
            carry_start(n_tp, *move)

    else:
        (out_ref,) = refs
    for j in range(steps):
        both = slice(2 * j * sub, 2 * (j + 1) * sub)
        one = slice(j * sub, (j + 1) * sub)
        total = dot_tn(u_refs[0][...], dgu_refs[0][:, both])
        for m in range(1, batches):
            total += dot_tn(u_refs[m][...], dgu_refs[m][:, both])
        out_ref[0, :, 3 * j * sub : 3 * j * sub + 2 * sub] = total.astype(BF16)
        total = dot_tn(g_refs[0][...], hid_refs[0][:, one])
        for m in range(1, batches):
            total += dot_tn(g_refs[m][...], hid_refs[m][:, one])
        out_ref[0, :, 3 * j * sub + 2 * sub : 3 * (j + 1) * sub] = total.astype(BF16)
    if n_tp:

        @pl.when(pl.program_id(0) == pl.num_programs(0) - 1)
        def _():
            carry_end(n_tp, *move)


def outer_products(us, gs, hids, dgus, own, sub, n_tp=0, carry=None):
    batches = len(us)
    rows, depth = us[0].shape
    n_dp = depth // own
    width = hids[0].shape[1]
    steps = width // sub
    whole = functools.partial(pl.BlockSpec, pipeline_mode=pl.Buffered(1))
    column = pl.BlockSpec((rows, own), lambda i: (0, i))
    anywhere = pl.BlockSpec(memory_space=pl.ANY)
    return pl.pallas_call(
        functools.partial(outer_kernel, n_tp, batches, sub, steps),
        grid=(n_dp,),
        in_specs=[column] * (2 * batches)
        + [whole((rows, width), lambda i: (0, 0))] * batches
        + [whole((rows, 2 * width), lambda i: (0, 0))] * batches
        + ([anywhere] if n_tp else []),
        out_specs=[pl.BlockSpec((1, own, 3 * width), lambda i: (i, 0, 0))]
        + ([anywhere] if n_tp else []),
        out_shape=[jax.ShapeDtypeStruct((n_dp, own, 3 * width), BF16)]
        + ([jax.ShapeDtypeStruct((n_tp, rows // n_tp, depth), BF16)] if n_tp else []),
        scratch_shapes=[pltpu.SemaphoreType.DMA((n_tp,))] * 2 if n_tp else [],
        compiler_params=carrier_params(n_tp, 4),
        cost_estimate=hint(
            flops=6 * rows * batches * depth * width,
            bytes_accessed=6 * depth * width,
            transcendentals=0,
        ),
        name="outer_products",
    )(*us, *gs, *hids, *dgus, *([carry] if n_tp else []))


def attn_grad_kernel(a_ref, m_ref, qkv_ref, att_ref, gain_ref, out_ref):
    width = qkv_ref.shape[1]
    both = width + att_ref.shape[1]
    out_ref[0, :, :width] = dot_tn(a_ref[...], qkv_ref[...]).astype(BF16)
    out_ref[0, :, width:both] = dot_tn(m_ref[...], att_ref[...]).astype(BF16)
    gains = gain_ref[...]
    filler = jnp.zeros((out_ref.shape[2] - both - gains.shape[0], gains.shape[1]), F32)
    out_ref[0, :, both:] = jnp.concatenate([gains, filler], axis=0).T.astype(BF16)


def attn_weight_grads(attn_in, d_mid, d_qkv, attended, gain_grads, own):
    rows, depth = attn_in.shape
    width, q_width = d_qkv.shape[1], attended.shape[1]
    total = width + q_width + 128
    column = pl.BlockSpec((rows, own), lambda i: (0, i))
    whole = functools.partial(pl.BlockSpec, pipeline_mode=pl.Buffered(1))
    return pl.pallas_call(
        attn_grad_kernel,
        grid=(depth // own,),
        in_specs=[
            column,
            column,
            whole((rows, width), lambda i: (0, 0)),
            whole((rows, q_width), lambda i: (0, 0)),
            pl.BlockSpec((2, own), lambda i: (0, i)),
        ],
        out_specs=pl.BlockSpec((1, own, total), lambda i: (i, 0, 0)),
        out_shape=jax.ShapeDtypeStruct((depth // own, own, total), BF16),
        compiler_params=pltpu.CompilerParams(vmem_limit_bytes=VMEM_LIMIT),
        cost_estimate=hint(
            flops=2 * rows * depth * total, bytes_accessed=4 * rows * depth, transcendentals=0
        ),
        name="attn_weight_grads",
    )(attn_in, d_mid, d_qkv, attended, gain_grads)


def step_kernel(turned, decay, steps, chunks, *refs):
    grads = refs[:chunks]
    mean_ref, square_ref, weight_ref, grad_ref, moment_ref, spread_ref, update_ref = refs[chunks:]
    place = pl.program_id(1)
    for c in range(chunks):

        @pl.when(place // steps == c)
        def _(c=c):
            gradient = grads[c][...].astype(F32)
            if turned:
                gradient = gradient.T
            gradient = gradient.reshape(grad_ref.shape)
            moment, spread, change = adam_update(
                gradient, mean_ref[...], square_ref[...], weight_ref[...].astype(F32), decay
            )
            grad_ref[...] = gradient
            moment_ref[...] = moment
            spread_ref[...] = spread
            update_ref[...] = change


def step_from_chunks(grads, old_mean, square, weight, sub, offset, turned, decay):
    chunks, own = len(grads), grads[0].shape[0]
    steps = grads[0].shape[1] // (3 * sub)

    def grad_spec(c):
        def index(i, p):
            j = jnp.clip(p - c * steps, 0, steps - 1)
            return (0, 3 * j + i + offset)

        return pl.BlockSpec((own, sub), index)

    if turned:
        lead, spec = 1, pl.BlockSpec((sub, own), lambda i, p: (p, 0))
    else:
        lead, spec = old_mean.shape[0], pl.BlockSpec((1, own, sub), lambda i, p: (i, 0, p))
    return tuple(
        pl.pallas_call(
            functools.partial(step_kernel, turned, decay, steps, chunks),
            grid=(lead, chunks * steps),
            in_specs=[grad_spec(c) for c in range(chunks)] + [spec] * 3,
            out_specs=[spec] * 4,
            out_shape=[jax.ShapeDtypeStruct(old_mean.shape, F32)] * 4,
            compiler_params=pltpu.CompilerParams(vmem_limit_bytes=VMEM_LIMIT),
            cost_estimate=hint(
                flops=20 * old_mean.size, bytes_accessed=28 * old_mean.size, transcendentals=0
            ),
            name="weight_step",
        )(*grads, old_mean, square, weight)
    )


def rows_kernel(n_tp, *refs):
    count = (len(refs) - 1) // 4
    lows, gots, sems = refs[:count], refs[count : 2 * count], refs[2 * count : -1]
    local_sem = refs[-1]
    dp, tp = lax.axis_index("dp"), lax.axis_index("tp")

    def rank(k):
        return (dp, paired(tp, k))

    meet([rank(k) for k in range(1, n_tp)])
    plans = [
        row_moves(remote, rank, n_tp, lows[i], gots[i], sems[2 * i], sems[2 * i + 1])
        for i in range(count)
    ]
    keep = [
        pltpu.make_async_copy(lows[i].at[m], gots[i].at[m, 0], local_sem.at[i, m])
        for i in range(count)
        for m in range(MICRO)
    ]
    for first, _ in plans:
        for moves in first:
            start(moves)
    start(keep)
    for first, relay in plans:
        relay_rows(first, relay)
    for first, relay in plans:
        close_rows(first, relay)
    for copy in keep:
        copy.wait()


def gather_rows(n_tp, lows):
    micro, rows, depth = lows[0].shape
    count = len(lows)
    anywhere = pl.BlockSpec(memory_space=pl.ANY)
    return pl.pallas_call(
        functools.partial(rows_kernel, n_tp),
        in_specs=[anywhere] * count,
        out_specs=[anywhere] * count,
        out_shape=[jax.ShapeDtypeStruct((micro, n_tp, rows, depth), BF16)] * count,
        scratch_shapes=[pltpu.SemaphoreType.DMA((micro, n_tp))] * (2 * count)
        + [pltpu.SemaphoreType.DMA((count, micro))],
        compiler_params=pltpu.CompilerParams(
            collective_id=1, has_side_effects=True, vmem_limit_bytes=VMEM_LIMIT
        ),
        cost_estimate=hint(flops=10**10, bytes_accessed=10**8, transcendentals=0),
        name="gather_rows",
    )(*lows)


def tail_kernel(n_dp, n_tp, group, *refs):
    (
        du_refs,
        y_refs,
        du_ins,
        seed_ref,
        middle_ref,
        x_ref,
        gains_ref,
        out_refs,
        qkv_refs,
        q_ref,
        kv_ref,
        qpos_ref,
        kpos_ref,
        cos_ref,
        sin_ref,
        d_qkv_ref,
        mid_rows,
        out_rows,
        tok_low,
        gain_ref,
    ) = (refs[0:2], refs[2:4], refs[4:6]) + refs[6:10] + (refs[10:12], refs[12:14]) + refs[14:25]
    (
        weights,
        du_got,
        y_got,
        own_mid,
        mid_low,
        block_low,
        do_send,
        do_got,
        shares,
        met,
        z_send,
        z_got,
        heads_got,
        local_sem,
        block_s,
        block_r,
        y_s,
        y_r,
        mid_s,
        mid_r,
        do_s,
        do_r,
        core_s,
        core_r,
        z_s,
        z_r,
        heads_s,
        heads_r,
    ) = refs[25:]
    line = n_dp // 2
    batches = range(MICRO)
    others = range(1, n_tp)
    dp, tp = lax.axis_index("dp"), lax.axis_index("tp")
    place, core = dp // 2, dp % 2
    depth = middle_ref.shape[1]
    rows = mid_low.shape[1]
    seq_rows = q_ref.shape[2]
    q_width = q_ref.shape[3]
    kv_width = kv_ref.shape[4]
    width = q_width + kv_width
    half = depth // 2

    def rank(k):
        return (dp, paired(tp, k))

    def spot(k):
        return (paired(place, k) * 2 + core, tp)

    other_core = (place * 2 + 1 - core, tp)

    def block(k):
        return pl.ds(k * rows, rows)

    y_moves = [
        [
            remote(y_refs[m].at[block(k)], y_got.at[m, k], y_s.at[m, k], y_r.at[m, k], rank(k))
            for k in others
        ]
        for m in batches
    ]

    block_first, block_relay = row_moves(
        remote, rank, n_tp, block_low, out_rows, block_s, block_r
    )
    mid_first, mid_relay = row_moves(remote, rank, n_tp, mid_low, mid_rows, mid_s, mid_r)
    do_moves = [
        [
            remote(
                do_send.at[m, k], do_got.at[m, block(k)], do_s.at[m, k], do_r.at[m, k], rank(k)
            )
            for k in others
        ]
        for m in batches
    ]
    core_moves = [
        remote(shares.at[m, 1 - core], met.at[m], core_s.at[m], core_r.at[m], other_core)
        for m in batches
    ]
    z_moves = [
        [
            remote(z_send.at[m, k], z_got.at[m, k], z_s.at[m, k], z_r.at[m, k], spot(k))
            for k in range(1, line)
        ]
        for m in batches
    ]
    heads_moves = [
        [
            remote(
                d_qkv_ref.at[m, block(k)],
                heads_got.at[m, k],
                heads_s.at[m, k],
                heads_r.at[m, k],
                rank(k),
            )
            for k in others
        ]
        for m in batches
    ]

    own_copies = [
        pltpu.make_async_copy(ref.at[pl.ds(0, rows)], got.at[m, 0], local_sem.at[i, m])
        for i, (pair, got) in enumerate(((du_refs, du_got), (y_refs, y_got)))
        for m, ref in enumerate(pair)
    ]
    own_copies += [
        pltpu.make_async_copy(
            ref.at[pl.ds(1, n_tp - 1)], du_got.at[m, pl.ds(1, n_tp - 1)], local_sem.at[4, m]
        )
        for m, ref in enumerate(du_ins)
    ]
    keep_block = [
        pltpu.make_async_copy(block_low.at[m], out_rows.at[m, 0], local_sem.at[5, m])
        for m in batches
    ]
    load_out = [
        pltpu.make_async_copy(
            ref, weights.at[side, :, pl.ds(0, n_tp * q_width)], local_sem.at[6, side]
        )
        for side, ref in enumerate(out_refs)
    ]
    load_qkv = [
        pltpu.make_async_copy(ref, weights.at[side], local_sem.at[2, side])
        for side, ref in enumerate(qkv_refs)
    ]
    keep = [
        pltpu.make_async_copy(mid_low.at[m], mid_rows.at[m, 0], local_sem.at[3, m])
        for m in batches
    ]

    meet([rank(k) for k in others] + [other_core] + [spot(k) for k in range(1, line)])
    start(own_copies)
    start(load_out)
    gain_one = gains_ref[0:1, :].astype(F32)
    gain_two = gains_ref[1:2, :].astype(F32)
    gain_ref[...] = jnp.zeros_like(gain_ref)

    def total_of(got, m):
        total = got[m, 0].astype(F32)
        for k in others:
            total = total + got[m, k].astype(F32)
        return total

    for copy in own_copies:
        copy.wait()
    for m in batches:
        part = slice(m * rows, (m + 1) * rows)
        d_mixed = total_of(du_got, m)
        middle = middle_ref[part, :]
        scale = mean_square_scale(middle)
        normed = middle * scale
        gain_ref[1:2, :] += jnp.sum(d_mixed * normed, axis=0, keepdims=True)
        d_middle = seed_ref[part, :].astype(F32) + norm_back(d_mixed * gain_two, normed, scale)
        own_mid[m] = d_middle
        mid_low[m] = d_middle.astype(BF16)
        if m == 0:
            for copy in load_out:
                copy.wait()
        near_cols = pl.ds(pl.multiple_of(core * half, half), half)
        far_cols = pl.ds(pl.multiple_of((1 - core) * half, half), half)
        near, far = mid_low[m, :, near_cols], mid_low[m, :, far_cols]
        for k in range(n_tp):
            lanes = slice(k * q_width, (k + 1) * q_width)
            rows_out = (dot(near, weights[0, :, lanes]) + dot(far, weights[1, :, lanes])).astype(
                BF16
            )
            if k == 0:
                do_got[m, 0:rows, :] = rows_out
            else:
                do_send[m, k] = rows_out
        start(do_moves[m])
    start(load_qkv)
    for m in batches:
        start(mid_first[m])
        keep[m].start()
    for m in batches:
        start(y_moves[m])

    def attend_back_seq(m, s):
        seq = pl.ds(s * seq_rows, seq_rows)
        for h in range(kv_width // (2 * HD)):
            pair = slice(h * 2 * HD, (h + 1) * 2 * HD)
            keyvals = kv_ref[:, m, s, :, pair].reshape(-1, 2 * HD)
            grads = None
            for part in range(group // 2):
                lanes = slice((h * group + 2 * part) * HD, (h * group + 2 * part + 2) * HD)
                q_pad = stack_heads(q_ref[m, s, :, lanes], 2, False)
                do_pad = stack_heads(do_got[m, seq, lanes], 2, True)
                probs = scores_and_probs(q_pad, keyvals, qpos_ref[...], kpos_ref[...], 2)
                d_probs = dot_nt(do_pad, keyvals)
                d_scores = probs * (d_probs - jnp.sum(d_probs * probs, axis=-1, keepdims=True))
                ds_low = d_scores.astype(BF16) * HD ** (-0.5)
                dq = unstack_heads(dot(ds_low, keyvals), 2, False)
                cos_q, sin_q = cos_ref[:, 0 : 2 * HD], sin_ref[:, 0 : 2 * HD]
                dq = dq * cos_q + half_turn(dq * sin_q)
                d_qkv_ref[m, seq, lanes] = dq.astype(BF16)
                term = dot_tn(ds_low, q_pad) + dot_tn(probs.astype(BF16), do_pad)
                grads = term if grads is None else grads + term
            grads = grads.astype(BF16)
            for i in range(n_dp):
                shares[m, i % 2, i // 2, seq, pair] = grads[i * seq_rows : (i + 1) * seq_rows]

    def attend_back_range(m, low, high):
        @pl.loop(low, high)
        def _(s):
            attend_back_seq(m, s)

    def send_along(m):
        arrive([core_moves[m]])
        for k in range(1, line):
            there = paired(place, k)
            z_send[m, k] = (
                shares[m, core, there].astype(F32) + met[m, there].astype(F32)
            ).astype(BF16)
        start(z_moves[m])

    def close_keys(m):
        arrive(z_moves[m])
        total = shares[m, core, place].astype(F32) + met[m, place].astype(F32)
        for k in range(1, line):
            total = total + z_got[m, k].astype(F32)
        cos_k, sin_k = cos_ref[:, q_width:], sin_ref[:, q_width:]
        for s in range(SEQS):
            seq = slice(s * seq_rows, (s + 1) * seq_rows)
            grad = total[seq]
            d_qkv_ref[m, seq, q_width:] = (grad * cos_k + half_turn(grad * sin_k)).astype(BF16)
        start(heads_moves[m])

    def close_block(m):
        arrive(y_moves[m])
        part = slice(m * rows, (m + 1) * rows)
        block_low[m] = (middle_ref[part, :] + total_of(y_got, m)).astype(BF16)
        start(block_first[m])
        keep_block[m].start()

    def close_tokens(m):
        arrive(heads_moves[m])
        part = slice(m * rows, (m + 1) * rows)
        heads = [d_qkv_ref[m, 0:rows, :]] + [heads_got[m, k] for k in others]
        sides = []
        for side in range(2):
            total = dot_nt(heads[0], weights[side, :, 0:width])
            for k in others:
                total = total + dot_nt(heads[k], weights[side, :, k * width : (k + 1) * width])
            sides.append(total)
        d_act = jnp.where(
            core == 0,
            jnp.concatenate(sides, axis=1),
            jnp.concatenate(sides[::-1], axis=1),
        )
        x_part = x_ref[part, :].astype(F32)
        scale = mean_square_scale(x_part)
        normed = x_part * scale
        gain_ref[0:1, :] += jnp.sum(d_act * normed, axis=0, keepdims=True)
        tok_low[m] = (own_mid[m] + norm_back(d_act * gain_one, normed, scale)).astype(BF16)

    arrive(do_moves[0])
    attend_back_range(0, 0, SEQS)
    core_moves[0].start()
    arrive(do_moves[1])
    attend_back_range(1, 0, SEQS // 2)
    send_along(0)
    relay_rows(mid_first, mid_relay)
    attend_back_range(1, SEQS // 2, SEQS)
    core_moves[1].start()
    for copy in load_qkv:
        copy.wait()
    close_block(0)
    close_keys(0)
    send_along(1)
    close_block(1)
    close_tokens(0)
    close_keys(1)
    relay_rows(block_first, block_relay)
    close_tokens(1)
    close_rows(mid_first, mid_relay)
    close_rows(block_first, block_relay)
    for m in batches:
        for moves in (y_moves[m], do_moves[m], [core_moves[m]], z_moves[m], heads_moves[m]):
            sent(moves)
        keep[m].wait()
        keep_block[m].wait()


def tail(
    n_dp, n_tp, group, sums, arrived, seed, middle, x, gains, out_w, qkv_w, q, kv, qpos, kpos, cos, sin
):
    own_rows, depth = middle.shape
    rows = own_rows // MICRO
    batch_rows = n_tp * rows
    line = n_dp // 2
    q_width, kv_width = q.shape[3], kv.shape[4]
    width = q_width + kv_width
    anywhere = pl.BlockSpec(memory_space=pl.ANY)
    vmem = pl.BlockSpec(memory_space=pltpu.VMEM)
    dma = pltpu.SemaphoreType.DMA
    gathered = jax.ShapeDtypeStruct((MICRO, n_tp, rows, depth), BF16)
    return pl.pallas_call(
        functools.partial(tail_kernel, n_dp, n_tp, group),
        in_specs=[anywhere] * 6 + [vmem] * 4 + [anywhere] * 4 + [vmem] * 6,
        out_specs=[vmem, anywhere, anywhere, vmem, vmem],
        out_shape=[
            jax.ShapeDtypeStruct((MICRO, batch_rows, width), BF16),
            gathered,
            gathered,
            jax.ShapeDtypeStruct((MICRO, rows, depth), BF16),
            jax.ShapeDtypeStruct((2, depth), F32),
        ],
        scratch_shapes=[
            pltpu.VMEM((2, depth // 2, n_tp * width), BF16),
            pltpu.VMEM((MICRO, n_tp, rows, depth), BF16),
            pltpu.VMEM((MICRO, n_tp, rows, depth), BF16),
            pltpu.VMEM((MICRO, rows, depth), F32),
            pltpu.VMEM((MICRO, rows, depth), BF16),
            pltpu.VMEM((MICRO, rows, depth), BF16),
            pltpu.VMEM((MICRO, n_tp, rows, q_width), BF16),
            pltpu.VMEM((MICRO, batch_rows, q_width), BF16),
            pltpu.VMEM((MICRO, 2, line, batch_rows, kv_width), BF16),
            pltpu.VMEM((MICRO, line, batch_rows, kv_width), BF16),
            pltpu.VMEM((MICRO, line, batch_rows, kv_width), BF16),
            pltpu.VMEM((MICRO, line, batch_rows, kv_width), BF16),
            pltpu.VMEM((MICRO, n_tp, rows, width), BF16),
            dma((7, 2)),
        ]
        + [dma((MICRO, n_tp))] * 8
        + [dma((MICRO,))] * 2
        + [dma((MICRO, line))] * 2
        + [dma((MICRO, n_tp))] * 2,
        compiler_params=pltpu.CompilerParams(
            collective_id=0, has_side_effects=True, vmem_limit_bytes=VMEM_LIMIT
        ),
        cost_estimate=hint(
            flops=10**10,
            bytes_accessed=10**8,
            transcendentals=0,
        ),
        name="tail",
    )(
        sums[0][1],
        sums[1][1],
        sums[0][0],
        sums[1][0],
        *arrived,
        seed,
        middle,
        x,
        gains,
        *out_w,
        *qkv_w,
        q,
        kv,
        qpos,
        kpos,
        cos,
        sin,
    )


def spread_kernel(rank_ref, out_ref, tok_ref, block_ref, grad_ref):
    block_ref[...] = out_ref[...]
    grad_ref[...] = tok_ref[...].astype(F32)


def spread(rank, out_rows, tok_rows):
    micro, n_tp, rows, depth = out_rows.shape
    here = pl.BlockSpec((1, 1, rows, depth), lambda m, k, r: (m, k, 0, 0))
    there = pl.BlockSpec((1, 1, rows, depth), lambda m, k, r: (m, r[0] ^ k, 0, 0))
    return pl.pallas_call(
        spread_kernel,
        grid_spec=pltpu.PrefetchScalarGridSpec(
            num_scalar_prefetch=1,
            grid=(micro, n_tp),
            in_specs=[here, here],
            out_specs=[there, there],
        ),
        out_shape=[
            jax.ShapeDtypeStruct(out_rows.shape, BF16),
            jax.ShapeDtypeStruct(out_rows.shape, F32),
        ],
        compiler_params=pltpu.CompilerParams(vmem_limit_bytes=VMEM_LIMIT),
        name="spread",
    )(rank, out_rows, tok_rows)


def per_device(
    n_dp,
    n_tp,
    tokens,
    cotangent,
    span_order,
    w_query,
    w_keyval,
    w_output,
    w_gateup,
    w_down,
    norm_gains,
    mean_query,
    square_query,
    mean_keyval,
    square_keyval,
    mean_output,
    square_output,
    mean_gateup,
    square_gateup,
    mean_down,
    square_down,
    mean_gains,
    square_gains,
):
    depth = tokens.shape[1]
    span_rows = 2 * CH
    block_rows = SEQS * span_rows // n_tp
    parts = span_rows // min(span_rows, block_rows)
    q_width = w_query.shape[1]
    kv_width = w_keyval.shape[1]
    hidden_width = w_down.shape[0]
    own_depth = w_query.shape[0]
    group = q_width // HD // (kv_width // (2 * HD))
    device = lax.axis_index("dp")
    rank = lax.axis_index("tp")
    line = n_dp // 2
    place, core = device // 2, device % 2

    def swap(value, k):
        return lax.ppermute(value, "tp", [(i, i ^ k) for i in range(n_tp)])

    def reorder(value):
        return jnp.concatenate(
            [lax.dynamic_slice_in_dim(value, rank ^ k, 1, axis=1) for k in range(n_tp)], axis=1
        )

    def gather_blocks(own):
        half = own.shape[0] // 2
        got = [own, swap(own, 1), swap(own, 2)]
        got.append(jnp.concatenate([swap(got[1][:half], 2), swap(got[2][half:], 1)], axis=0))
        return got + [swap(own, k) for k in range(4, n_tp)]

    def exchange(blocks):
        return [blocks[0]] + [swap(blocks[k], k) for k in range(1, n_tp)]

    def total_of(parts):
        total = parts[0].astype(F32)
        for part in parts[1:]:
            total = total + part.astype(F32)
        return total

    def gather_pair(owns):
        got = [owns, [swap(own, 1) for own in owns], [swap(own, 2) for own in owns]]
        got.append([swap(got[1][0], 2)] + [swap(own, 1) for own in got[2][1:]])
        return got + [[swap(own, k) for own in owns] for k in range(4, n_tp)]

    def scatter_pair(blocks):
        first = swap(blocks[0][3], 1)
        seconds = [swap(blocks[m][3], 2) for m in range(1, MICRO)]
        to_two = total_of([blocks[0][2], first]).astype(BF16)
        to_one = [total_of([blocks[m][1], seconds[m - 1]]).astype(BF16) for m in range(1, MICRO)]
        yield [to_two] + to_one
        totals = []
        for m in range(MICRO):
            one = blocks[m][1] if m == 0 else to_one[m - 1]
            two = to_two if m == 0 else blocks[m][2]
            far = [swap(blocks[m][k], k) for k in range(4, n_tp)]
            totals.append(total_of([blocks[m][0], swap(one, 1), swap(two, 2)] + far))
        yield totals

    def line_sum(other, own):
        met = lax.ppermute(other, "dp", [(i, i ^ 1) for i in range(n_dp)])
        yield [met]

        def share(index):
            index = jnp.clip(index, 0, line - 1)
            return lax.dynamic_index_in_dim(own, index, 0, False).astype(
                F32
            ) + lax.dynamic_index_in_dim(met, index, 0, False).astype(F32)

        sends = []
        for far in range(1, line):
            for way in (far, -far):
                sends.append((way, share(place + way).astype(BF16)))
        yield [value for _, value in sends]
        total = share(place)
        for far in range(1, line):
            arrived = []
            for way, value in sends:
                if abs(way) == far:
                    pairs = [
                        (i, i + 2 * way) for i in range(n_dp) if 0 <= i + 2 * way < n_dp
                    ]
                    arrived.append(lax.ppermute(value, "dp", pairs))
            if far <= 3:
                yield arrived
            for value in arrived:
                total = total + value.astype(F32)
        yield [total]

    def my_half(value):
        return lax.dynamic_slice_in_dim(value, core * (depth // 2), depth // 2, axis=0)

    def swap_cores(value):
        return lax.ppermute(value, "dp", [(i, i ^ 1) for i in range(n_dp)])

    def both_halves(near, far):
        return jnp.where(
            core == 0,
            jnp.concatenate([near, far], axis=1),
            jnp.concatenate([far, near], axis=1),
        )

    def after(value, *earlier):
        return lax.optimization_barrier((value,) + earlier)[0]

    qkv_full = lax.all_gather(
        jnp.concatenate([w_query, w_keyval], axis=1), "dp", axis=0, tiled=True
    )
    gains_full = lax.all_gather(norm_gains, "dp", axis=1, tiled=True)
    out_t_full = lax.all_gather(w_output.T, "dp", axis=0, tiled=True)

    offsets = jnp.arange(CH, dtype=jnp.int32)
    all_pos = (span_order[:, None] * CH + offsets[None, :]).reshape(n_dp, parts, -1)
    all_pos = jnp.stack([all_pos[:, (rank % parts) ^ p] for p in range(parts)], axis=1)
    own_pos = lax.dynamic_slice_in_dim(all_pos, device, 1).reshape(-1)
    all_pos = all_pos.reshape(-1)
    qpos, kpos = own_pos[:, None], all_pos[None, :]
    kv_kinds = [True, False] * (kv_width // (2 * HD))
    cos_t, sin_t = lane_tables(own_pos, [True] * (q_width // HD) + kv_kinds)

    x = reorder(tokens.reshape(MICRO, n_tp, block_rows, depth))
    seed = reorder(cotangent.reshape(MICRO, n_tp, block_rows, depth))
    batch_rows = SEQS * span_rows
    rows = MICRO * batch_rows
    gain_one, gain_two = gains_full[0:1], gains_full[1:2]
    attn_in, qkv = project(x.reshape(rows, depth), gain_one, qkv_full, cos_t, sin_t)
    qkv = qkv.reshape(MICRO, SEQS, span_rows, q_width + kv_width)
    q, kv = qkv[..., :q_width], qkv[..., q_width:]
    kv_all = lax.all_gather(kv, "dp", axis=0, tiled=False)

    sub = min(SUB, hidden_width // CHUNKS)
    chunk = hidden_width // CHUNKS
    w_down_t = w_down.T
    mlp_full = []
    for c in range(CHUNKS):
        pieces = []
        for start in range(c * chunk, (c + 1) * chunk, sub):
            cols = slice(start, start + sub)
            pieces += [w_gateup[0][:, cols], w_gateup[1][:, cols], w_down_t[:, cols]]
        shard = jnp.concatenate(pieces, axis=1)
        mlp_full.append(lax.all_gather(shard, "dp", axis=0, tiled=True))

    attended = attend(qpos, kpos, q, kv_all, group)
    attended_blocks = attended.reshape(MICRO, n_tp, block_rows, q_width)
    out_near = my_half(out_t_full)
    out_near = jnp.concatenate([out_near] + [swap(out_near, k) for k in range(1, n_tp)], axis=1)
    out_far = swap_cores(out_near)
    heads_in = exchange([attended_blocks[:, k] for k in range(n_tp)])
    own_rows = MICRO * block_rows
    x_own = x[:, 0].reshape(own_rows, depth).astype(F32)
    heads_cat = jnp.concatenate([v.reshape(own_rows, q_width) for v in heads_in], axis=1)
    middle = x_own + both_halves(dot_nt(heads_cat, out_near), dot_nt(heads_cat, out_far))
    scale_two = mean_square_scale(middle)
    normed_two = middle * scale_two
    u_own = (normed_two * gain_two.astype(F32)).astype(BF16)
    batches = range(MICRO)
    gathered = [g.reshape(MICRO, block_rows, depth) for g in gather_blocks(u_own)]
    u = [jnp.concatenate([gathered[k][m] for k in range(n_tp)], axis=0) for m in batches]
    g = [seed[m].reshape(batch_rows, depth) for m in batches]

    qkv_half = after(my_half(qkv_full), u[0])
    quarter = depth // 4
    qkv_width = q_width + kv_width
    qkv_near = jnp.zeros((depth // 2, n_tp * qkv_width), BF16)
    qkv_near = lax.dynamic_update_slice(qkv_near, qkv_half, (0, 0))
    qkv_moves = [(k, i) for i in range(2) for k in range(1, min(n_tp, 3))]
    qkv_moves = [qkv_moves[:2], qkv_moves[2:]] + [
        [(k, i) for k in range(3, n_tp)] for i in range(2)
    ]

    def move_qkv(buffer):
        for k, i in qkv_moves.pop(0) if qkv_moves else []:
            got = swap(qkv_half[i * quarter : (i + 1) * quarter], k)
            buffer = lax.dynamic_update_slice(buffer, got, (i * quarter, k * qkv_width))
        return buffer

    def blocks_of(value):
        return [value[k * block_rows : (k + 1) * block_rows] for k in range(n_tp)]

    def own_part(value, m):
        return value[m * block_rows : (m + 1) * block_rows]

    core_index = core.astype(jnp.int32).reshape(1)
    gain_two_f = gain_two.astype(F32)
    gain_one_f = gain_one.astype(F32)
    cos_q, sin_q = cos_t[:, : group * HD], sin_t[:, : group * HD]
    cos_k, sin_k = cos_t[:, q_width:], sin_t[:, q_width:]
    gain_grads = [0.0, 0.0]
    sums = [None] * MICRO

    arrived = []

    def expand(c, m, *earlier):
        carry = (n_tp, sums[m - 1][1]) if c == CHUNKS - 1 and m else ()
        hid, dgu, y_low, du_low, *got = feed_forward(
            after(u[m], *earlier), g[m], mlp_full[c], sub, sums[m], *carry
        )
        sums[m] = (y_low, du_low)
        arrived.extend(got)
        return hid, dgu

    def close(hids, dgus, last, *earlier):
        carry = (n_tp, sums[-1][1]) if last else ()
        grads, *got = outer_products(
            [after(u[0], *earlier)] + u[1:], g, hids, dgus, own_depth, sub, *carry
        )
        arrived.extend(got)
        return grads, lax.psum_scatter(grads, "dp", scatter_dimension=0, tiled=False)

    chunk_grads = []
    earlier = []
    for c in range(CHUNKS - 1):
        hids, dgus = [], []
        for m in batches:
            hid, dgu = expand(c, m, *earlier)
            qkv_near = move_qkv(qkv_near)
            earlier = [hid, qkv_near]
            hids.append(hid)
            dgus.append(dgu)
        grads, owned = close(hids, dgus, False, *earlier)
        qkv_near = move_qkv(qkv_near)
        earlier = [grads, qkv_near]
        chunk_grads.append(owned)

    d_middles, d_mid_lows, d_attends, all_rows = [], [], [], []
    hids, dgus = [], []
    for m in batches:
        hid, dgu = expand(CHUNKS - 1, m, *earlier)
        qkv_near = move_qkv(qkv_near)
        earlier = [hid, qkv_near]
        if m == 0:
            qkv_far = swap_cores(qkv_near)
        hids.append(hid)
        dgus.append(dgu)
    grads, owned = close(hids, dgus, True, *earlier, qkv_far)
    chunk_grads.append(owned)
    tail_sums = [after(sums[0], grads)] + sums[1:]
    d_qkv, mid_rows, out_rows, tok_low, gain_part = tail(
        n_dp,
        n_tp,
        group,
        tail_sums,
        arrived,
        seed[:, 0].reshape(own_rows, depth),
        middle,
        x[:, 0].reshape(own_rows, depth),
        gains_full,
        (out_near, out_far),
        (qkv_near, qkv_far),
        q,
        kv_all,
        qpos,
        kpos,
        cos_t,
        sin_t,
    )
    mlp_grads = [v.reshape(own_depth, -1) for v in chunk_grads]
    attn_part = attn_weight_grads(
        attn_in,
        mid_rows.reshape(rows, depth),
        d_qkv.reshape(rows, q_width + kv_width),
        attended.reshape(rows, q_width),
        gain_part,
        own_depth,
    )
    attn_part = after(attn_part, *chunk_grads)
    attn_grads = lax.psum_scatter(attn_part, "dp", scatter_dimension=0, tiled=False)
    (tok_rows,) = gather_rows(n_tp, (after(tok_low, attn_part),))
    block_output, grad_tokens = spread(rank.astype(jnp.int32).reshape(1), out_rows, tok_rows)
    block_output = block_output.reshape(rows, depth)
    grad_tokens = grad_tokens.reshape(rows, depth)
    gain_part = attn_grads[:, 2 * q_width + kv_width :]
    gain_sum = gain_part.astype(F32)
    for k in range(1, n_tp):
        gain_sum = gain_sum + swap(gain_part, k).astype(F32)

    grad_query = attn_grads[:, :q_width].astype(F32)
    grad_keyval = attn_grads[:, q_width : q_width + kv_width].astype(F32)
    grad_output = attn_grads[:, q_width + kv_width : 2 * q_width + kv_width].astype(F32).T
    grad_gains = gain_sum[:, :2].T
    def with_update(gradient, old_mean, square, weight, decay):
        return (gradient,) + adam_update(gradient, old_mean, square, weight.astype(F32), decay)

    return (
        (block_output, grad_tokens)
        + with_update(grad_query, mean_query, square_query, w_query, weight_decay)
        + with_update(grad_keyval, mean_keyval, square_keyval, w_keyval, weight_decay)
        + with_update(grad_output, mean_output, square_output, w_output, weight_decay)
        + step_from_chunks(
            mlp_grads, mean_gateup, square_gateup, w_gateup, sub, 0, False, weight_decay
        )
        + step_from_chunks(mlp_grads, mean_down, square_down, w_down, sub, 2, True, weight_decay)
        + with_update(grad_gains, mean_gains, square_gains, norm_gains, 0.0)
    )


def solution(mesh):
    rows_first = P("dp", "tp")
    cols_last = P("tp", "dp")
    stacked = P(None, "dp", "tp")
    gains = P(None, "dp")
    token_rows = P("dp", None)
    placed = (
        (token_rows, token_rows, P())
        + (rows_first, rows_first, cols_last, stacked, cols_last, gains)
        + (rows_first,) * 4
        + (cols_last,) * 2
        + (stacked,) * 2
        + (cols_last,) * 2
        + (gains,) * 2
    )
    results = (
        (token_rows, token_rows)
        + (rows_first,) * 8
        + (cols_last,) * 4
        + (stacked,) * 4
        + (cols_last,) * 4
        + (gains,) * 4
    )
    return jax.shard_map(
        functools.partial(per_device, mesh.shape["dp"], mesh.shape["tp"]),
        mesh=mesh,
        in_specs=placed,
        out_specs=results,
        check_vma=False,
    )
```

```python
import functools

import jax
import jax.numpy as jnp
from jax import lax
from jax.experimental import pallas as pl
from jax.experimental.pallas import tpu as pltpu
from jax.sharding import PartitionSpec as P

HD = 64
CH = 64
SEQS = 4
MICRO = 2
STEP = 5
CHUNKS = 2
SUB = 512

norm_eps = 1e-05
rope_base = 500000.0
beta_one = 0.9
beta_two = 0.95
learn_rate = 0.01
weight_decay = 0.1
adam_eps = 1e-08
masked_score = -1e30

F32 = jnp.float32
BF16 = jnp.bfloat16
VMEM_LIMIT = 60 * 1024 * 1024
HINT = 20


def hint(flops, bytes_accessed, transcendentals):
    return pl.CostEstimate(
        flops=flops // HINT, bytes_accessed=bytes_accessed // HINT, transcendentals=transcendentals
    )


def lane_tables(positions, kinds):
    half_size = HD // 2
    frequencies = rope_base ** (-(jnp.arange(half_size, dtype=F32) * 2.0 / HD))
    angles = positions.astype(F32)[:, None] * frequencies[None, :]
    cos_half, sin_half = jnp.cos(angles), jnp.sin(angles)
    cos_head = jnp.concatenate([cos_half, cos_half], axis=-1)
    sin_head = jnp.concatenate([-sin_half, sin_half], axis=-1)
    ones, zeros = jnp.ones_like(cos_head), jnp.zeros_like(cos_head)
    cos_all, sin_all = [], []
    for kind in kinds:
        cos_all.append(cos_head if kind else ones)
        sin_all.append(sin_head if kind else zeros)
    return jnp.concatenate(cos_all, axis=-1), jnp.concatenate(sin_all, axis=-1)


def half_turn(values):
    width = values.shape[-1]
    axis = values.ndim - 1
    lane = lax.broadcasted_iota(jnp.int32, values.shape, axis)
    ahead = pltpu.roll(values, width - HD // 2, axis)
    behind = pltpu.roll(values, HD // 2, axis)
    return jnp.where(lane % HD < HD // 2, ahead, behind)


def mean_square_scale(values):
    return lax.rsqrt(jnp.mean(values * values, axis=-1, keepdims=True) + norm_eps)


def project_kernel(x_ref, gain_ref, w_ref, cos_ref, sin_ref, a_ref, qkv_ref):
    x = x_ref[...].astype(F32)
    a = (x * mean_square_scale(x) * gain_ref[...].astype(F32)).astype(BF16)
    a_ref[...] = a
    t = jnp.dot(a, w_ref[...], preferred_element_type=F32)
    qkv_ref[...] = (t * cos_ref[...] + half_turn(t) * sin_ref[...]).astype(BF16)


def project(x, gain, weight, cos_t, sin_t):
    rows, depth = x.shape
    width = weight.shape[1]
    block = cos_t.shape[0]
    return pl.pallas_call(
        project_kernel,
        grid=(rows // block,),
        in_specs=[
            pl.BlockSpec((block, depth), lambda i: (i, 0)),
            pl.BlockSpec((1, depth), lambda i: (0, 0)),
            pl.BlockSpec((depth, width), lambda i: (0, 0)),
            pl.BlockSpec((block, width), lambda i: (0, 0)),
            pl.BlockSpec((block, width), lambda i: (0, 0)),
        ],
        out_specs=[
            pl.BlockSpec((block, depth), lambda i: (i, 0)),
            pl.BlockSpec((block, width), lambda i: (i, 0)),
        ],
        out_shape=[
            jax.ShapeDtypeStruct((rows, depth), BF16),
            jax.ShapeDtypeStruct((rows, width), BF16),
        ],
        compiler_params=pltpu.CompilerParams(vmem_limit_bytes=VMEM_LIMIT),
        cost_estimate=hint(
            flops=2 * rows * depth * width, bytes_accessed=4 * rows * depth, transcendentals=0
        ),
        name="project",
    )(x, gain, weight, cos_t, sin_t)


def stack_heads(block, group, upper):
    lane = lax.broadcasted_iota(jnp.int32, (block.shape[0], 2 * HD), 1)
    keep = (lane >= HD) if upper else (lane < HD)
    parts = []
    for head in range(group):
        pair = block[:, (head // 2) * 2 * HD : (head // 2 + 1) * 2 * HD].astype(F32)
        if (head % 2 == 1) != upper:
            pair = pltpu.roll(pair, HD, 1)
        parts.append(jnp.where(keep, pair, 0.0).astype(BF16))
    return jnp.concatenate(parts, axis=0)


def unstack_heads(stacked, group, upper):
    rows = stacked.shape[0] // group
    lane = lax.broadcasted_iota(jnp.int32, (rows, 2 * HD), 1)
    pairs = []
    for pair in range(group // 2):
        even = stacked[(2 * pair) * rows : (2 * pair + 1) * rows]
        odd = stacked[(2 * pair + 1) * rows : (2 * pair + 2) * rows]
        if upper:
            even = pltpu.roll(even, HD, 1)
        else:
            odd = pltpu.roll(odd, HD, 1)
        pairs.append(jnp.where(lane < HD, even, odd))
    return jnp.concatenate(pairs, axis=1)


def scores_and_probs(q_pad, keys, qpos, kpos, group):
    scores = (
        lax.dot_general(q_pad, keys, (((1,), (1,)), ((), ())), preferred_element_type=F32)
        * HD ** (-0.5)
    )
    rows = qpos.shape[0]
    blocked = kpos > qpos
    masked = [
        jnp.where(blocked, masked_score, scores[h * rows : (h + 1) * rows]) for h in range(group)
    ]
    scores = jnp.concatenate(masked, axis=0)
    exponent = jnp.exp(scores - jnp.max(scores, axis=-1, keepdims=True))
    return exponent * (1.0 / jnp.sum(exponent, axis=-1, keepdims=True))


def attend_kernel(group, qpos_ref, kpos_ref, q_ref, kv_ref, o_ref):
    keyvals = kv_ref[...].reshape(-1, 2 * HD)
    q_pad = stack_heads(q_ref[...].reshape(-1, group * HD), group, False)
    probs = scores_and_probs(q_pad, keyvals, qpos_ref[...], kpos_ref[...], group)
    out = jnp.dot(probs.astype(BF16), keyvals, preferred_element_type=F32)
    o_ref[...] = unstack_heads(out, group, True).astype(BF16).reshape(o_ref.shape)


def attend_back_kernel(
    group, qpos_ref, kpos_ref, cos_ref, sin_ref, q_ref, do_ref, kv_ref, dq_ref, dkv_ref
):
    keyvals = kv_ref[...].reshape(-1, 2 * HD)
    q_pad = stack_heads(q_ref[...].reshape(-1, group * HD), group, False)
    do_pad = stack_heads(do_ref[...].reshape(-1, group * HD), group, True)
    probs = scores_and_probs(q_pad, keyvals, qpos_ref[...], kpos_ref[...], group)
    d_probs = lax.dot_general(
        do_pad, keyvals, (((1,), (1,)), ((), ())), preferred_element_type=F32
    )
    d_scores = probs * (d_probs - jnp.sum(d_probs * probs, axis=-1, keepdims=True))
    ds_low = d_scores.astype(BF16) * HD ** (-0.5)
    dq = jnp.dot(ds_low, keyvals, preferred_element_type=F32)
    dq = unstack_heads(dq, group, False)
    dq = dq * cos_ref[...] + half_turn(dq * sin_ref[...])
    dq_ref[...] = dq.astype(BF16).reshape(dq_ref.shape)
    contract = (((0,), (0,)), ((), ()))
    d_keyvals = lax.dot_general(
        ds_low, q_pad, contract, preferred_element_type=F32
    ) + lax.dot_general(probs.astype(BF16), do_pad, contract, preferred_element_type=F32)
    dkv_ref[...] = d_keyvals.astype(BF16).reshape(dkv_ref.shape)


def attention_specs(qkv_heads, n_dp, span_rows, group):
    q_spec = pl.BlockSpec((1, 1, span_rows, group * HD), lambda m, s, h: (m, s, 0, h))
    kv_spec = pl.BlockSpec(
        (n_dp, 1, 1, span_rows, 2 * HD), lambda m, s, h: (0, m, s, 0, h)
    )
    pos_q = pl.BlockSpec((span_rows, 1), lambda m, s, h: (0, 0))
    pos_k = pl.BlockSpec((1, n_dp * span_rows), lambda m, s, h: (0, 0))
    return q_spec, kv_spec, pos_q, pos_k


def attend(qpos, kpos, q, kv, group):
    micro, seqs, span_rows, width = q.shape
    n_dp, heads = kv.shape[0], width // (group * HD)
    q_spec, kv_spec, pos_q, pos_k = attention_specs(heads, n_dp, span_rows, group)
    return pl.pallas_call(
        functools.partial(attend_kernel, group),
        grid=(micro, seqs, heads),
        in_specs=[pos_q, pos_k, q_spec, kv_spec],
        out_specs=q_spec,
        out_shape=jax.ShapeDtypeStruct(q.shape, BF16),
        compiler_params=pltpu.CompilerParams(vmem_limit_bytes=VMEM_LIMIT),
        cost_estimate=hint(
            flops=16 * micro * seqs * span_rows * width * n_dp * span_rows,
            bytes_accessed=4 * q.size + 2 * kv.size,
            transcendentals=0,
        ),
        name="attend",
    )(qpos, kpos, q, kv)


def attend_back(qpos, kpos, cos_q, sin_q, q, d_out, kv, group):
    micro, seqs, span_rows, width = q.shape
    n_dp, heads = kv.shape[0], width // (group * HD)
    q_spec, kv_spec, pos_q, pos_k = attention_specs(heads, n_dp, span_rows, group)
    table = pl.BlockSpec((span_rows, group * HD), lambda m, s, h: (0, 0))
    return pl.pallas_call(
        functools.partial(attend_back_kernel, group),
        grid=(micro, seqs, heads),
        in_specs=[pos_q, pos_k, table, table, q_spec, q_spec, kv_spec],
        out_specs=[q_spec, kv_spec],
        out_shape=[
            jax.ShapeDtypeStruct(q.shape, BF16),
            jax.ShapeDtypeStruct(kv.shape, BF16),
        ],
        compiler_params=pltpu.CompilerParams(vmem_limit_bytes=VMEM_LIMIT),
        cost_estimate=hint(
            flops=40 * micro * seqs * span_rows * width * n_dp * span_rows,
            bytes_accessed=6 * q.size + 4 * kv.size,
            transcendentals=0,
        ),
        name="attend_back",
    )(qpos, kpos, cos_q, sin_q, q, d_out, kv)


def norm_back(d_normed, normed, scale):
    return scale * (d_normed - normed * jnp.mean(d_normed * normed, axis=-1, keepdims=True))


def adam_update(gradient, old_mean, square, weight, decay_factor):
    moment = beta_one * old_mean + (1.0 - beta_one) * gradient
    spread = beta_two * square + (1.0 - beta_two) * gradient * gradient
    change = -learn_rate * (
        moment / (1.0 - beta_one**STEP) / (jnp.sqrt(spread / (1.0 - beta_two**STEP)) + adam_eps)
        + decay_factor * weight
    )
    return (moment, spread, change)


def dot(left, right):
    return jnp.dot(left, right, preferred_element_type=F32)


def dot_nt(left, right):
    return lax.dot_general(left, right, (((1,), (1,)), ((), ())), preferred_element_type=F32)


def dot_tn(left, right):
    return lax.dot_general(left, right, (((0,), (0,)), ((), ())), preferred_element_type=F32)


def paired(index, k):
    bit = 1
    while bit <= k:
        if k & bit:
            index = index + bit - 2 * bit * ((index // bit) % 2)
        bit *= 2
    return index


def remote(src, dst, send, recv, device):
    return pltpu.make_async_remote_copy(
        src_ref=src,
        dst_ref=dst,
        send_sem=send,
        recv_sem=recv,
        device_id=device,
        device_id_type=pl.DeviceIdType.MESH,
    )


def meet(peers):
    barrier = pltpu.get_barrier_semaphore()
    for peer in peers:
        pl.semaphore_signal(barrier, inc=1, device_id=peer, device_id_type=pl.DeviceIdType.MESH)
    pl.semaphore_wait(barrier, len(peers))


def start(moves):
    for move in moves:
        move.start()


def arrive(moves):
    for move in moves:
        move.wait_recv()


def sent(moves):
    for move in moves:
        move.wait_send()


def row_moves(remote, rank, n_tp, low, got, send, recv):
    first = [
        [
            remote(low.at[m], got.at[m, k], send.at[m, k], recv.at[m, k], rank(k))
            for k in range(1, n_tp)
            if k != 3
        ]
        for m in range(MICRO)
    ]
    relay = [
        remote(got.at[m, 1 + m], got.at[m, 3], send.at[m, 3], recv.at[m, 3], rank(2 - m))
        for m in range(MICRO)
    ]
    return first, relay


def relay_rows(first, relay):
    for m in range(MICRO):
        first[m][m].wait_recv()
        relay[m].start()


def close_rows(first, relay):
    for m in range(MICRO):
        for i, move in enumerate(first[m]):
            if i != m:
                move.wait_recv()
            move.wait_send()
        relay[m].wait_recv()
        relay[m].wait_send()


def carried(n_tp, src, got, send, recv):
    dp, tp = lax.axis_index("dp"), lax.axis_index("tp")
    rows = got.shape[1]
    return [
        remote(
            src.at[pl.ds(k * rows, rows)],
            got.at[k],
            send.at[k],
            recv.at[k],
            (dp, paired(tp, k)),
        )
        for k in range(1, n_tp)
    ]


def carry_start(n_tp, *move):
    dp, tp = lax.axis_index("dp"), lax.axis_index("tp")
    meet([(dp, paired(tp, k)) for k in range(1, n_tp)])
    start(carried(n_tp, *move))


def carry_end(n_tp, *move):
    moves = carried(n_tp, *move)
    arrive(moves)
    sent(moves)


def gated_kernel(n_tp, last, steps, u_ref, g_ref, w_ref, *refs):
    refs = list(refs)
    move = None
    if n_tp:
        send, recv = refs[-2:]
        src, got = refs.pop(2), refs[6]
        move = (src, got, send, recv)
        refs = refs[:6] + refs[7:-2]
    if last:
        y_old, du_old = refs[:2]
        refs = refs[2:]
    hid_ref, dgu_ref, y_out, du_out, y_sum, du_sum, y_low, du_low, sem = refs
    step = pl.program_id(0)
    depth = w_ref.shape[0]
    sub = hid_ref.shape[1]
    cols = min(512, depth)

    @pl.when(step == 0)
    def _():
        if move:
            carry_start(n_tp, *move)
        y_sum[...] = jnp.zeros_like(y_sum)
        du_sum[...] = jnp.zeros_like(du_sum)
        if last:
            pltpu.make_async_copy(y_old, y_low, sem.at[0]).start()
            pltpu.make_async_copy(du_old, du_low, sem.at[1]).start()

    gate_proj = dot(u_ref[...], w_ref[:, :sub])
    up_proj = dot(u_ref[...], w_ref[:, sub : 2 * sub])
    sigmoid_gate = jax.nn.sigmoid(gate_proj)
    silu_gate = gate_proj * sigmoid_gate
    hid_ref[...] = (silu_gate * up_proj).astype(BF16)
    d_hidden = dot(g_ref[...], w_ref[:, 2 * sub :])
    d_gate = d_hidden * up_proj * sigmoid_gate * (1.0 + gate_proj * (1.0 - sigmoid_gate))
    dgu_ref[:, :sub] = d_gate.astype(BF16)
    dgu_ref[:, sub:] = (d_hidden * silu_gate).astype(BF16)
    for start in range(0, depth, cols):
        part = slice(start, start + cols)
        du_sum[:, part] += dot_nt(dgu_ref[...], w_ref[part, : 2 * sub])
        y_sum[:, part] += dot_nt(hid_ref[...], w_ref[part, 2 * sub :])

    @pl.when(step == steps - 1)
    def _():
        copy_y = pltpu.make_async_copy(y_low, y_out, sem.at[0])
        copy_du = pltpu.make_async_copy(du_low, du_out, sem.at[1])
        if last:
            pltpu.make_async_copy(y_old, y_low, sem.at[0]).wait()
            pltpu.make_async_copy(du_old, du_low, sem.at[1]).wait()
            du_low[...] = (du_sum[...] + du_low[...].astype(F32)).astype(BF16)
            copy_du.start()
            y_low[...] = (y_sum[...] + y_low[...].astype(F32)).astype(BF16)
        else:
            du_low[...] = du_sum[...].astype(BF16)
            copy_du.start()
            y_low[...] = y_sum[...].astype(BF16)
        copy_y.start()
        copy_du.wait()
        copy_y.wait()
        if move:
            carry_end(n_tp, *move)


def carrier_params(n_tp, collective_id):
    if not n_tp:
        return pltpu.CompilerParams(vmem_limit_bytes=VMEM_LIMIT)
    return pltpu.CompilerParams(
        collective_id=collective_id, has_side_effects=True, vmem_limit_bytes=VMEM_LIMIT
    )


def feed_forward(u, g, weights, sub, sums, n_tp=0, carry=None):
    rows, depth = u.shape
    steps = weights.shape[1] // (3 * sub)
    last = sums is not None
    whole = functools.partial(pl.BlockSpec, pipeline_mode=pl.Buffered(1))
    anywhere = pl.BlockSpec(memory_space=pl.ANY)
    return pl.pallas_call(
        functools.partial(gated_kernel, n_tp, last, steps),
        grid=(steps,),
        in_specs=[
            whole((rows, depth), lambda j: (0, 0)),
            whole((rows, depth), lambda j: (0, 0)),
            pl.BlockSpec((depth, 3 * sub), lambda j: (0, j)),
        ]
        + ([anywhere, anywhere] if last else [])
        + ([anywhere] if n_tp else []),
        out_specs=[
            pl.BlockSpec((rows, sub), lambda j: (0, j)),
            pl.BlockSpec((rows, 2 * sub), lambda j: (0, j)),
            anywhere,
            anywhere,
        ]
        + ([anywhere] if n_tp else []),
        out_shape=[
            jax.ShapeDtypeStruct((rows, steps * sub), BF16),
            jax.ShapeDtypeStruct((rows, 2 * steps * sub), BF16),
            jax.ShapeDtypeStruct((rows, depth), BF16),
            jax.ShapeDtypeStruct((rows, depth), BF16),
        ]
        + ([jax.ShapeDtypeStruct((n_tp, rows // n_tp, depth), BF16)] if n_tp else []),
        scratch_shapes=[
            pltpu.VMEM((rows, depth), F32),
            pltpu.VMEM((rows, depth), F32),
            pltpu.VMEM((rows, depth), BF16),
            pltpu.VMEM((rows, depth), BF16),
            pltpu.SemaphoreType.DMA((2,)),
        ]
        + ([pltpu.SemaphoreType.DMA((n_tp,))] * 2 if n_tp else []),
        compiler_params=carrier_params(n_tp, 3),
        cost_estimate=hint(
            flops=12 * rows * depth * steps * sub,
            bytes_accessed=2 * weights.size + 8 * rows * depth,
            transcendentals=0,
        ),
        name="feed_forward",
    )(u, g, weights, *(sums if last else ()), *([carry] if n_tp else []))


def outer_kernel(n_tp, batches, sub, steps, *refs):
    u_refs, g_refs = refs[:batches], refs[batches : 2 * batches]
    hid_refs, dgu_refs = refs[2 * batches : 3 * batches], refs[3 * batches : 4 * batches]
    refs = refs[4 * batches :]
    move = None
    if n_tp:
        src, out_ref, got, send, recv = refs
        move = (src, got, send, recv)

        @pl.when(pl.program_id(0) == 0)
        def _():
            carry_start(n_tp, *move)

    else:
        (out_ref,) = refs
    for j in range(steps):
        both = slice(2 * j * sub, 2 * (j + 1) * sub)
        one = slice(j * sub, (j + 1) * sub)
        total = dot_tn(u_refs[0][...], dgu_refs[0][:, both])
        for m in range(1, batches):
            total += dot_tn(u_refs[m][...], dgu_refs[m][:, both])
        out_ref[0, :, 3 * j * sub : 3 * j * sub + 2 * sub] = total.astype(BF16)
        total = dot_tn(g_refs[0][...], hid_refs[0][:, one])
        for m in range(1, batches):
            total += dot_tn(g_refs[m][...], hid_refs[m][:, one])
        out_ref[0, :, 3 * j * sub + 2 * sub : 3 * (j + 1) * sub] = total.astype(BF16)
    if n_tp:

        @pl.when(pl.program_id(0) == pl.num_programs(0) - 1)
        def _():
            carry_end(n_tp, *move)


def outer_products(us, gs, hids, dgus, own, sub, n_tp=0, carry=None):
    batches = len(us)
    rows, depth = us[0].shape
    n_dp = depth // own
    width = hids[0].shape[1]
    steps = width // sub
    whole = functools.partial(pl.BlockSpec, pipeline_mode=pl.Buffered(1))
    column = pl.BlockSpec((rows, own), lambda i: (0, i))
    anywhere = pl.BlockSpec(memory_space=pl.ANY)
    return pl.pallas_call(
        functools.partial(outer_kernel, n_tp, batches, sub, steps),
        grid=(n_dp,),
        in_specs=[column] * (2 * batches)
        + [whole((rows, width), lambda i: (0, 0))] * batches
        + [whole((rows, 2 * width), lambda i: (0, 0))] * batches
        + ([anywhere] if n_tp else []),
        out_specs=[pl.BlockSpec((1, own, 3 * width), lambda i: (i, 0, 0))]
        + ([anywhere] if n_tp else []),
        out_shape=[jax.ShapeDtypeStruct((n_dp, own, 3 * width), BF16)]
        + ([jax.ShapeDtypeStruct((n_tp, rows // n_tp, depth), BF16)] if n_tp else []),
        scratch_shapes=[pltpu.SemaphoreType.DMA((n_tp,))] * 2 if n_tp else [],
        compiler_params=carrier_params(n_tp, 4),
        cost_estimate=hint(
            flops=6 * rows * batches * depth * width,
            bytes_accessed=6 * depth * width,
            transcendentals=0,
        ),
        name="outer_products",
    )(*us, *gs, *hids, *dgus, *([carry] if n_tp else []))


def attn_grad_kernel(a_ref, m_ref, qkv_ref, att_ref, out_qkv, out_output):
    out_qkv[0] = dot_tn(a_ref[...], qkv_ref[...]).astype(BF16)
    out_output[0] = dot_tn(m_ref[...], att_ref[...]).astype(BF16)


def attn_weight_grads(attn_in, d_mid, d_qkv, attended, own):
    rows, depth = attn_in.shape
    column = pl.BlockSpec((rows, own), lambda i: (0, i))
    whole = functools.partial(pl.BlockSpec, pipeline_mode=pl.Buffered(1))
    widths = (d_qkv.shape[1], attended.shape[1])
    return pl.pallas_call(
        attn_grad_kernel,
        grid=(depth // own,),
        in_specs=[column, column] + [whole((rows, w), lambda i: (0, 0)) for w in widths],
        out_specs=[pl.BlockSpec((1, own, w), lambda i: (i, 0, 0)) for w in widths],
        out_shape=[jax.ShapeDtypeStruct((depth // own, own, w), BF16) for w in widths],
        compiler_params=pltpu.CompilerParams(vmem_limit_bytes=VMEM_LIMIT),
        cost_estimate=hint(
            flops=2 * rows * depth * sum(widths), bytes_accessed=4 * rows * depth, transcendentals=0
        ),
        name="attn_weight_grads",
    )(attn_in, d_mid, d_qkv, attended)


def small_steps_kernel(qkv_ref, out_ref, gain_ref, *refs):
    states, results = refs[:12], refs[12:]
    q_width = states[0].shape[1]
    gradients = (
        lambda: qkv_ref[0, :, :q_width].astype(F32),
        lambda: qkv_ref[0, :, q_width:].astype(F32),
        lambda: out_ref[...].T,
        lambda: gain_ref[...],
    )
    for i, read in enumerate(gradients):
        gradient = read()
        mean_ref, square_ref, weight_ref = states[3 * i : 3 * i + 3]
        decay = weight_decay if i < 3 else 0.0
        moment, spread, change = adam_update(
            gradient, mean_ref[...], square_ref[...], weight_ref[...].astype(F32), decay
        )
        for ref, value in zip(results[4 * i : 4 * i + 4], (gradient, moment, spread, change)):
            ref[...] = value


def small_steps(qkv_grad, out_grad, gain_grad, *states):
    vmem = pl.BlockSpec(memory_space=pltpu.VMEM)
    shapes = [jax.ShapeDtypeStruct(states[3 * i].shape, F32) for i in range(4)]
    return tuple(
        pl.pallas_call(
            small_steps_kernel,
            in_specs=[vmem] * 15,
            out_specs=[vmem] * 16,
            out_shape=[shape for shape in shapes for _ in range(4)],
            compiler_params=pltpu.CompilerParams(vmem_limit_bytes=VMEM_LIMIT),
            name="small_steps",
        )(qkv_grad, out_grad, gain_grad, *states)
    )


def step_kernel(turned, decay, steps, chunks, *refs):
    grads = refs[:chunks]
    mean_ref, square_ref, weight_ref, grad_ref, moment_ref, spread_ref, update_ref = refs[chunks:]
    place = pl.program_id(1)
    for c in range(chunks):

        @pl.when(place // steps == c)
        def _(c=c):
            gradient = grads[c][...].astype(F32)
            if turned:
                gradient = gradient.T
            gradient = gradient.reshape(grad_ref.shape)
            moment, spread, change = adam_update(
                gradient, mean_ref[...], square_ref[...], weight_ref[...].astype(F32), decay
            )
            grad_ref[...] = gradient
            moment_ref[...] = moment
            spread_ref[...] = spread
            update_ref[...] = change


def step_from_chunks(grads, old_mean, square, weight, sub, offset, turned, decay):
    chunks, own = len(grads), grads[0].shape[0]
    steps = grads[0].shape[1] // (3 * sub)

    def grad_spec(c):
        def index(i, p):
            j = jnp.clip(p - c * steps, 0, steps - 1)
            return (0, 3 * j + i + offset)

        return pl.BlockSpec((own, sub), index)

    if turned:
        lead, spec = 1, pl.BlockSpec((sub, own), lambda i, p: (p, 0))
    else:
        lead, spec = old_mean.shape[0], pl.BlockSpec((1, own, sub), lambda i, p: (i, 0, p))
    return tuple(
        pl.pallas_call(
            functools.partial(step_kernel, turned, decay, steps, chunks),
            grid=(lead, chunks * steps),
            in_specs=[grad_spec(c) for c in range(chunks)] + [spec] * 3,
            out_specs=[spec] * 4,
            out_shape=[jax.ShapeDtypeStruct(old_mean.shape, F32)] * 4,
            compiler_params=pltpu.CompilerParams(vmem_limit_bytes=VMEM_LIMIT),
            cost_estimate=hint(
                flops=20 * old_mean.size, bytes_accessed=28 * old_mean.size, transcendentals=0
            ),
            name="weight_step",
        )(*grads, old_mean, square, weight)
    )


def finish_kernel(
    n_dp,
    n_tp,
    tok_low,
    share_ref,
    gain_ref,
    tok_rows,
    grad_ref,
    gain_own,
    met,
    z_send,
    z_got,
    ranks_got,
    gain_sum,
    gain_got,
    local_sem,
    tok_s,
    tok_r,
    core_s,
    core_r,
    z_s,
    z_r,
    rank_s,
    rank_r,
    gain_s,
    gain_r,
):
    line = n_dp // 2
    own = share_ref.shape[1]
    dp, tp = lax.axis_index("dp"), lax.axis_index("tp")
    place, core = dp // 2, dp % 2

    def rank(k):
        return (dp, paired(tp, k))

    def columns(index):
        return pl.ds(pl.multiple_of(index * own, own), own)

    first, relay = row_moves(remote, rank, n_tp, tok_low, tok_rows, tok_s, tok_r)
    keep = [
        pltpu.make_async_copy(tok_low.at[m], tok_rows.at[m, 0], local_sem.at[m])
        for m in range(MICRO)
    ]
    core_moves = [
        remote(
            share_ref.at[z * 2 + 1 - core],
            met.at[z],
            core_s.at[z],
            core_r.at[z],
            (place * 2 + 1 - core, tp),
        )
        for z in range(line)
    ]
    z_moves = [
        remote(
            z_send.at[k], z_got.at[k], z_s.at[k], z_r.at[k], (paired(place, k) * 2 + core, tp)
        )
        for k in range(1, line)
    ]
    rank_moves = [
        remote(gain_ref, ranks_got.at[k], rank_s.at[k], rank_r.at[k], rank(k))
        for k in range(1, n_tp)
    ]
    gain_moves = [
        remote(
            gain_sum.at[:, columns(paired(dp, j))],
            gain_got.at[j],
            gain_s.at[j],
            gain_r.at[j],
            (paired(dp, j), tp),
        )
        for j in range(1, n_dp)
    ]

    meet([rank(k) for k in range(1, n_tp)] + [(paired(dp, j), tp) for j in range(1, n_dp)])
    start(core_moves)
    start(rank_moves)
    for moves in first:
        start(moves)
    start(keep)
    arrive(core_moves)
    for k in range(1, line):
        there = paired(place, k)
        total = share_ref[there * 2 + core].astype(F32) + met[there].astype(F32)
        z_send[k] = total.astype(BF16)
    start(z_moves)
    arrive(rank_moves)
    total = gain_ref[...]
    for k in range(1, n_tp):
        total = total + ranks_got[k]
    gain_sum[...] = total
    start(gain_moves)
    relay_rows(first, relay)
    arrive(gain_moves)
    total = gain_sum[:, columns(dp)]
    for j in range(1, n_dp):
        total = total + gain_got[j]
    gain_own[...] = total
    arrive(z_moves)
    total = share_ref[dp].astype(F32) + met[place].astype(F32)
    for k in range(1, line):
        total = total + z_got[k].astype(F32)
    grad_ref[...] = total
    close_rows(first, relay)
    for moves in (core_moves, z_moves, rank_moves, gain_moves):
        sent(moves)
    for copy in keep:
        copy.wait()


def finish(n_dp, n_tp, tok_low, shares, gain_part):
    micro, rows, depth = tok_low.shape
    _, own, width = shares.shape
    line = n_dp // 2
    anywhere = pl.BlockSpec(memory_space=pl.ANY)
    vmem = pl.BlockSpec(memory_space=pltpu.VMEM)
    dma = pltpu.SemaphoreType.DMA
    return pl.pallas_call(
        functools.partial(finish_kernel, n_dp, n_tp),
        in_specs=[anywhere, vmem, vmem],
        out_specs=[anywhere, vmem, vmem],
        out_shape=[
            jax.ShapeDtypeStruct((micro, n_tp, rows, depth), BF16),
            jax.ShapeDtypeStruct((own, width), F32),
            jax.ShapeDtypeStruct((2, own), F32),
        ],
        scratch_shapes=[
            pltpu.VMEM((line, own, width), BF16),
            pltpu.VMEM((line, own, width), BF16),
            pltpu.VMEM((line, own, width), BF16),
            pltpu.VMEM((n_tp, 2, depth), F32),
            pltpu.VMEM((2, depth), F32),
            pltpu.VMEM((n_dp, 2, own), F32),
            dma((micro,)),
            dma((micro, n_tp)),
            dma((micro, n_tp)),
            dma((line,)),
            dma((line,)),
            dma((line,)),
            dma((line,)),
            dma((n_tp,)),
            dma((n_tp,)),
            dma((n_dp,)),
            dma((n_dp,)),
        ],
        compiler_params=pltpu.CompilerParams(
            collective_id=1, has_side_effects=True, vmem_limit_bytes=VMEM_LIMIT
        ),
        cost_estimate=hint(flops=10**10, bytes_accessed=10**8, transcendentals=0),
        name="finish",
    )(tok_low, shares, gain_part)


def tail_kernel(n_dp, n_tp, group, *refs):
    (
        du_refs,
        y_refs,
        du_ins,
        seed_ref,
        middle_ref,
        x_ref,
        gains_ref,
        out_refs,
        qkv_refs,
        q_ref,
        kv_ref,
        qpos_ref,
        kpos_ref,
        cos_ref,
        sin_ref,
        d_qkv_ref,
        mid_rows,
        out_rows,
        tok_low,
        gain_ref,
    ) = (refs[0:2], refs[2:4], refs[4:6]) + refs[6:10] + (refs[10:12], refs[12:14]) + refs[14:25]
    (
        weights,
        du_got,
        y_got,
        own_mid,
        mid_low,
        block_low,
        do_send,
        do_got,
        shares,
        met,
        z_send,
        z_got,
        heads_got,
        local_sem,
        block_s,
        block_r,
        y_s,
        y_r,
        mid_s,
        mid_r,
        do_s,
        do_r,
        core_s,
        core_r,
        z_s,
        z_r,
        heads_s,
        heads_r,
    ) = refs[25:]
    line = n_dp // 2
    batches = range(MICRO)
    others = range(1, n_tp)
    dp, tp = lax.axis_index("dp"), lax.axis_index("tp")
    place, core = dp // 2, dp % 2
    depth = middle_ref.shape[1]
    rows = mid_low.shape[1]
    seq_rows = q_ref.shape[2]
    q_width = q_ref.shape[3]
    kv_width = kv_ref.shape[4]
    width = q_width + kv_width
    half = depth // 2

    def rank(k):
        return (dp, paired(tp, k))

    def spot(k):
        return (paired(place, k) * 2 + core, tp)

    other_core = (place * 2 + 1 - core, tp)

    def block(k):
        return pl.ds(k * rows, rows)

    y_moves = [
        [
            remote(y_refs[m].at[block(k)], y_got.at[m, k], y_s.at[m, k], y_r.at[m, k], rank(k))
            for k in others
        ]
        for m in batches
    ]

    block_first, block_relay = row_moves(
        remote, rank, n_tp, block_low, out_rows, block_s, block_r
    )
    mid_first, mid_relay = row_moves(remote, rank, n_tp, mid_low, mid_rows, mid_s, mid_r)
    do_moves = [
        [
            remote(
                do_send.at[m, k], do_got.at[m, block(k)], do_s.at[m, k], do_r.at[m, k], rank(k)
            )
            for k in others
        ]
        for m in batches
    ]
    core_moves = [
        remote(shares.at[m, 1 - core], met.at[m], core_s.at[m], core_r.at[m], other_core)
        for m in batches
    ]
    z_moves = [
        [
            remote(z_send.at[m, k], z_got.at[m, k], z_s.at[m, k], z_r.at[m, k], spot(k))
            for k in range(1, line)
        ]
        for m in batches
    ]
    heads_moves = [
        [
            remote(
                d_qkv_ref.at[m, block(k)],
                heads_got.at[m, k],
                heads_s.at[m, k],
                heads_r.at[m, k],
                rank(k),
            )
            for k in others
        ]
        for m in batches
    ]

    own_copies = [
        pltpu.make_async_copy(ref.at[pl.ds(0, rows)], got.at[m, 0], local_sem.at[i, m])
        for i, (pair, got) in enumerate(((du_refs, du_got), (y_refs, y_got)))
        for m, ref in enumerate(pair)
    ]
    own_copies += [
        pltpu.make_async_copy(
            ref.at[pl.ds(1, n_tp - 1)], du_got.at[m, pl.ds(1, n_tp - 1)], local_sem.at[4, m]
        )
        for m, ref in enumerate(du_ins)
    ]
    keep_block = [
        pltpu.make_async_copy(block_low.at[m], out_rows.at[m, 0], local_sem.at[5, m])
        for m in batches
    ]
    load_out = [
        pltpu.make_async_copy(
            ref, weights.at[side, :, pl.ds(0, n_tp * q_width)], local_sem.at[6, side]
        )
        for side, ref in enumerate(out_refs)
    ]
    load_qkv = [
        pltpu.make_async_copy(ref, weights.at[side], local_sem.at[2, side])
        for side, ref in enumerate(qkv_refs)
    ]
    keep = [
        pltpu.make_async_copy(mid_low.at[m], mid_rows.at[m, 0], local_sem.at[3, m])
        for m in batches
    ]

    meet([rank(k) for k in others] + [other_core] + [spot(k) for k in range(1, line)])
    start(own_copies)
    start(load_out)
    gain_one = gains_ref[0:1, :].astype(F32)
    gain_two = gains_ref[1:2, :].astype(F32)
    gain_ref[...] = jnp.zeros_like(gain_ref)

    def total_of(got, m):
        total = got[m, 0].astype(F32)
        for k in others:
            total = total + got[m, k].astype(F32)
        return total

    for copy in own_copies:
        copy.wait()
    for m in batches:
        part = slice(m * rows, (m + 1) * rows)
        d_mixed = total_of(du_got, m)
        middle = middle_ref[part, :]
        scale = mean_square_scale(middle)
        normed = middle * scale
        gain_ref[1:2, :] += jnp.sum(d_mixed * normed, axis=0, keepdims=True)
        d_middle = seed_ref[part, :].astype(F32) + norm_back(d_mixed * gain_two, normed, scale)
        own_mid[m] = d_middle
        mid_low[m] = d_middle.astype(BF16)
        if m == 0:
            for copy in load_out:
                copy.wait()
        near_cols = pl.ds(pl.multiple_of(core * half, half), half)
        far_cols = pl.ds(pl.multiple_of((1 - core) * half, half), half)
        near, far = mid_low[m, :, near_cols], mid_low[m, :, far_cols]
        for k in range(n_tp):
            lanes = slice(k * q_width, (k + 1) * q_width)
            rows_out = (dot(near, weights[0, :, lanes]) + dot(far, weights[1, :, lanes])).astype(
                BF16
            )
            if k == 0:
                do_got[m, 0:rows, :] = rows_out
            else:
                do_send[m, k] = rows_out
        start(do_moves[m])
    start(load_qkv)
    for m in batches:
        start(mid_first[m])
        keep[m].start()
    for m in batches:
        start(y_moves[m])

    def attend_back_seq(m, s):
        seq = pl.ds(s * seq_rows, seq_rows)
        for h in range(kv_width // (2 * HD)):
            pair = slice(h * 2 * HD, (h + 1) * 2 * HD)
            keyvals = kv_ref[:, m, s, :, pair].reshape(-1, 2 * HD)
            grads = None
            for part in range(group // 2):
                lanes = slice((h * group + 2 * part) * HD, (h * group + 2 * part + 2) * HD)
                q_pad = stack_heads(q_ref[m, s, :, lanes], 2, False)
                do_pad = stack_heads(do_got[m, seq, lanes], 2, True)
                probs = scores_and_probs(q_pad, keyvals, qpos_ref[...], kpos_ref[...], 2)
                d_probs = dot_nt(do_pad, keyvals)
                d_scores = probs * (d_probs - jnp.sum(d_probs * probs, axis=-1, keepdims=True))
                ds_low = d_scores.astype(BF16) * HD ** (-0.5)
                dq = unstack_heads(dot(ds_low, keyvals), 2, False)
                cos_q, sin_q = cos_ref[:, 0 : 2 * HD], sin_ref[:, 0 : 2 * HD]
                dq = dq * cos_q + half_turn(dq * sin_q)
                d_qkv_ref[m, seq, lanes] = dq.astype(BF16)
                term = dot_tn(ds_low, q_pad) + dot_tn(probs.astype(BF16), do_pad)
                grads = term if grads is None else grads + term
            grads = grads.astype(BF16)
            for i in range(n_dp):
                shares[m, i % 2, i // 2, seq, pair] = grads[i * seq_rows : (i + 1) * seq_rows]

    def attend_back_range(m, low, high):
        @pl.loop(low, high)
        def _(s):
            attend_back_seq(m, s)

    def send_along(m):
        arrive([core_moves[m]])
        for k in range(1, line):
            there = paired(place, k)
            z_send[m, k] = (
                shares[m, core, there].astype(F32) + met[m, there].astype(F32)
            ).astype(BF16)
        start(z_moves[m])

    def close_keys(m):
        arrive(z_moves[m])
        total = shares[m, core, place].astype(F32) + met[m, place].astype(F32)
        for k in range(1, line):
            total = total + z_got[m, k].astype(F32)
        cos_k, sin_k = cos_ref[:, q_width:], sin_ref[:, q_width:]
        for s in range(SEQS):
            seq = slice(s * seq_rows, (s + 1) * seq_rows)
            grad = total[seq]
            d_qkv_ref[m, seq, q_width:] = (grad * cos_k + half_turn(grad * sin_k)).astype(BF16)
        start(heads_moves[m])

    def close_block(m):
        arrive(y_moves[m])
        part = slice(m * rows, (m + 1) * rows)
        block_low[m] = (middle_ref[part, :] + total_of(y_got, m)).astype(BF16)
        start(block_first[m])
        keep_block[m].start()

    def close_tokens(m):
        arrive(heads_moves[m])
        part = slice(m * rows, (m + 1) * rows)
        heads = [d_qkv_ref[m, 0:rows, :]] + [heads_got[m, k] for k in others]
        sides = []
        for side in range(2):
            total = dot_nt(heads[0], weights[side, :, 0:width])
            for k in others:
                total = total + dot_nt(heads[k], weights[side, :, k * width : (k + 1) * width])
            sides.append(total)
        d_act = jnp.where(
            core == 0,
            jnp.concatenate(sides, axis=1),
            jnp.concatenate(sides[::-1], axis=1),
        )
        x_part = x_ref[part, :].astype(F32)
        scale = mean_square_scale(x_part)
        normed = x_part * scale
        gain_ref[0:1, :] += jnp.sum(d_act * normed, axis=0, keepdims=True)
        tok_low[m] = (own_mid[m] + norm_back(d_act * gain_one, normed, scale)).astype(BF16)

    arrive(do_moves[0])
    attend_back_range(0, 0, SEQS)
    core_moves[0].start()
    arrive(do_moves[1])
    attend_back_range(1, 0, SEQS // 2)
    send_along(0)
    relay_rows(mid_first, mid_relay)
    attend_back_range(1, SEQS // 2, SEQS)
    core_moves[1].start()
    for copy in load_qkv:
        copy.wait()
    close_block(0)
    close_keys(0)
    send_along(1)
    close_block(1)
    close_tokens(0)
    close_keys(1)
    relay_rows(block_first, block_relay)
    close_tokens(1)
    close_rows(mid_first, mid_relay)
    close_rows(block_first, block_relay)
    for m in batches:
        for moves in (y_moves[m], do_moves[m], [core_moves[m]], z_moves[m], heads_moves[m]):
            sent(moves)
        keep[m].wait()
        keep_block[m].wait()


def tail(
    n_dp, n_tp, group, sums, arrived, seed, middle, x, gains, out_w, qkv_w, q, kv, qpos, kpos, cos, sin
):
    own_rows, depth = middle.shape
    rows = own_rows // MICRO
    batch_rows = n_tp * rows
    line = n_dp // 2
    q_width, kv_width = q.shape[3], kv.shape[4]
    width = q_width + kv_width
    anywhere = pl.BlockSpec(memory_space=pl.ANY)
    vmem = pl.BlockSpec(memory_space=pltpu.VMEM)
    dma = pltpu.SemaphoreType.DMA
    gathered = jax.ShapeDtypeStruct((MICRO, n_tp, rows, depth), BF16)
    return pl.pallas_call(
        functools.partial(tail_kernel, n_dp, n_tp, group),
        in_specs=[anywhere] * 6 + [vmem] * 4 + [anywhere] * 4 + [vmem] * 6,
        out_specs=[vmem, anywhere, anywhere, vmem, vmem],
        out_shape=[
            jax.ShapeDtypeStruct((MICRO, batch_rows, width), BF16),
            gathered,
            gathered,
            jax.ShapeDtypeStruct((MICRO, rows, depth), BF16),
            jax.ShapeDtypeStruct((2, depth), F32),
        ],
        scratch_shapes=[
            pltpu.VMEM((2, depth // 2, n_tp * width), BF16),
            pltpu.VMEM((MICRO, n_tp, rows, depth), BF16),
            pltpu.VMEM((MICRO, n_tp, rows, depth), BF16),
            pltpu.VMEM((MICRO, rows, depth), F32),
            pltpu.VMEM((MICRO, rows, depth), BF16),
            pltpu.VMEM((MICRO, rows, depth), BF16),
            pltpu.VMEM((MICRO, n_tp, rows, q_width), BF16),
            pltpu.VMEM((MICRO, batch_rows, q_width), BF16),
            pltpu.VMEM((MICRO, 2, line, batch_rows, kv_width), BF16),
            pltpu.VMEM((MICRO, line, batch_rows, kv_width), BF16),
            pltpu.VMEM((MICRO, line, batch_rows, kv_width), BF16),
            pltpu.VMEM((MICRO, line, batch_rows, kv_width), BF16),
            pltpu.VMEM((MICRO, n_tp, rows, width), BF16),
            dma((7, 2)),
        ]
        + [dma((MICRO, n_tp))] * 8
        + [dma((MICRO,))] * 2
        + [dma((MICRO, line))] * 2
        + [dma((MICRO, n_tp))] * 2,
        compiler_params=pltpu.CompilerParams(
            collective_id=0, has_side_effects=True, vmem_limit_bytes=VMEM_LIMIT
        ),
        cost_estimate=hint(
            flops=10**10,
            bytes_accessed=10**8,
            transcendentals=0,
        ),
        name="tail",
    )(
        sums[0][1],
        sums[1][1],
        sums[0][0],
        sums[1][0],
        *arrived,
        seed,
        middle,
        x,
        gains,
        *out_w,
        *qkv_w,
        q,
        kv,
        qpos,
        kpos,
        cos,
        sin,
    )


def spread_kernel(rank_ref, out_ref, tok_ref, block_ref, grad_ref):
    block_ref[...] = out_ref[...]
    grad_ref[...] = tok_ref[...].astype(F32)


def spread(rank, out_rows, tok_rows):
    micro, n_tp, rows, depth = out_rows.shape
    here = pl.BlockSpec((1, 1, rows, depth), lambda m, k, r: (m, k, 0, 0))
    there = pl.BlockSpec((1, 1, rows, depth), lambda m, k, r: (m, r[0] ^ k, 0, 0))
    return pl.pallas_call(
        spread_kernel,
        grid_spec=pltpu.PrefetchScalarGridSpec(
            num_scalar_prefetch=1,
            grid=(micro, n_tp),
            in_specs=[here, here],
            out_specs=[there, there],
        ),
        out_shape=[
            jax.ShapeDtypeStruct(out_rows.shape, BF16),
            jax.ShapeDtypeStruct(out_rows.shape, F32),
        ],
        compiler_params=pltpu.CompilerParams(vmem_limit_bytes=VMEM_LIMIT),
        name="spread",
    )(rank, out_rows, tok_rows)


def per_device(
    n_dp,
    n_tp,
    tokens,
    cotangent,
    span_order,
    w_query,
    w_keyval,
    w_output,
    w_gateup,
    w_down,
    norm_gains,
    mean_query,
    square_query,
    mean_keyval,
    square_keyval,
    mean_output,
    square_output,
    mean_gateup,
    square_gateup,
    mean_down,
    square_down,
    mean_gains,
    square_gains,
):
    depth = tokens.shape[1]
    span_rows = 2 * CH
    block_rows = SEQS * span_rows // n_tp
    parts = span_rows // min(span_rows, block_rows)
    q_width = w_query.shape[1]
    kv_width = w_keyval.shape[1]
    hidden_width = w_down.shape[0]
    own_depth = w_query.shape[0]
    group = q_width // HD // (kv_width // (2 * HD))
    device = lax.axis_index("dp")
    rank = lax.axis_index("tp")
    line = n_dp // 2
    place, core = device // 2, device % 2

    def swap(value, k):
        return lax.ppermute(value, "tp", [(i, i ^ k) for i in range(n_tp)])

    def reorder(value):
        return jnp.concatenate(
            [lax.dynamic_slice_in_dim(value, rank ^ k, 1, axis=1) for k in range(n_tp)], axis=1
        )

    def gather_blocks(own):
        half = own.shape[0] // 2
        got = [own, swap(own, 1), swap(own, 2)]
        got.append(jnp.concatenate([swap(got[1][:half], 2), swap(got[2][half:], 1)], axis=0))
        return got + [swap(own, k) for k in range(4, n_tp)]

    def exchange(blocks):
        return [blocks[0]] + [swap(blocks[k], k) for k in range(1, n_tp)]

    def total_of(parts):
        total = parts[0].astype(F32)
        for part in parts[1:]:
            total = total + part.astype(F32)
        return total

    def gather_pair(owns):
        got = [owns, [swap(own, 1) for own in owns], [swap(own, 2) for own in owns]]
        got.append([swap(got[1][0], 2)] + [swap(own, 1) for own in got[2][1:]])
        return got + [[swap(own, k) for own in owns] for k in range(4, n_tp)]

    def scatter_pair(blocks):
        first = swap(blocks[0][3], 1)
        seconds = [swap(blocks[m][3], 2) for m in range(1, MICRO)]
        to_two = total_of([blocks[0][2], first]).astype(BF16)
        to_one = [total_of([blocks[m][1], seconds[m - 1]]).astype(BF16) for m in range(1, MICRO)]
        yield [to_two] + to_one
        totals = []
        for m in range(MICRO):
            one = blocks[m][1] if m == 0 else to_one[m - 1]
            two = to_two if m == 0 else blocks[m][2]
            far = [swap(blocks[m][k], k) for k in range(4, n_tp)]
            totals.append(total_of([blocks[m][0], swap(one, 1), swap(two, 2)] + far))
        yield totals

    def line_sum(other, own):
        met = lax.ppermute(other, "dp", [(i, i ^ 1) for i in range(n_dp)])
        yield [met]

        def share(index):
            index = jnp.clip(index, 0, line - 1)
            return lax.dynamic_index_in_dim(own, index, 0, False).astype(
                F32
            ) + lax.dynamic_index_in_dim(met, index, 0, False).astype(F32)

        sends = []
        for far in range(1, line):
            for way in (far, -far):
                sends.append((way, share(place + way).astype(BF16)))
        yield [value for _, value in sends]
        total = share(place)
        for far in range(1, line):
            arrived = []
            for way, value in sends:
                if abs(way) == far:
                    pairs = [
                        (i, i + 2 * way) for i in range(n_dp) if 0 <= i + 2 * way < n_dp
                    ]
                    arrived.append(lax.ppermute(value, "dp", pairs))
            if far <= 3:
                yield arrived
            for value in arrived:
                total = total + value.astype(F32)
        yield [total]

    def my_half(value):
        return lax.dynamic_slice_in_dim(value, core * (depth // 2), depth // 2, axis=0)

    def swap_cores(value):
        return lax.ppermute(value, "dp", [(i, i ^ 1) for i in range(n_dp)])

    def both_halves(near, far):
        return jnp.where(
            core == 0,
            jnp.concatenate([near, far], axis=1),
            jnp.concatenate([far, near], axis=1),
        )

    def after(value, *earlier):
        return lax.optimization_barrier((value,) + earlier)[0]

    qkv_full = lax.all_gather(
        jnp.concatenate([w_query, w_keyval], axis=1), "dp", axis=0, tiled=True
    )
    gains_full = lax.all_gather(norm_gains, "dp", axis=1, tiled=True)
    out_t_full = lax.all_gather(w_output.T, "dp", axis=0, tiled=True)

    offsets = jnp.arange(CH, dtype=jnp.int32)
    all_pos = (span_order[:, None] * CH + offsets[None, :]).reshape(n_dp, parts, -1)
    all_pos = jnp.stack([all_pos[:, (rank % parts) ^ p] for p in range(parts)], axis=1)
    own_pos = lax.dynamic_slice_in_dim(all_pos, device, 1).reshape(-1)
    all_pos = all_pos.reshape(-1)
    qpos, kpos = own_pos[:, None], all_pos[None, :]
    kv_kinds = [True, False] * (kv_width // (2 * HD))
    cos_t, sin_t = lane_tables(own_pos, [True] * (q_width // HD) + kv_kinds)

    x = reorder(tokens.reshape(MICRO, n_tp, block_rows, depth))
    seed = reorder(cotangent.reshape(MICRO, n_tp, block_rows, depth))
    batch_rows = SEQS * span_rows
    rows = MICRO * batch_rows
    gain_one, gain_two = gains_full[0:1], gains_full[1:2]
    attn_in, qkv = project(x.reshape(rows, depth), gain_one, qkv_full, cos_t, sin_t)
    qkv = qkv.reshape(MICRO, SEQS, span_rows, q_width + kv_width)
    q, kv = qkv[..., :q_width], qkv[..., q_width:]
    kv_all = lax.all_gather(kv, "dp", axis=0, tiled=False)

    sub = min(SUB, hidden_width // CHUNKS)
    chunk = hidden_width // CHUNKS
    w_down_t = w_down.T
    mlp_full = []
    for c in range(CHUNKS):
        pieces = []
        for start in range(c * chunk, (c + 1) * chunk, sub):
            cols = slice(start, start + sub)
            pieces += [w_gateup[0][:, cols], w_gateup[1][:, cols], w_down_t[:, cols]]
        shard = jnp.concatenate(pieces, axis=1)
        mlp_full.append(lax.all_gather(shard, "dp", axis=0, tiled=True))

    attended = attend(qpos, kpos, q, kv_all, group)
    attended_blocks = attended.reshape(MICRO, n_tp, block_rows, q_width)
    out_near = my_half(out_t_full)
    out_near = jnp.concatenate([out_near] + [swap(out_near, k) for k in range(1, n_tp)], axis=1)
    out_far = swap_cores(out_near)
    heads_in = exchange([attended_blocks[:, k] for k in range(n_tp)])
    own_rows = MICRO * block_rows
    x_own = x[:, 0].reshape(own_rows, depth).astype(F32)
    heads_cat = jnp.concatenate([v.reshape(own_rows, q_width) for v in heads_in], axis=1)
    middle = x_own + both_halves(dot_nt(heads_cat, out_near), dot_nt(heads_cat, out_far))
    scale_two = mean_square_scale(middle)
    normed_two = middle * scale_two
    u_own = (normed_two * gain_two.astype(F32)).astype(BF16)
    batches = range(MICRO)
    gathered = [g.reshape(MICRO, block_rows, depth) for g in gather_blocks(u_own)]
    u = [jnp.concatenate([gathered[k][m] for k in range(n_tp)], axis=0) for m in batches]
    g = [seed[m].reshape(batch_rows, depth) for m in batches]

    qkv_half = after(my_half(qkv_full), u[0])
    quarter = depth // 4
    qkv_width = q_width + kv_width
    qkv_near = jnp.zeros((depth // 2, n_tp * qkv_width), BF16)
    qkv_near = lax.dynamic_update_slice(qkv_near, qkv_half, (0, 0))
    qkv_moves = [(k, i) for i in range(2) for k in range(1, min(n_tp, 3))]
    qkv_moves = [qkv_moves[:2], qkv_moves[2:]] + [
        [(k, i) for k in range(3, n_tp)] for i in range(2)
    ]

    def move_qkv(buffer):
        for k, i in qkv_moves.pop(0) if qkv_moves else []:
            got = swap(qkv_half[i * quarter : (i + 1) * quarter], k)
            buffer = lax.dynamic_update_slice(buffer, got, (i * quarter, k * qkv_width))
        return buffer

    def blocks_of(value):
        return [value[k * block_rows : (k + 1) * block_rows] for k in range(n_tp)]

    def own_part(value, m):
        return value[m * block_rows : (m + 1) * block_rows]

    core_index = core.astype(jnp.int32).reshape(1)
    gain_two_f = gain_two.astype(F32)
    gain_one_f = gain_one.astype(F32)
    cos_q, sin_q = cos_t[:, : group * HD], sin_t[:, : group * HD]
    cos_k, sin_k = cos_t[:, q_width:], sin_t[:, q_width:]
    gain_grads = [0.0, 0.0]
    sums = [None] * MICRO

    arrived = []

    def expand(c, m, *earlier):
        carry = (n_tp, sums[m - 1][1]) if c == CHUNKS - 1 and m else ()
        hid, dgu, y_low, du_low, *got = feed_forward(
            after(u[m], *earlier), g[m], mlp_full[c], sub, sums[m], *carry
        )
        sums[m] = (y_low, du_low)
        arrived.extend(got)
        return hid, dgu

    def close(hids, dgus, last, *earlier):
        carry = (n_tp, sums[-1][1]) if last else ()
        grads, *got = outer_products(
            [after(u[0], *earlier)] + u[1:], g, hids, dgus, own_depth, sub, *carry
        )
        arrived.extend(got)
        return grads, lax.psum_scatter(grads, "dp", scatter_dimension=0, tiled=False)

    chunk_grads = []
    earlier = []
    for c in range(CHUNKS - 1):
        hids, dgus = [], []
        for m in batches:
            hid, dgu = expand(c, m, *earlier)
            qkv_near = move_qkv(qkv_near)
            earlier = [hid, qkv_near]
            hids.append(hid)
            dgus.append(dgu)
        grads, owned = close(hids, dgus, False, *earlier)
        qkv_near = move_qkv(qkv_near)
        earlier = [grads, qkv_near]
        chunk_grads.append(owned)

    d_middles, d_mid_lows, d_attends, all_rows = [], [], [], []
    hids, dgus = [], []
    for m in batches:
        hid, dgu = expand(CHUNKS - 1, m, *earlier)
        qkv_near = move_qkv(qkv_near)
        earlier = [hid, qkv_near]
        if m == 0:
            qkv_far = swap_cores(qkv_near)
        hids.append(hid)
        dgus.append(dgu)
    grads, owned = close(hids, dgus, True, *earlier, qkv_far)
    chunk_grads.append(owned)
    tail_sums = [after(sums[0], grads)] + sums[1:]
    d_qkv, mid_rows, out_rows, tok_low, gain_part = tail(
        n_dp,
        n_tp,
        group,
        tail_sums,
        arrived,
        seed[:, 0].reshape(own_rows, depth),
        middle,
        x[:, 0].reshape(own_rows, depth),
        gains_full,
        (out_near, out_far),
        (qkv_near, qkv_far),
        q,
        kv_all,
        qpos,
        kpos,
        cos_t,
        sin_t,
    )
    mlp_grads = [v.reshape(own_depth, -1) for v in chunk_grads]
    qkv_shares, out_shares = attn_weight_grads(
        attn_in,
        mid_rows.reshape(rows, depth),
        d_qkv.reshape(rows, q_width + kv_width),
        attended.reshape(rows, q_width),
        own_depth,
    )
    tok_rows, out_grad, gain_grad = finish(n_dp, n_tp, tok_low, out_shares, gain_part)
    qkv_shares = after(qkv_shares, out_grad, *chunk_grads)
    qkv_grad = lax.psum_scatter(qkv_shares, "dp", scatter_dimension=0, tiled=False)
    block_output, grad_tokens = spread(rank.astype(jnp.int32).reshape(1), out_rows, tok_rows)
    block_output = block_output.reshape(rows, depth)
    grad_tokens = grad_tokens.reshape(rows, depth)
    small = small_steps(
        qkv_grad.reshape(1, own_depth, q_width + kv_width),
        out_grad,
        gain_grad,
        mean_query,
        square_query,
        w_query,
        mean_keyval,
        square_keyval,
        w_keyval,
        mean_output,
        square_output,
        w_output,
        mean_gains,
        square_gains,
        norm_gains,
    )
    return (
        (block_output, grad_tokens)
        + small[:12]
        + step_from_chunks(
            mlp_grads, mean_gateup, square_gateup, w_gateup, sub, 0, False, weight_decay
        )
        + step_from_chunks(mlp_grads, mean_down, square_down, w_down, sub, 2, True, weight_decay)
        + small[12:]
    )


def solution(mesh):
    rows_first = P("dp", "tp")
    cols_last = P("tp", "dp")
    stacked = P(None, "dp", "tp")
    gains = P(None, "dp")
    token_rows = P("dp", None)
    placed = (
        (token_rows, token_rows, P())
        + (rows_first, rows_first, cols_last, stacked, cols_last, gains)
        + (rows_first,) * 4
        + (cols_last,) * 2
        + (stacked,) * 2
        + (cols_last,) * 2
        + (gains,) * 2
    )
    results = (
        (token_rows, token_rows)
        + (rows_first,) * 8
        + (cols_last,) * 4
        + (stacked,) * 4
        + (cols_last,) * 4
        + (gains,) * 4
    )
    return jax.shard_map(
        functools.partial(per_device, mesh.shape["dp"], mesh.shape["tp"]),
        mesh=mesh,
        in_specs=placed,
        out_specs=results,
        check_vma=False,
    )
```

```python
import functools

import jax
import jax.numpy as jnp
from jax import lax
from jax.experimental import pallas as pl
from jax.experimental.pallas import tpu as pltpu
from jax.sharding import PartitionSpec as P

HD = 64
CH = 64
SEQS = 4
MICRO = 2
STEP = 5
CHUNKS = 2
SUB = 512

norm_eps = 1e-05
rope_base = 500000.0
beta_one = 0.9
beta_two = 0.95
learn_rate = 0.01
weight_decay = 0.1
adam_eps = 1e-08
masked_score = -1e30

F32 = jnp.float32
BF16 = jnp.bfloat16
VMEM_LIMIT = 60 * 1024 * 1024
HINT = 20


def hint(flops, bytes_accessed, transcendentals):
    return pl.CostEstimate(
        flops=flops // HINT, bytes_accessed=bytes_accessed // HINT, transcendentals=transcendentals
    )


def lane_tables(positions, kinds):
    half_size = HD // 2
    frequencies = rope_base ** (-(jnp.arange(half_size, dtype=F32) * 2.0 / HD))
    angles = positions.astype(F32)[:, None] * frequencies[None, :]
    cos_half, sin_half = jnp.cos(angles), jnp.sin(angles)
    cos_head = jnp.concatenate([cos_half, cos_half], axis=-1)
    sin_head = jnp.concatenate([-sin_half, sin_half], axis=-1)
    ones, zeros = jnp.ones_like(cos_head), jnp.zeros_like(cos_head)
    cos_all, sin_all = [], []
    for kind in kinds:
        cos_all.append(cos_head if kind else ones)
        sin_all.append(sin_head if kind else zeros)
    return jnp.concatenate(cos_all, axis=-1), jnp.concatenate(sin_all, axis=-1)


def half_turn(values):
    width = values.shape[-1]
    axis = values.ndim - 1
    lane = lax.broadcasted_iota(jnp.int32, values.shape, axis)
    ahead = pltpu.roll(values, width - HD // 2, axis)
    behind = pltpu.roll(values, HD // 2, axis)
    return jnp.where(lane % HD < HD // 2, ahead, behind)


def mean_square_scale(values):
    return lax.rsqrt(jnp.mean(values * values, axis=-1, keepdims=True) + norm_eps)


def project_kernel(x_ref, gain_ref, w_ref, cos_ref, sin_ref, a_ref, qkv_ref):
    x = x_ref[...].astype(F32)
    a = (x * mean_square_scale(x) * gain_ref[...].astype(F32)).astype(BF16)
    a_ref[...] = a
    t = jnp.dot(a, w_ref[...], preferred_element_type=F32)
    qkv_ref[...] = (t * cos_ref[...] + half_turn(t) * sin_ref[...]).astype(BF16)


def project(x, gain, weight, cos_t, sin_t):
    rows, depth = x.shape
    width = weight.shape[1]
    block = cos_t.shape[0]
    return pl.pallas_call(
        project_kernel,
        grid=(rows // block,),
        in_specs=[
            pl.BlockSpec((block, depth), lambda i: (i, 0)),
            pl.BlockSpec((1, depth), lambda i: (0, 0)),
            pl.BlockSpec((depth, width), lambda i: (0, 0)),
            pl.BlockSpec((block, width), lambda i: (0, 0)),
            pl.BlockSpec((block, width), lambda i: (0, 0)),
        ],
        out_specs=[
            pl.BlockSpec((block, depth), lambda i: (i, 0)),
            pl.BlockSpec((block, width), lambda i: (i, 0)),
        ],
        out_shape=[
            jax.ShapeDtypeStruct((rows, depth), BF16),
            jax.ShapeDtypeStruct((rows, width), BF16),
        ],
        compiler_params=pltpu.CompilerParams(vmem_limit_bytes=VMEM_LIMIT),
        cost_estimate=hint(
            flops=2 * rows * depth * width, bytes_accessed=4 * rows * depth, transcendentals=0
        ),
        name="project",
    )(x, gain, weight, cos_t, sin_t)


def stack_heads(block, group, upper):
    lane = lax.broadcasted_iota(jnp.int32, (block.shape[0], 2 * HD), 1)
    keep = (lane >= HD) if upper else (lane < HD)
    parts = []
    for head in range(group):
        pair = block[:, (head // 2) * 2 * HD : (head // 2 + 1) * 2 * HD].astype(F32)
        if (head % 2 == 1) != upper:
            pair = pltpu.roll(pair, HD, 1)
        parts.append(jnp.where(keep, pair, 0.0).astype(BF16))
    return jnp.concatenate(parts, axis=0)


def unstack_heads(stacked, group, upper):
    rows = stacked.shape[0] // group
    lane = lax.broadcasted_iota(jnp.int32, (rows, 2 * HD), 1)
    pairs = []
    for pair in range(group // 2):
        even = stacked[(2 * pair) * rows : (2 * pair + 1) * rows]
        odd = stacked[(2 * pair + 1) * rows : (2 * pair + 2) * rows]
        if upper:
            even = pltpu.roll(even, HD, 1)
        else:
            odd = pltpu.roll(odd, HD, 1)
        pairs.append(jnp.where(lane < HD, even, odd))
    return jnp.concatenate(pairs, axis=1)


def scores_and_probs(q_pad, keys, qpos, kpos, group):
    scores = (
        lax.dot_general(q_pad, keys, (((1,), (1,)), ((), ())), preferred_element_type=F32)
        * HD ** (-0.5)
    )
    rows = qpos.shape[0]
    blocked = kpos > qpos
    masked = [
        jnp.where(blocked, masked_score, scores[h * rows : (h + 1) * rows]) for h in range(group)
    ]
    scores = jnp.concatenate(masked, axis=0)
    exponent = jnp.exp(scores - jnp.max(scores, axis=-1, keepdims=True))
    return exponent * (1.0 / jnp.sum(exponent, axis=-1, keepdims=True))


def attend_kernel(group, qpos_ref, kpos_ref, q_ref, kv_ref, o_ref):
    keyvals = kv_ref[...].reshape(-1, 2 * HD)
    q_pad = stack_heads(q_ref[...].reshape(-1, group * HD), group, False)
    probs = scores_and_probs(q_pad, keyvals, qpos_ref[...], kpos_ref[...], group)
    out = jnp.dot(probs.astype(BF16), keyvals, preferred_element_type=F32)
    o_ref[...] = unstack_heads(out, group, True).astype(BF16).reshape(o_ref.shape)


def attend_back_kernel(
    group, qpos_ref, kpos_ref, cos_ref, sin_ref, q_ref, do_ref, kv_ref, dq_ref, dkv_ref
):
    keyvals = kv_ref[...].reshape(-1, 2 * HD)
    q_pad = stack_heads(q_ref[...].reshape(-1, group * HD), group, False)
    do_pad = stack_heads(do_ref[...].reshape(-1, group * HD), group, True)
    probs = scores_and_probs(q_pad, keyvals, qpos_ref[...], kpos_ref[...], group)
    d_probs = lax.dot_general(
        do_pad, keyvals, (((1,), (1,)), ((), ())), preferred_element_type=F32
    )
    d_scores = probs * (d_probs - jnp.sum(d_probs * probs, axis=-1, keepdims=True))
    ds_low = d_scores.astype(BF16) * HD ** (-0.5)
    dq = jnp.dot(ds_low, keyvals, preferred_element_type=F32)
    dq = unstack_heads(dq, group, False)
    dq = dq * cos_ref[...] + half_turn(dq * sin_ref[...])
    dq_ref[...] = dq.astype(BF16).reshape(dq_ref.shape)
    contract = (((0,), (0,)), ((), ()))
    d_keyvals = lax.dot_general(
        ds_low, q_pad, contract, preferred_element_type=F32
    ) + lax.dot_general(probs.astype(BF16), do_pad, contract, preferred_element_type=F32)
    dkv_ref[...] = d_keyvals.astype(BF16).reshape(dkv_ref.shape)


def attention_specs(qkv_heads, n_dp, span_rows, group):
    q_spec = pl.BlockSpec((1, 1, span_rows, group * HD), lambda m, s, h: (m, s, 0, h))
    kv_spec = pl.BlockSpec(
        (n_dp, 1, 1, span_rows, 2 * HD), lambda m, s, h: (0, m, s, 0, h)
    )
    pos_q = pl.BlockSpec((span_rows, 1), lambda m, s, h: (0, 0))
    pos_k = pl.BlockSpec((1, n_dp * span_rows), lambda m, s, h: (0, 0))
    return q_spec, kv_spec, pos_q, pos_k


def attend(qpos, kpos, q, kv, group):
    micro, seqs, span_rows, width = q.shape
    n_dp, heads = kv.shape[0], width // (group * HD)
    q_spec, kv_spec, pos_q, pos_k = attention_specs(heads, n_dp, span_rows, group)
    return pl.pallas_call(
        functools.partial(attend_kernel, group),
        grid=(micro, seqs, heads),
        in_specs=[pos_q, pos_k, q_spec, kv_spec],
        out_specs=q_spec,
        out_shape=jax.ShapeDtypeStruct(q.shape, BF16),
        compiler_params=pltpu.CompilerParams(vmem_limit_bytes=VMEM_LIMIT),
        cost_estimate=hint(
            flops=16 * micro * seqs * span_rows * width * n_dp * span_rows,
            bytes_accessed=4 * q.size + 2 * kv.size,
            transcendentals=0,
        ),
        name="attend",
    )(qpos, kpos, q, kv)


def attend_back(qpos, kpos, cos_q, sin_q, q, d_out, kv, group):
    micro, seqs, span_rows, width = q.shape
    n_dp, heads = kv.shape[0], width // (group * HD)
    q_spec, kv_spec, pos_q, pos_k = attention_specs(heads, n_dp, span_rows, group)
    table = pl.BlockSpec((span_rows, group * HD), lambda m, s, h: (0, 0))
    return pl.pallas_call(
        functools.partial(attend_back_kernel, group),
        grid=(micro, seqs, heads),
        in_specs=[pos_q, pos_k, table, table, q_spec, q_spec, kv_spec],
        out_specs=[q_spec, kv_spec],
        out_shape=[
            jax.ShapeDtypeStruct(q.shape, BF16),
            jax.ShapeDtypeStruct(kv.shape, BF16),
        ],
        compiler_params=pltpu.CompilerParams(vmem_limit_bytes=VMEM_LIMIT),
        cost_estimate=hint(
            flops=40 * micro * seqs * span_rows * width * n_dp * span_rows,
            bytes_accessed=6 * q.size + 4 * kv.size,
            transcendentals=0,
        ),
        name="attend_back",
    )(qpos, kpos, cos_q, sin_q, q, d_out, kv)


def norm_back(d_normed, normed, scale):
    return scale * (d_normed - normed * jnp.mean(d_normed * normed, axis=-1, keepdims=True))


def adam_update(gradient, old_mean, square, weight, decay_factor):
    moment = beta_one * old_mean + (1.0 - beta_one) * gradient
    spread = beta_two * square + (1.0 - beta_two) * gradient * gradient
    change = -learn_rate * (
        moment / (1.0 - beta_one**STEP) / (jnp.sqrt(spread / (1.0 - beta_two**STEP)) + adam_eps)
        + decay_factor * weight
    )
    return (moment, spread, change)


def dot(left, right):
    return jnp.dot(left, right, preferred_element_type=F32)


def dot_nt(left, right):
    return lax.dot_general(left, right, (((1,), (1,)), ((), ())), preferred_element_type=F32)


def dot_tn(left, right):
    return lax.dot_general(left, right, (((0,), (0,)), ((), ())), preferred_element_type=F32)


def paired(index, k):
    bit = 1
    while bit <= k:
        if k & bit:
            index = index + bit - 2 * bit * ((index // bit) % 2)
        bit *= 2
    return index


def remote(src, dst, send, recv, device):
    return pltpu.make_async_remote_copy(
        src_ref=src,
        dst_ref=dst,
        send_sem=send,
        recv_sem=recv,
        device_id=device,
        device_id_type=pl.DeviceIdType.MESH,
    )


def meet(peers):
    barrier = pltpu.get_barrier_semaphore()
    for peer in peers:
        pl.semaphore_signal(barrier, inc=1, device_id=peer, device_id_type=pl.DeviceIdType.MESH)
    pl.semaphore_wait(barrier, len(peers))


def start(moves):
    for move in moves:
        move.start()


def arrive(moves):
    for move in moves:
        move.wait_recv()


def sent(moves):
    for move in moves:
        move.wait_send()


class LineSum:

    def __init__(self, line, place, core, tp, value, send, got, send_sem, recv_sem):
        self.value, self.send, self.got = value, send, got
        self.slots, self.moves = [], []
        count, step = 0, 0
        while (1 << step) < line:
            size = line >> (step + 1)
            self.slots.append(list(range(count, count + size)))
            partner = (paired(place, 1 << step) * 2 + core, tp)
            self.moves.append(
                [
                    remote(send.at[i], got.at[i], send_sem.at[i], recv_sem.at[i], partner)
                    for i in self.slots[-1]
                ]
            )
            count, step = count + size, step + 1
        self.steps = step

    def held(self, r, step):
        total = self.value(r)
        for s in range(step):
            total = total + self.got[self.slots[s][r >> (s + 1)]].astype(F32)
        return total

    def begin(self, step):
        if step:
            arrive(self.moves[step - 1])
        for j, i in enumerate(self.slots[step]):
            self.send[i] = self.held((1 << step) | (j << (step + 1)), step).astype(BF16)
        start(self.moves[step])

    def total(self):
        arrive(self.moves[-1])
        return self.held(0, self.steps)

    def close(self):
        for moves in self.moves:
            sent(moves)


def row_moves(remote, rank, n_tp, low, got, send, recv):
    first = [
        [
            remote(low.at[m], got.at[m, k], send.at[m, k], recv.at[m, k], rank(k))
            for k in range(1, n_tp)
            if k != 3
        ]
        for m in range(MICRO)
    ]
    relay = [
        remote(got.at[m, 1 + m], got.at[m, 3], send.at[m, 3], recv.at[m, 3], rank(2 - m))
        for m in range(MICRO)
    ]
    return first, relay


def relay_rows(first, relay):
    for m in range(MICRO):
        first[m][m].wait_recv()
        relay[m].start()


def close_rows(first, relay):
    for m in range(MICRO):
        for i, move in enumerate(first[m]):
            if i != m:
                move.wait_recv()
            move.wait_send()
        relay[m].wait_recv()
        relay[m].wait_send()


def carried(n_tp, src, got, send, recv):
    dp, tp = lax.axis_index("dp"), lax.axis_index("tp")
    rows = got.shape[1]
    return [
        remote(
            src.at[pl.ds(k * rows, rows)],
            got.at[k],
            send.at[k],
            recv.at[k],
            (dp, paired(tp, k)),
        )
        for k in range(1, n_tp)
    ]


def carry_start(n_tp, *move):
    dp, tp = lax.axis_index("dp"), lax.axis_index("tp")
    meet([(dp, paired(tp, k)) for k in range(1, n_tp)])
    start(carried(n_tp, *move))


def carry_end(n_tp, *move):
    moves = carried(n_tp, *move)
    arrive(moves)
    sent(moves)


def gated_kernel(n_tp, last, steps, u_ref, g_ref, w_ref, *refs):
    refs = list(refs)
    move = None
    if n_tp:
        send, recv = refs[-2:]
        src, got = refs.pop(2), refs[6]
        move = (src, got, send, recv)
        refs = refs[:6] + refs[7:-2]
    if last:
        y_old, du_old = refs[:2]
        refs = refs[2:]
    hid_ref, dgu_ref, y_out, du_out, y_sum, du_sum, y_low, du_low, sem = refs
    step = pl.program_id(0)
    depth = w_ref.shape[0]
    sub = hid_ref.shape[1]
    cols = min(512, depth)

    @pl.when(step == 0)
    def _():
        if move:
            carry_start(n_tp, *move)
        y_sum[...] = jnp.zeros_like(y_sum)
        du_sum[...] = jnp.zeros_like(du_sum)
        if last:
            pltpu.make_async_copy(y_old, y_low, sem.at[0]).start()
            pltpu.make_async_copy(du_old, du_low, sem.at[1]).start()

    gate_proj = dot(u_ref[...], w_ref[:, :sub])
    up_proj = dot(u_ref[...], w_ref[:, sub : 2 * sub])
    sigmoid_gate = jax.nn.sigmoid(gate_proj)
    silu_gate = gate_proj * sigmoid_gate
    hid_ref[...] = (silu_gate * up_proj).astype(BF16)
    d_hidden = dot(g_ref[...], w_ref[:, 2 * sub :])
    d_gate = d_hidden * up_proj * sigmoid_gate * (1.0 + gate_proj * (1.0 - sigmoid_gate))
    dgu_ref[:, :sub] = d_gate.astype(BF16)
    dgu_ref[:, sub:] = (d_hidden * silu_gate).astype(BF16)
    for start in range(0, depth, cols):
        part = slice(start, start + cols)
        du_sum[:, part] += dot_nt(dgu_ref[...], w_ref[part, : 2 * sub])
        y_sum[:, part] += dot_nt(hid_ref[...], w_ref[part, 2 * sub :])

    @pl.when(step == steps - 1)
    def _():
        copy_y = pltpu.make_async_copy(y_low, y_out, sem.at[0])
        copy_du = pltpu.make_async_copy(du_low, du_out, sem.at[1])
        if last:
            pltpu.make_async_copy(y_old, y_low, sem.at[0]).wait()
            pltpu.make_async_copy(du_old, du_low, sem.at[1]).wait()
            du_low[...] = (du_sum[...] + du_low[...].astype(F32)).astype(BF16)
            copy_du.start()
            y_low[...] = (y_sum[...] + y_low[...].astype(F32)).astype(BF16)
        else:
            du_low[...] = du_sum[...].astype(BF16)
            copy_du.start()
            y_low[...] = y_sum[...].astype(BF16)
        copy_y.start()
        copy_du.wait()
        copy_y.wait()
        if move:
            carry_end(n_tp, *move)


def carrier_params(n_tp, collective_id):
    if not n_tp:
        return pltpu.CompilerParams(vmem_limit_bytes=VMEM_LIMIT)
    return pltpu.CompilerParams(
        collective_id=collective_id, has_side_effects=True, vmem_limit_bytes=VMEM_LIMIT
    )


def feed_forward(u, g, weights, sub, sums, n_tp=0, carry=None):
    rows, depth = u.shape
    steps = weights.shape[1] // (3 * sub)
    last = sums is not None
    whole = functools.partial(pl.BlockSpec, pipeline_mode=pl.Buffered(1))
    anywhere = pl.BlockSpec(memory_space=pl.ANY)
    return pl.pallas_call(
        functools.partial(gated_kernel, n_tp, last, steps),
        grid=(steps,),
        in_specs=[
            whole((rows, depth), lambda j: (0, 0)),
            whole((rows, depth), lambda j: (0, 0)),
            pl.BlockSpec((depth, 3 * sub), lambda j: (0, j)),
        ]
        + ([anywhere, anywhere] if last else [])
        + ([anywhere] if n_tp else []),
        out_specs=[
            pl.BlockSpec((rows, sub), lambda j: (0, j)),
            pl.BlockSpec((rows, 2 * sub), lambda j: (0, j)),
            anywhere,
            anywhere,
        ]
        + ([anywhere] if n_tp else []),
        out_shape=[
            jax.ShapeDtypeStruct((rows, steps * sub), BF16),
            jax.ShapeDtypeStruct((rows, 2 * steps * sub), BF16),
            jax.ShapeDtypeStruct((rows, depth), BF16),
            jax.ShapeDtypeStruct((rows, depth), BF16),
        ]
        + ([jax.ShapeDtypeStruct((n_tp, rows // n_tp, depth), BF16)] if n_tp else []),
        scratch_shapes=[
            pltpu.VMEM((rows, depth), F32),
            pltpu.VMEM((rows, depth), F32),
            pltpu.VMEM((rows, depth), BF16),
            pltpu.VMEM((rows, depth), BF16),
            pltpu.SemaphoreType.DMA((2,)),
        ]
        + ([pltpu.SemaphoreType.DMA((n_tp,))] * 2 if n_tp else []),
        compiler_params=carrier_params(n_tp, 3),
        cost_estimate=hint(
            flops=12 * rows * depth * steps * sub,
            bytes_accessed=2 * weights.size + 8 * rows * depth,
            transcendentals=0,
        ),
        name="feed_forward",
    )(u, g, weights, *(sums if last else ()), *([carry] if n_tp else []))


def outer_kernel(n_tp, batches, sub, steps, *refs):
    u_refs, g_refs = refs[:batches], refs[batches : 2 * batches]
    hid_refs, dgu_refs = refs[2 * batches : 3 * batches], refs[3 * batches : 4 * batches]
    refs = refs[4 * batches :]
    move = None
    if n_tp:
        src, out_ref, got, send, recv = refs
        move = (src, got, send, recv)

        @pl.when(pl.program_id(0) == 0)
        def _():
            carry_start(n_tp, *move)

    else:
        (out_ref,) = refs
    for j in range(steps):
        both = slice(2 * j * sub, 2 * (j + 1) * sub)
        one = slice(j * sub, (j + 1) * sub)
        total = dot_tn(u_refs[0][...], dgu_refs[0][:, both])
        for m in range(1, batches):
            total += dot_tn(u_refs[m][...], dgu_refs[m][:, both])
        out_ref[0, :, 3 * j * sub : 3 * j * sub + 2 * sub] = total.astype(BF16)
        total = dot_tn(g_refs[0][...], hid_refs[0][:, one])
        for m in range(1, batches):
            total += dot_tn(g_refs[m][...], hid_refs[m][:, one])
        out_ref[0, :, 3 * j * sub + 2 * sub : 3 * (j + 1) * sub] = total.astype(BF16)
    if n_tp:

        @pl.when(pl.program_id(0) == pl.num_programs(0) - 1)
        def _():
            carry_end(n_tp, *move)


def outer_products(us, gs, hids, dgus, own, sub, n_tp=0, carry=None):
    batches = len(us)
    rows, depth = us[0].shape
    n_dp = depth // own
    width = hids[0].shape[1]
    steps = width // sub
    whole = functools.partial(pl.BlockSpec, pipeline_mode=pl.Buffered(1))
    column = pl.BlockSpec((rows, own), lambda i: (0, i))
    anywhere = pl.BlockSpec(memory_space=pl.ANY)
    return pl.pallas_call(
        functools.partial(outer_kernel, n_tp, batches, sub, steps),
        grid=(n_dp,),
        in_specs=[column] * (2 * batches)
        + [whole((rows, width), lambda i: (0, 0))] * batches
        + [whole((rows, 2 * width), lambda i: (0, 0))] * batches
        + ([anywhere] if n_tp else []),
        out_specs=[pl.BlockSpec((1, own, 3 * width), lambda i: (i, 0, 0))]
        + ([anywhere] if n_tp else []),
        out_shape=[jax.ShapeDtypeStruct((n_dp, own, 3 * width), BF16)]
        + ([jax.ShapeDtypeStruct((n_tp, rows // n_tp, depth), BF16)] if n_tp else []),
        scratch_shapes=[pltpu.SemaphoreType.DMA((n_tp,))] * 2 if n_tp else [],
        compiler_params=carrier_params(n_tp, 4),
        cost_estimate=hint(
            flops=6 * rows * batches * depth * width,
            bytes_accessed=6 * depth * width,
            transcendentals=0,
        ),
        name="outer_products",
    )(*us, *gs, *hids, *dgus, *([carry] if n_tp else []))


def attn_grad_kernel(a_ref, m_ref, qkv_ref, att_ref, out_qkv, out_output):
    out_qkv[0] = dot_tn(a_ref[...], qkv_ref[...]).astype(BF16)
    out_output[0] = dot_tn(m_ref[...], att_ref[...]).astype(BF16)


def attn_weight_grads(attn_in, d_mid, d_qkv, attended, own):
    rows, depth = attn_in.shape
    column = pl.BlockSpec((rows, own), lambda i: (0, i))
    whole = functools.partial(pl.BlockSpec, pipeline_mode=pl.Buffered(1))
    widths = (d_qkv.shape[1], attended.shape[1])
    return pl.pallas_call(
        attn_grad_kernel,
        grid=(depth // own,),
        in_specs=[column, column] + [whole((rows, w), lambda i: (0, 0)) for w in widths],
        out_specs=[pl.BlockSpec((1, own, w), lambda i: (i, 0, 0)) for w in widths],
        out_shape=[jax.ShapeDtypeStruct((depth // own, own, w), BF16) for w in widths],
        compiler_params=pltpu.CompilerParams(vmem_limit_bytes=VMEM_LIMIT),
        cost_estimate=hint(
            flops=2 * rows * depth * sum(widths), bytes_accessed=4 * rows * depth, transcendentals=0
        ),
        name="attn_weight_grads",
    )(attn_in, d_mid, d_qkv, attended)


def small_steps_kernel(qkv_ref, out_ref, gain_ref, *refs):
    states, results = refs[:12], refs[12:]
    q_width = states[0].shape[1]
    gradients = (
        lambda: qkv_ref[0, :, :q_width].astype(F32),
        lambda: qkv_ref[0, :, q_width:].astype(F32),
        lambda: out_ref[...].T,
        lambda: gain_ref[...],
    )
    for i, read in enumerate(gradients):
        gradient = read()
        mean_ref, square_ref, weight_ref = states[3 * i : 3 * i + 3]
        decay = weight_decay if i < 3 else 0.0
        moment, spread, change = adam_update(
            gradient, mean_ref[...], square_ref[...], weight_ref[...].astype(F32), decay
        )
        for ref, value in zip(results[4 * i : 4 * i + 4], (gradient, moment, spread, change)):
            ref[...] = value


def small_steps(qkv_grad, out_grad, gain_grad, *states):
    vmem = pl.BlockSpec(memory_space=pltpu.VMEM)
    shapes = [jax.ShapeDtypeStruct(states[3 * i].shape, F32) for i in range(4)]
    return tuple(
        pl.pallas_call(
            small_steps_kernel,
            in_specs=[vmem] * 15,
            out_specs=[vmem] * 16,
            out_shape=[shape for shape in shapes for _ in range(4)],
            compiler_params=pltpu.CompilerParams(vmem_limit_bytes=VMEM_LIMIT),
            name="small_steps",
        )(qkv_grad, out_grad, gain_grad, *states)
    )


def step_kernel(turned, decay, steps, chunks, *refs):
    grads = refs[:chunks]
    mean_ref, square_ref, weight_ref, grad_ref, moment_ref, spread_ref, update_ref = refs[chunks:]
    place = pl.program_id(1)
    for c in range(chunks):

        @pl.when(place // steps == c)
        def _(c=c):
            gradient = grads[c][...].astype(F32)
            if turned:
                gradient = gradient.T
            gradient = gradient.reshape(grad_ref.shape)
            moment, spread, change = adam_update(
                gradient, mean_ref[...], square_ref[...], weight_ref[...].astype(F32), decay
            )
            grad_ref[...] = gradient
            moment_ref[...] = moment
            spread_ref[...] = spread
            update_ref[...] = change


def step_from_chunks(grads, old_mean, square, weight, sub, offset, turned, decay):
    chunks, own = len(grads), grads[0].shape[0]
    steps = grads[0].shape[1] // (3 * sub)

    def grad_spec(c):
        def index(i, p):
            j = jnp.clip(p - c * steps, 0, steps - 1)
            return (0, 3 * j + i + offset)

        return pl.BlockSpec((own, sub), index)

    if turned:
        lead, spec = 1, pl.BlockSpec((sub, own), lambda i, p: (p, 0))
    else:
        lead, spec = old_mean.shape[0], pl.BlockSpec((1, own, sub), lambda i, p: (i, 0, p))
    return tuple(
        pl.pallas_call(
            functools.partial(step_kernel, turned, decay, steps, chunks),
            grid=(lead, chunks * steps),
            in_specs=[grad_spec(c) for c in range(chunks)] + [spec] * 3,
            out_specs=[spec] * 4,
            out_shape=[jax.ShapeDtypeStruct(old_mean.shape, F32)] * 4,
            compiler_params=pltpu.CompilerParams(vmem_limit_bytes=VMEM_LIMIT),
            cost_estimate=hint(
                flops=20 * old_mean.size, bytes_accessed=28 * old_mean.size, transcendentals=0
            ),
            name="weight_step",
        )(*grads, old_mean, square, weight)
    )


def finish_kernel(
    n_dp,
    n_tp,
    tok_low,
    share_ref,
    gain_ref,
    tok_rows,
    grad_ref,
    gain_own,
    met,
    z_send,
    z_got,
    ranks_got,
    gain_sum,
    gain_got,
    local_sem,
    tok_s,
    tok_r,
    core_s,
    core_r,
    z_s,
    z_r,
    rank_s,
    rank_r,
    gain_s,
    gain_r,
):
    line = n_dp // 2
    own = share_ref.shape[1]
    dp, tp = lax.axis_index("dp"), lax.axis_index("tp")
    place, core = dp // 2, dp % 2

    def rank(k):
        return (dp, paired(tp, k))

    def columns(index):
        return pl.ds(pl.multiple_of(index * own, own), own)

    first, relay = row_moves(remote, rank, n_tp, tok_low, tok_rows, tok_s, tok_r)
    keep = [
        pltpu.make_async_copy(tok_low.at[m], tok_rows.at[m, 0], local_sem.at[m])
        for m in range(MICRO)
    ]
    core_moves = [
        remote(
            share_ref.at[z * 2 + 1 - core],
            met.at[z],
            core_s.at[z],
            core_r.at[z],
            (place * 2 + 1 - core, tp),
        )
        for z in range(line)
    ]
    sums = LineSum(
        line,
        place,
        core,
        tp,
        lambda r: share_ref[paired(place, r) * 2 + core].astype(F32)
        + met[paired(place, r)].astype(F32),
        z_send,
        z_got,
        z_s,
        z_r,
    )
    rank_moves = [
        remote(gain_ref, ranks_got.at[k], rank_s.at[k], rank_r.at[k], rank(k))
        for k in range(1, n_tp)
    ]
    gain_moves = [
        remote(
            gain_sum.at[:, columns(paired(dp, j))],
            gain_got.at[j],
            gain_s.at[j],
            gain_r.at[j],
            (paired(dp, j), tp),
        )
        for j in range(1, n_dp)
    ]

    meet([rank(k) for k in range(1, n_tp)] + [(paired(dp, j), tp) for j in range(1, n_dp)])
    start(core_moves)
    start(rank_moves)
    for moves in first:
        start(moves)
    start(keep)
    arrive(core_moves)
    sums.begin(0)
    arrive(rank_moves)
    total = gain_ref[...]
    for k in range(1, n_tp):
        total = total + ranks_got[k]
    gain_sum[...] = total
    start(gain_moves)
    for step in range(1, sums.steps):
        sums.begin(step)
    relay_rows(first, relay)
    arrive(gain_moves)
    total = gain_sum[:, columns(dp)]
    for j in range(1, n_dp):
        total = total + gain_got[j]
    gain_own[...] = total
    grad_ref[...] = sums.total()
    close_rows(first, relay)
    sums.close()
    for moves in (core_moves, rank_moves, gain_moves):
        sent(moves)
    for copy in keep:
        copy.wait()


def finish(n_dp, n_tp, tok_low, shares, gain_part):
    micro, rows, depth = tok_low.shape
    _, own, width = shares.shape
    line = n_dp // 2
    anywhere = pl.BlockSpec(memory_space=pl.ANY)
    vmem = pl.BlockSpec(memory_space=pltpu.VMEM)
    dma = pltpu.SemaphoreType.DMA
    return pl.pallas_call(
        functools.partial(finish_kernel, n_dp, n_tp),
        in_specs=[anywhere, vmem, vmem],
        out_specs=[anywhere, vmem, vmem],
        out_shape=[
            jax.ShapeDtypeStruct((micro, n_tp, rows, depth), BF16),
            jax.ShapeDtypeStruct((own, width), F32),
            jax.ShapeDtypeStruct((2, own), F32),
        ],
        scratch_shapes=[
            pltpu.VMEM((line, own, width), BF16),
            pltpu.VMEM((line, own, width), BF16),
            pltpu.VMEM((line, own, width), BF16),
            pltpu.VMEM((n_tp, 2, depth), F32),
            pltpu.VMEM((2, depth), F32),
            pltpu.VMEM((n_dp, 2, own), F32),
            dma((micro,)),
            dma((micro, n_tp)),
            dma((micro, n_tp)),
            dma((line,)),
            dma((line,)),
            dma((line,)),
            dma((line,)),
            dma((n_tp,)),
            dma((n_tp,)),
            dma((n_dp,)),
            dma((n_dp,)),
        ],
        compiler_params=pltpu.CompilerParams(
            collective_id=1, has_side_effects=True, vmem_limit_bytes=VMEM_LIMIT
        ),
        cost_estimate=hint(flops=10**10, bytes_accessed=10**8, transcendentals=0),
        name="finish",
    )(tok_low, shares, gain_part)


def tail_kernel(n_dp, n_tp, group, *refs):
    (
        du_refs,
        y_refs,
        du_ins,
        seed_ref,
        middle_ref,
        x_ref,
        gains_ref,
        out_refs,
        qkv_refs,
        q_ref,
        kv_ref,
        qpos_ref,
        kpos_ref,
        cos_ref,
        sin_ref,
        d_qkv_ref,
        mid_rows,
        out_rows,
        tok_low,
        gain_ref,
    ) = (refs[0:2], refs[2:4], refs[4:6]) + refs[6:10] + (refs[10:12], refs[12:14]) + refs[14:25]
    (
        weights,
        du_got,
        y_got,
        own_mid,
        mid_low,
        block_low,
        do_send,
        do_got,
        shares,
        met,
        z_send,
        z_got,
        heads_got,
        local_sem,
        block_s,
        block_r,
        y_s,
        y_r,
        mid_s,
        mid_r,
        do_s,
        do_r,
        core_s,
        core_r,
        z_s,
        z_r,
        heads_s,
        heads_r,
    ) = refs[25:]
    line = n_dp // 2
    batches = range(MICRO)
    others = range(1, n_tp)
    dp, tp = lax.axis_index("dp"), lax.axis_index("tp")
    place, core = dp // 2, dp % 2
    depth = middle_ref.shape[1]
    rows = mid_low.shape[1]
    seq_rows = q_ref.shape[2]
    q_width = q_ref.shape[3]
    kv_width = kv_ref.shape[4]
    width = q_width + kv_width
    half = depth // 2

    def rank(k):
        return (dp, paired(tp, k))

    def spot(k):
        return (paired(place, k) * 2 + core, tp)

    other_core = (place * 2 + 1 - core, tp)

    def block(k):
        return pl.ds(k * rows, rows)

    y_moves = [
        [
            remote(y_refs[m].at[block(k)], y_got.at[m, k], y_s.at[m, k], y_r.at[m, k], rank(k))
            for k in others
        ]
        for m in batches
    ]

    block_first, block_relay = row_moves(
        remote, rank, n_tp, block_low, out_rows, block_s, block_r
    )
    mid_first, mid_relay = row_moves(remote, rank, n_tp, mid_low, mid_rows, mid_s, mid_r)
    do_moves = [
        [
            remote(
                do_send.at[m, k], do_got.at[m, block(k)], do_s.at[m, k], do_r.at[m, k], rank(k)
            )
            for k in others
        ]
        for m in batches
    ]
    core_moves = [
        remote(shares.at[m, 1 - core], met.at[m], core_s.at[m], core_r.at[m], other_core)
        for m in batches
    ]
    key_sums = [
        LineSum(
            line,
            place,
            core,
            tp,
            lambda r, m=m: shares[m, core, paired(place, r)].astype(F32)
            + met[m, paired(place, r)].astype(F32),
            z_send.at[m],
            z_got.at[m],
            z_s.at[m],
            z_r.at[m],
        )
        for m in batches
    ]
    heads_moves = [
        [
            remote(
                d_qkv_ref.at[m, block(k)],
                heads_got.at[m, k],
                heads_s.at[m, k],
                heads_r.at[m, k],
                rank(k),
            )
            for k in others
        ]
        for m in batches
    ]

    own_copies = [
        pltpu.make_async_copy(ref.at[pl.ds(0, rows)], got.at[m, 0], local_sem.at[i, m])
        for i, (pair, got) in enumerate(((du_refs, du_got), (y_refs, y_got)))
        for m, ref in enumerate(pair)
    ]
    own_copies += [
        pltpu.make_async_copy(
            ref.at[pl.ds(1, n_tp - 1)], du_got.at[m, pl.ds(1, n_tp - 1)], local_sem.at[4, m]
        )
        for m, ref in enumerate(du_ins)
    ]
    keep_block = [
        pltpu.make_async_copy(block_low.at[m], out_rows.at[m, 0], local_sem.at[5, m])
        for m in batches
    ]
    load_out = [
        pltpu.make_async_copy(
            ref, weights.at[side, :, pl.ds(0, n_tp * q_width)], local_sem.at[6, side]
        )
        for side, ref in enumerate(out_refs)
    ]
    load_qkv = [
        pltpu.make_async_copy(ref, weights.at[side], local_sem.at[2, side])
        for side, ref in enumerate(qkv_refs)
    ]
    keep = [
        pltpu.make_async_copy(mid_low.at[m], mid_rows.at[m, 0], local_sem.at[3, m])
        for m in batches
    ]

    meet([rank(k) for k in others] + [other_core] + [spot(k) for k in range(1, line)])
    start(own_copies)
    start(load_out)
    gain_one = gains_ref[0:1, :].astype(F32)
    gain_two = gains_ref[1:2, :].astype(F32)
    gain_ref[...] = jnp.zeros_like(gain_ref)

    def total_of(got, m):
        total = got[m, 0].astype(F32)
        for k in others:
            total = total + got[m, k].astype(F32)
        return total

    for copy in own_copies:
        copy.wait()
    for m in batches:
        part = slice(m * rows, (m + 1) * rows)
        d_mixed = total_of(du_got, m)
        middle = middle_ref[part, :]
        scale = mean_square_scale(middle)
        normed = middle * scale
        gain_ref[1:2, :] += jnp.sum(d_mixed * normed, axis=0, keepdims=True)
        d_middle = seed_ref[part, :].astype(F32) + norm_back(d_mixed * gain_two, normed, scale)
        own_mid[m] = d_middle
        mid_low[m] = d_middle.astype(BF16)
        if m == 0:
            for copy in load_out:
                copy.wait()
        near_cols = pl.ds(pl.multiple_of(core * half, half), half)
        far_cols = pl.ds(pl.multiple_of((1 - core) * half, half), half)
        near, far = mid_low[m, :, near_cols], mid_low[m, :, far_cols]
        for k in range(n_tp):
            lanes = slice(k * q_width, (k + 1) * q_width)
            rows_out = (dot(near, weights[0, :, lanes]) + dot(far, weights[1, :, lanes])).astype(
                BF16
            )
            if k == 0:
                do_got[m, 0:rows, :] = rows_out
            else:
                do_send[m, k] = rows_out
        start(do_moves[m])
    start(load_qkv)
    for m in batches:
        start(y_moves[m])

    def attend_back_seq(m, s):
        seq = pl.ds(s * seq_rows, seq_rows)
        for h in range(kv_width // (2 * HD)):
            pair = slice(h * 2 * HD, (h + 1) * 2 * HD)
            keyvals = kv_ref[:, m, s, :, pair].reshape(-1, 2 * HD)
            grads = None
            for part in range(group // 2):
                lanes = slice((h * group + 2 * part) * HD, (h * group + 2 * part + 2) * HD)
                q_pad = stack_heads(q_ref[m, s, :, lanes], 2, False)
                do_pad = stack_heads(do_got[m, seq, lanes], 2, True)
                probs = scores_and_probs(q_pad, keyvals, qpos_ref[...], kpos_ref[...], 2)
                d_probs = dot_nt(do_pad, keyvals)
                d_scores = probs * (d_probs - jnp.sum(d_probs * probs, axis=-1, keepdims=True))
                ds_low = d_scores.astype(BF16) * HD ** (-0.5)
                dq = unstack_heads(dot(ds_low, keyvals), 2, False)
                cos_q, sin_q = cos_ref[:, 0 : 2 * HD], sin_ref[:, 0 : 2 * HD]
                dq = dq * cos_q + half_turn(dq * sin_q)
                d_qkv_ref[m, seq, lanes] = dq.astype(BF16)
                term = dot_tn(ds_low, q_pad) + dot_tn(probs.astype(BF16), do_pad)
                grads = term if grads is None else grads + term
            grads = grads.astype(BF16)
            for i in range(n_dp):
                shares[m, i % 2, i // 2, seq, pair] = grads[i * seq_rows : (i + 1) * seq_rows]

    def attend_back_range(m, low, high):
        @pl.loop(low, high)
        def _(s):
            attend_back_seq(m, s)

    def send_along(m):
        arrive([core_moves[m]])
        key_sums[m].begin(0)

    def advance(m):
        for step in range(1, key_sums[m].steps):
            key_sums[m].begin(step)

    def close_keys(m):
        total = key_sums[m].total()
        cos_k, sin_k = cos_ref[:, q_width:], sin_ref[:, q_width:]
        for s in range(SEQS):
            seq = slice(s * seq_rows, (s + 1) * seq_rows)
            grad = total[seq]
            d_qkv_ref[m, seq, q_width:] = (grad * cos_k + half_turn(grad * sin_k)).astype(BF16)
        start(heads_moves[m])

    def close_block(m):
        arrive(y_moves[m])
        part = slice(m * rows, (m + 1) * rows)
        block_low[m] = (middle_ref[part, :] + total_of(y_got, m)).astype(BF16)
        start(block_first[m])
        keep_block[m].start()

    def close_tokens(m):
        arrive(heads_moves[m])
        part = slice(m * rows, (m + 1) * rows)
        heads = [d_qkv_ref[m, 0:rows, :]] + [heads_got[m, k] for k in others]
        sides = []
        for side in range(2):
            total = dot_nt(heads[0], weights[side, :, 0:width])
            for k in others:
                total = total + dot_nt(heads[k], weights[side, :, k * width : (k + 1) * width])
            sides.append(total)
        d_act = jnp.where(
            core == 0,
            jnp.concatenate(sides, axis=1),
            jnp.concatenate(sides[::-1], axis=1),
        )
        x_part = x_ref[part, :].astype(F32)
        scale = mean_square_scale(x_part)
        normed = x_part * scale
        gain_ref[0:1, :] += jnp.sum(d_act * normed, axis=0, keepdims=True)
        tok_low[m] = (own_mid[m] + norm_back(d_act * gain_one, normed, scale)).astype(BF16)

    arrive(do_moves[0])
    attend_back_range(0, 0, SEQS)
    core_moves[0].start()
    for m in batches:
        start(mid_first[m])
        keep[m].start()
    arrive(do_moves[1])
    attend_back_range(1, 0, SEQS // 2)
    send_along(0)
    attend_back_range(1, SEQS // 2, SEQS)
    core_moves[1].start()
    advance(0)
    for copy in load_qkv:
        copy.wait()
    send_along(1)
    close_block(0)
    close_keys(0)
    advance(1)
    close_block(1)
    relay_rows(mid_first, mid_relay)
    close_tokens(0)
    close_keys(1)
    relay_rows(block_first, block_relay)
    close_tokens(1)
    close_rows(mid_first, mid_relay)
    close_rows(block_first, block_relay)
    for m in batches:
        key_sums[m].close()
        for moves in (y_moves[m], do_moves[m], [core_moves[m]], heads_moves[m]):
            sent(moves)
        keep[m].wait()
        keep_block[m].wait()


def tail(
    n_dp, n_tp, group, sums, arrived, seed, middle, x, gains, out_w, qkv_w, q, kv, qpos, kpos, cos, sin
):
    own_rows, depth = middle.shape
    rows = own_rows // MICRO
    batch_rows = n_tp * rows
    line = n_dp // 2
    q_width, kv_width = q.shape[3], kv.shape[4]
    width = q_width + kv_width
    anywhere = pl.BlockSpec(memory_space=pl.ANY)
    vmem = pl.BlockSpec(memory_space=pltpu.VMEM)
    dma = pltpu.SemaphoreType.DMA
    gathered = jax.ShapeDtypeStruct((MICRO, n_tp, rows, depth), BF16)
    return pl.pallas_call(
        functools.partial(tail_kernel, n_dp, n_tp, group),
        in_specs=[anywhere] * 6 + [vmem] * 4 + [anywhere] * 4 + [vmem] * 6,
        out_specs=[vmem, anywhere, anywhere, vmem, vmem],
        out_shape=[
            jax.ShapeDtypeStruct((MICRO, batch_rows, width), BF16),
            gathered,
            gathered,
            jax.ShapeDtypeStruct((MICRO, rows, depth), BF16),
            jax.ShapeDtypeStruct((2, depth), F32),
        ],
        scratch_shapes=[
            pltpu.VMEM((2, depth // 2, n_tp * width), BF16),
            pltpu.VMEM((MICRO, n_tp, rows, depth), BF16),
            pltpu.VMEM((MICRO, n_tp, rows, depth), BF16),
            pltpu.VMEM((MICRO, rows, depth), F32),
            pltpu.VMEM((MICRO, rows, depth), BF16),
            pltpu.VMEM((MICRO, rows, depth), BF16),
            pltpu.VMEM((MICRO, n_tp, rows, q_width), BF16),
            pltpu.VMEM((MICRO, batch_rows, q_width), BF16),
            pltpu.VMEM((MICRO, 2, line, batch_rows, kv_width), BF16),
            pltpu.VMEM((MICRO, line, batch_rows, kv_width), BF16),
            pltpu.VMEM((MICRO, line, batch_rows, kv_width), BF16),
            pltpu.VMEM((MICRO, line, batch_rows, kv_width), BF16),
            pltpu.VMEM((MICRO, n_tp, rows, width), BF16),
            dma((7, 2)),
        ]
        + [dma((MICRO, n_tp))] * 8
        + [dma((MICRO,))] * 2
        + [dma((MICRO, line))] * 2
        + [dma((MICRO, n_tp))] * 2,
        compiler_params=pltpu.CompilerParams(
            collective_id=0, has_side_effects=True, vmem_limit_bytes=VMEM_LIMIT
        ),
        cost_estimate=hint(
            flops=10**10,
            bytes_accessed=10**8,
            transcendentals=0,
        ),
        name="tail",
    )(
        sums[0][1],
        sums[1][1],
        sums[0][0],
        sums[1][0],
        *arrived,
        seed,
        middle,
        x,
        gains,
        *out_w,
        *qkv_w,
        q,
        kv,
        qpos,
        kpos,
        cos,
        sin,
    )


def spread_kernel(rank_ref, out_ref, tok_ref, block_ref, grad_ref):
    block_ref[...] = out_ref[...]
    grad_ref[...] = tok_ref[...].astype(F32)


def spread(rank, out_rows, tok_rows):
    micro, n_tp, rows, depth = out_rows.shape
    here = pl.BlockSpec((1, 1, rows, depth), lambda m, k, r: (m, k, 0, 0))
    there = pl.BlockSpec((1, 1, rows, depth), lambda m, k, r: (m, r[0] ^ k, 0, 0))
    return pl.pallas_call(
        spread_kernel,
        grid_spec=pltpu.PrefetchScalarGridSpec(
            num_scalar_prefetch=1,
            grid=(micro, n_tp),
            in_specs=[here, here],
            out_specs=[there, there],
        ),
        out_shape=[
            jax.ShapeDtypeStruct(out_rows.shape, BF16),
            jax.ShapeDtypeStruct(out_rows.shape, F32),
        ],
        compiler_params=pltpu.CompilerParams(vmem_limit_bytes=VMEM_LIMIT),
        name="spread",
    )(rank, out_rows, tok_rows)


def per_device(
    n_dp,
    n_tp,
    tokens,
    cotangent,
    span_order,
    w_query,
    w_keyval,
    w_output,
    w_gateup,
    w_down,
    norm_gains,
    mean_query,
    square_query,
    mean_keyval,
    square_keyval,
    mean_output,
    square_output,
    mean_gateup,
    square_gateup,
    mean_down,
    square_down,
    mean_gains,
    square_gains,
):
    depth = tokens.shape[1]
    span_rows = 2 * CH
    block_rows = SEQS * span_rows // n_tp
    parts = span_rows // min(span_rows, block_rows)
    q_width = w_query.shape[1]
    kv_width = w_keyval.shape[1]
    hidden_width = w_down.shape[0]
    own_depth = w_query.shape[0]
    group = q_width // HD // (kv_width // (2 * HD))
    device = lax.axis_index("dp")
    rank = lax.axis_index("tp")
    line = n_dp // 2
    place, core = device // 2, device % 2

    def swap(value, k):
        return lax.ppermute(value, "tp", [(i, i ^ k) for i in range(n_tp)])

    def reorder(value):
        return jnp.concatenate(
            [lax.dynamic_slice_in_dim(value, rank ^ k, 1, axis=1) for k in range(n_tp)], axis=1
        )

    def gather_blocks(own):
        half = own.shape[0] // 2
        got = [own, swap(own, 1), swap(own, 2)]
        got.append(jnp.concatenate([swap(got[1][:half], 2), swap(got[2][half:], 1)], axis=0))
        return got + [swap(own, k) for k in range(4, n_tp)]

    def exchange(blocks):
        return [blocks[0]] + [swap(blocks[k], k) for k in range(1, n_tp)]

    def total_of(parts):
        total = parts[0].astype(F32)
        for part in parts[1:]:
            total = total + part.astype(F32)
        return total

    def gather_pair(owns):
        got = [owns, [swap(own, 1) for own in owns], [swap(own, 2) for own in owns]]
        got.append([swap(got[1][0], 2)] + [swap(own, 1) for own in got[2][1:]])
        return got + [[swap(own, k) for own in owns] for k in range(4, n_tp)]

    def scatter_pair(blocks):
        first = swap(blocks[0][3], 1)
        seconds = [swap(blocks[m][3], 2) for m in range(1, MICRO)]
        to_two = total_of([blocks[0][2], first]).astype(BF16)
        to_one = [total_of([blocks[m][1], seconds[m - 1]]).astype(BF16) for m in range(1, MICRO)]
        yield [to_two] + to_one
        totals = []
        for m in range(MICRO):
            one = blocks[m][1] if m == 0 else to_one[m - 1]
            two = to_two if m == 0 else blocks[m][2]
            far = [swap(blocks[m][k], k) for k in range(4, n_tp)]
            totals.append(total_of([blocks[m][0], swap(one, 1), swap(two, 2)] + far))
        yield totals

    def line_sum(other, own):
        met = lax.ppermute(other, "dp", [(i, i ^ 1) for i in range(n_dp)])
        yield [met]

        def share(index):
            index = jnp.clip(index, 0, line - 1)
            return lax.dynamic_index_in_dim(own, index, 0, False).astype(
                F32
            ) + lax.dynamic_index_in_dim(met, index, 0, False).astype(F32)

        sends = []
        for far in range(1, line):
            for way in (far, -far):
                sends.append((way, share(place + way).astype(BF16)))
        yield [value for _, value in sends]
        total = share(place)
        for far in range(1, line):
            arrived = []
            for way, value in sends:
                if abs(way) == far:
                    pairs = [
                        (i, i + 2 * way) for i in range(n_dp) if 0 <= i + 2 * way < n_dp
                    ]
                    arrived.append(lax.ppermute(value, "dp", pairs))
            if far <= 3:
                yield arrived
            for value in arrived:
                total = total + value.astype(F32)
        yield [total]

    def my_half(value):
        return lax.dynamic_slice_in_dim(value, core * (depth // 2), depth // 2, axis=0)

    def swap_cores(value):
        return lax.ppermute(value, "dp", [(i, i ^ 1) for i in range(n_dp)])

    def both_halves(near, far):
        return jnp.where(
            core == 0,
            jnp.concatenate([near, far], axis=1),
            jnp.concatenate([far, near], axis=1),
        )

    def after(value, *earlier):
        return lax.optimization_barrier((value,) + earlier)[0]

    qkv_full = lax.all_gather(
        jnp.concatenate([w_query, w_keyval], axis=1), "dp", axis=0, tiled=True
    )
    gains_full = lax.all_gather(norm_gains, "dp", axis=1, tiled=True)
    out_t_full = lax.all_gather(w_output.T, "dp", axis=0, tiled=True)

    offsets = jnp.arange(CH, dtype=jnp.int32)
    all_pos = (span_order[:, None] * CH + offsets[None, :]).reshape(n_dp, parts, -1)
    all_pos = jnp.stack([all_pos[:, (rank % parts) ^ p] for p in range(parts)], axis=1)
    own_pos = lax.dynamic_slice_in_dim(all_pos, device, 1).reshape(-1)
    all_pos = all_pos.reshape(-1)
    qpos, kpos = own_pos[:, None], all_pos[None, :]
    kv_kinds = [True, False] * (kv_width // (2 * HD))
    cos_t, sin_t = lane_tables(own_pos, [True] * (q_width // HD) + kv_kinds)

    x = reorder(tokens.reshape(MICRO, n_tp, block_rows, depth))
    seed = reorder(cotangent.reshape(MICRO, n_tp, block_rows, depth))
    batch_rows = SEQS * span_rows
    rows = MICRO * batch_rows
    gain_one, gain_two = gains_full[0:1], gains_full[1:2]
    attn_in, qkv = project(x.reshape(rows, depth), gain_one, qkv_full, cos_t, sin_t)
    qkv = qkv.reshape(MICRO, SEQS, span_rows, q_width + kv_width)
    q, kv = qkv[..., :q_width], qkv[..., q_width:]
    kv_all = lax.all_gather(kv, "dp", axis=0, tiled=False)

    sub = min(SUB, hidden_width // CHUNKS)
    chunk = hidden_width // CHUNKS
    w_down_t = w_down.T
    mlp_full = []
    for c in range(CHUNKS):
        pieces = []
        for start in range(c * chunk, (c + 1) * chunk, sub):
            cols = slice(start, start + sub)
            pieces += [w_gateup[0][:, cols], w_gateup[1][:, cols], w_down_t[:, cols]]
        shard = jnp.concatenate(pieces, axis=1)
        mlp_full.append(lax.all_gather(shard, "dp", axis=0, tiled=True))

    attended = attend(qpos, kpos, q, kv_all, group)
    attended_blocks = attended.reshape(MICRO, n_tp, block_rows, q_width)
    out_near = my_half(out_t_full)
    out_near = jnp.concatenate([out_near] + [swap(out_near, k) for k in range(1, n_tp)], axis=1)
    out_far = swap_cores(out_near)
    heads_in = exchange([attended_blocks[:, k] for k in range(n_tp)])
    own_rows = MICRO * block_rows
    x_own = x[:, 0].reshape(own_rows, depth).astype(F32)
    heads_cat = jnp.concatenate([v.reshape(own_rows, q_width) for v in heads_in], axis=1)
    middle = x_own + both_halves(dot_nt(heads_cat, out_near), dot_nt(heads_cat, out_far))
    scale_two = mean_square_scale(middle)
    normed_two = middle * scale_two
    u_own = (normed_two * gain_two.astype(F32)).astype(BF16)
    batches = range(MICRO)
    gathered = [g.reshape(MICRO, block_rows, depth) for g in gather_blocks(u_own)]
    u = [jnp.concatenate([gathered[k][m] for k in range(n_tp)], axis=0) for m in batches]
    g = [seed[m].reshape(batch_rows, depth) for m in batches]

    qkv_half = after(my_half(qkv_full), u[0])
    quarter = depth // 4
    qkv_width = q_width + kv_width
    qkv_near = jnp.zeros((depth // 2, n_tp * qkv_width), BF16)
    qkv_near = lax.dynamic_update_slice(qkv_near, qkv_half, (0, 0))
    qkv_moves = [(k, i) for i in range(2) for k in range(1, min(n_tp, 3))]
    qkv_moves = [qkv_moves[:2], qkv_moves[2:]] + [
        [(k, i) for k in range(3, n_tp)] for i in range(2)
    ]

    def move_qkv(buffer):
        for k, i in qkv_moves.pop(0) if qkv_moves else []:
            got = swap(qkv_half[i * quarter : (i + 1) * quarter], k)
            buffer = lax.dynamic_update_slice(buffer, got, (i * quarter, k * qkv_width))
        return buffer

    def blocks_of(value):
        return [value[k * block_rows : (k + 1) * block_rows] for k in range(n_tp)]

    def own_part(value, m):
        return value[m * block_rows : (m + 1) * block_rows]

    core_index = core.astype(jnp.int32).reshape(1)
    gain_two_f = gain_two.astype(F32)
    gain_one_f = gain_one.astype(F32)
    cos_q, sin_q = cos_t[:, : group * HD], sin_t[:, : group * HD]
    cos_k, sin_k = cos_t[:, q_width:], sin_t[:, q_width:]
    gain_grads = [0.0, 0.0]
    sums = [None] * MICRO

    arrived = []

    def expand(c, m, *earlier):
        carry = (n_tp, sums[m - 1][1]) if c == CHUNKS - 1 and m else ()
        hid, dgu, y_low, du_low, *got = feed_forward(
            after(u[m], *earlier), g[m], mlp_full[c], sub, sums[m], *carry
        )
        sums[m] = (y_low, du_low)
        arrived.extend(got)
        return hid, dgu

    def close(hids, dgus, last, *earlier):
        carry = (n_tp, sums[-1][1]) if last else ()
        grads, *got = outer_products(
            [after(u[0], *earlier)] + u[1:], g, hids, dgus, own_depth, sub, *carry
        )
        arrived.extend(got)
        return grads, lax.psum_scatter(grads, "dp", scatter_dimension=0, tiled=False)

    chunk_grads = []
    earlier = []
    for c in range(CHUNKS - 1):
        hids, dgus = [], []
        for m in batches:
            hid, dgu = expand(c, m, *earlier)
            qkv_near = move_qkv(qkv_near)
            earlier = [hid, qkv_near]
            hids.append(hid)
            dgus.append(dgu)
        grads, owned = close(hids, dgus, False, *earlier)
        qkv_near = move_qkv(qkv_near)
        earlier = [grads, qkv_near]
        chunk_grads.append(owned)

    d_middles, d_mid_lows, d_attends, all_rows = [], [], [], []
    hids, dgus = [], []
    for m in batches:
        hid, dgu = expand(CHUNKS - 1, m, *earlier)
        qkv_near = move_qkv(qkv_near)
        earlier = [hid, qkv_near]
        if m == 0:
            qkv_far = swap_cores(qkv_near)
        hids.append(hid)
        dgus.append(dgu)
    grads, owned = close(hids, dgus, True, *earlier, qkv_far)
    chunk_grads.append(owned)
    tail_sums = [after(sums[0], grads)] + sums[1:]
    d_qkv, mid_rows, out_rows, tok_low, gain_part = tail(
        n_dp,
        n_tp,
        group,
        tail_sums,
        arrived,
        seed[:, 0].reshape(own_rows, depth),
        middle,
        x[:, 0].reshape(own_rows, depth),
        gains_full,
        (out_near, out_far),
        (qkv_near, qkv_far),
        q,
        kv_all,
        qpos,
        kpos,
        cos_t,
        sin_t,
    )
    mlp_grads = [v.reshape(own_depth, -1) for v in chunk_grads]
    qkv_shares, out_shares = attn_weight_grads(
        attn_in,
        mid_rows.reshape(rows, depth),
        d_qkv.reshape(rows, q_width + kv_width),
        attended.reshape(rows, q_width),
        own_depth,
    )
    tok_rows, out_grad, gain_grad = finish(n_dp, n_tp, tok_low, out_shares, gain_part)
    qkv_shares = after(qkv_shares, out_grad, *chunk_grads)
    qkv_grad = lax.psum_scatter(qkv_shares, "dp", scatter_dimension=0, tiled=False)
    block_output, grad_tokens = spread(rank.astype(jnp.int32).reshape(1), out_rows, tok_rows)
    block_output = block_output.reshape(rows, depth)
    grad_tokens = grad_tokens.reshape(rows, depth)
    small = small_steps(
        qkv_grad.reshape(1, own_depth, q_width + kv_width),
        out_grad,
        gain_grad,
        mean_query,
        square_query,
        w_query,
        mean_keyval,
        square_keyval,
        w_keyval,
        mean_output,
        square_output,
        w_output,
        mean_gains,
        square_gains,
        norm_gains,
    )
    return (
        (block_output, grad_tokens)
        + small[:12]
        + step_from_chunks(
            mlp_grads, mean_gateup, square_gateup, w_gateup, sub, 0, False, weight_decay
        )
        + step_from_chunks(mlp_grads, mean_down, square_down, w_down, sub, 2, True, weight_decay)
        + small[12:]
    )


def solution(mesh):
    rows_first = P("dp", "tp")
    cols_last = P("tp", "dp")
    stacked = P(None, "dp", "tp")
    gains = P(None, "dp")
    token_rows = P("dp", None)
    placed = (
        (token_rows, token_rows, P())
        + (rows_first, rows_first, cols_last, stacked, cols_last, gains)
        + (rows_first,) * 4
        + (cols_last,) * 2
        + (stacked,) * 2
        + (cols_last,) * 2
        + (gains,) * 2
    )
    results = (
        (token_rows, token_rows)
        + (rows_first,) * 8
        + (cols_last,) * 4
        + (stacked,) * 4
        + (cols_last,) * 4
        + (gains,) * 4
    )
    return jax.shard_map(
        functools.partial(per_device, mesh.shape["dp"], mesh.shape["tp"]),
        mesh=mesh,
        in_specs=placed,
        out_specs=results,
        check_vma=False,
    )
```

```python
import functools

import jax
import jax.numpy as jnp
from jax import lax
from jax.experimental import pallas as pl
from jax.experimental.pallas import tpu as pltpu
from jax.sharding import PartitionSpec as P

HD = 64
CH = 64
SEQS = 4
MICRO = 2
STEP = 5
CHUNKS = 2
SUB = 512

norm_eps = 1e-05
rope_base = 500000.0
beta_one = 0.9
beta_two = 0.95
learn_rate = 0.01
weight_decay = 0.1
adam_eps = 1e-08
masked_score = -1e30

F32 = jnp.float32
BF16 = jnp.bfloat16
VMEM_LIMIT = 60 * 1024 * 1024
HINT = 20


def hint(flops, bytes_accessed, transcendentals):
    return pl.CostEstimate(
        flops=flops // HINT, bytes_accessed=bytes_accessed // HINT, transcendentals=transcendentals
    )


def lane_tables(positions, kinds):
    half_size = HD // 2
    frequencies = rope_base ** (-(jnp.arange(half_size, dtype=F32) * 2.0 / HD))
    angles = positions.astype(F32)[:, None] * frequencies[None, :]
    cos_half, sin_half = jnp.cos(angles), jnp.sin(angles)
    cos_head = jnp.concatenate([cos_half, cos_half], axis=-1)
    sin_head = jnp.concatenate([-sin_half, sin_half], axis=-1)
    ones, zeros = jnp.ones_like(cos_head), jnp.zeros_like(cos_head)
    cos_all, sin_all = [], []
    for kind in kinds:
        cos_all.append(cos_head if kind else ones)
        sin_all.append(sin_head if kind else zeros)
    return jnp.concatenate(cos_all, axis=-1), jnp.concatenate(sin_all, axis=-1)


def half_turn(values):
    width = values.shape[-1]
    axis = values.ndim - 1
    lane = lax.broadcasted_iota(jnp.int32, values.shape, axis)
    ahead = pltpu.roll(values, width - HD // 2, axis)
    behind = pltpu.roll(values, HD // 2, axis)
    return jnp.where(lane % HD < HD // 2, ahead, behind)


def mean_square_scale(values):
    return lax.rsqrt(jnp.mean(values * values, axis=-1, keepdims=True) + norm_eps)


def project_kernel(x_ref, gain_ref, w_ref, cos_ref, sin_ref, out_ref, *a_ref):
    x = x_ref[...].astype(F32)
    a = (x * mean_square_scale(x) * gain_ref[...].astype(F32)).astype(BF16)
    for ref in a_ref:
        ref[...] = a
    t = jnp.dot(a, w_ref[...], preferred_element_type=F32)
    out_ref[...] = (t * cos_ref[...] + half_turn(t) * sin_ref[...]).astype(BF16)


def project(x, gain, weights, place, cos_t, sin_t, keep):
    rows, depth = x.shape
    block, width = cos_t.shape
    whole = functools.partial(pl.BlockSpec, pipeline_mode=pl.Buffered(1))
    return pl.pallas_call(
        project_kernel,
        grid=(rows // block,),
        in_specs=[
            pl.BlockSpec((block, depth), lambda i: (i, 0)),
            pl.BlockSpec((1, depth), lambda i: (0, 0)),
            whole((depth, width), lambda i: (0, place)),
            pl.BlockSpec((block, width), lambda i: (0, 0)),
            pl.BlockSpec((block, width), lambda i: (0, 0)),
        ],
        out_specs=[pl.BlockSpec((block, width), lambda i: (i, 0))]
        + [pl.BlockSpec((block, depth), lambda i: (i, 0))] * keep,
        out_shape=[jax.ShapeDtypeStruct((rows, width), BF16)]
        + [jax.ShapeDtypeStruct((rows, depth), BF16)] * keep,
        compiler_params=pltpu.CompilerParams(vmem_limit_bytes=VMEM_LIMIT),
        cost_estimate=hint(
            flops=2 * rows * depth * width, bytes_accessed=4 * rows * depth, transcendentals=0
        ),
        name="project",
    )(x, gain, weights, cos_t, sin_t)


def stack_heads(block, group, upper):
    lane = lax.broadcasted_iota(jnp.int32, (block.shape[0], 2 * HD), 1)
    keep = (lane >= HD) if upper else (lane < HD)
    parts = []
    for head in range(group):
        pair = block[:, (head // 2) * 2 * HD : (head // 2 + 1) * 2 * HD].astype(F32)
        if (head % 2 == 1) != upper:
            pair = pltpu.roll(pair, HD, 1)
        parts.append(jnp.where(keep, pair, 0.0).astype(BF16))
    return jnp.concatenate(parts, axis=0)


def unstack_heads(stacked, group, upper):
    rows = stacked.shape[0] // group
    lane = lax.broadcasted_iota(jnp.int32, (rows, 2 * HD), 1)
    pairs = []
    for pair in range(group // 2):
        even = stacked[(2 * pair) * rows : (2 * pair + 1) * rows]
        odd = stacked[(2 * pair + 1) * rows : (2 * pair + 2) * rows]
        if upper:
            even = pltpu.roll(even, HD, 1)
        else:
            odd = pltpu.roll(odd, HD, 1)
        pairs.append(jnp.where(lane < HD, even, odd))
    return jnp.concatenate(pairs, axis=1)


def scores_and_probs(q_pad, keys, qpos, kpos, group):
    scores = (
        lax.dot_general(q_pad, keys, (((1,), (1,)), ((), ())), preferred_element_type=F32)
        * HD ** (-0.5)
    )
    rows = qpos.shape[0]
    blocked = kpos > qpos
    masked = [
        jnp.where(blocked, masked_score, scores[h * rows : (h + 1) * rows]) for h in range(group)
    ]
    scores = jnp.concatenate(masked, axis=0)
    exponent = jnp.exp(scores - jnp.max(scores, axis=-1, keepdims=True))
    return exponent * (1.0 / jnp.sum(exponent, axis=-1, keepdims=True))


def attend_kernel(group, qpos_ref, kpos_ref, q_ref, kv_ref, o_ref):
    keyvals = kv_ref[...].reshape(-1, 2 * HD)
    q_pad = stack_heads(q_ref[...].reshape(-1, group * HD), group, False)
    probs = scores_and_probs(q_pad, keyvals, qpos_ref[...], kpos_ref[...], group)
    out = jnp.dot(probs.astype(BF16), keyvals, preferred_element_type=F32)
    o_ref[...] = unstack_heads(out, group, True).astype(BF16).reshape(o_ref.shape)


def attend_back_kernel(
    group, qpos_ref, kpos_ref, cos_ref, sin_ref, q_ref, do_ref, kv_ref, dq_ref, dkv_ref
):
    keyvals = kv_ref[...].reshape(-1, 2 * HD)
    q_pad = stack_heads(q_ref[...].reshape(-1, group * HD), group, False)
    do_pad = stack_heads(do_ref[...].reshape(-1, group * HD), group, True)
    probs = scores_and_probs(q_pad, keyvals, qpos_ref[...], kpos_ref[...], group)
    d_probs = lax.dot_general(
        do_pad, keyvals, (((1,), (1,)), ((), ())), preferred_element_type=F32
    )
    d_scores = probs * (d_probs - jnp.sum(d_probs * probs, axis=-1, keepdims=True))
    ds_low = d_scores.astype(BF16) * HD ** (-0.5)
    dq = jnp.dot(ds_low, keyvals, preferred_element_type=F32)
    dq = unstack_heads(dq, group, False)
    dq = dq * cos_ref[...] + half_turn(dq * sin_ref[...])
    dq_ref[...] = dq.astype(BF16).reshape(dq_ref.shape)
    contract = (((0,), (0,)), ((), ()))
    d_keyvals = lax.dot_general(
        ds_low, q_pad, contract, preferred_element_type=F32
    ) + lax.dot_general(probs.astype(BF16), do_pad, contract, preferred_element_type=F32)
    dkv_ref[...] = d_keyvals.astype(BF16).reshape(dkv_ref.shape)


def attention_specs(qkv_heads, n_dp, span_rows, group):
    q_spec = pl.BlockSpec((1, 1, span_rows, group * HD), lambda m, s, h: (m, s, 0, h))
    kv_spec = pl.BlockSpec(
        (n_dp, 1, 1, span_rows, 2 * HD), lambda m, s, h: (0, m, s, 0, h)
    )
    pos_q = pl.BlockSpec((span_rows, 1), lambda m, s, h: (0, 0))
    pos_k = pl.BlockSpec((1, n_dp * span_rows), lambda m, s, h: (0, 0))
    return q_spec, kv_spec, pos_q, pos_k


def attend(qpos, kpos, q, kv, group):
    micro, seqs, span_rows, width = q.shape
    n_dp, heads = kv.shape[0], width // (group * HD)
    q_spec, kv_spec, pos_q, pos_k = attention_specs(heads, n_dp, span_rows, group)
    return pl.pallas_call(
        functools.partial(attend_kernel, group),
        grid=(micro, seqs, heads),
        in_specs=[pos_q, pos_k, q_spec, kv_spec],
        out_specs=q_spec,
        out_shape=jax.ShapeDtypeStruct(q.shape, BF16),
        compiler_params=pltpu.CompilerParams(vmem_limit_bytes=VMEM_LIMIT),
        cost_estimate=hint(
            flops=16 * micro * seqs * span_rows * width * n_dp * span_rows,
            bytes_accessed=4 * q.size + 2 * kv.size,
            transcendentals=0,
        ),
        name="attend",
    )(qpos, kpos, q, kv)


def attend_back(qpos, kpos, cos_q, sin_q, q, d_out, kv, group):
    micro, seqs, span_rows, width = q.shape
    n_dp, heads = kv.shape[0], width // (group * HD)
    q_spec, kv_spec, pos_q, pos_k = attention_specs(heads, n_dp, span_rows, group)
    table = pl.BlockSpec((span_rows, group * HD), lambda m, s, h: (0, 0))
    return pl.pallas_call(
        functools.partial(attend_back_kernel, group),
        grid=(micro, seqs, heads),
        in_specs=[pos_q, pos_k, table, table, q_spec, q_spec, kv_spec],
        out_specs=[q_spec, kv_spec],
        out_shape=[
            jax.ShapeDtypeStruct(q.shape, BF16),
            jax.ShapeDtypeStruct(kv.shape, BF16),
        ],
        compiler_params=pltpu.CompilerParams(vmem_limit_bytes=VMEM_LIMIT),
        cost_estimate=hint(
            flops=40 * micro * seqs * span_rows * width * n_dp * span_rows,
            bytes_accessed=6 * q.size + 4 * kv.size,
            transcendentals=0,
        ),
        name="attend_back",
    )(qpos, kpos, cos_q, sin_q, q, d_out, kv)


def norm_back(d_normed, normed, scale):
    return scale * (d_normed - normed * jnp.mean(d_normed * normed, axis=-1, keepdims=True))


def adam_update(gradient, old_mean, square, weight, decay_factor):
    moment = beta_one * old_mean + (1.0 - beta_one) * gradient
    spread = beta_two * square + (1.0 - beta_two) * gradient * gradient
    change = -learn_rate * (
        moment / (1.0 - beta_one**STEP) / (jnp.sqrt(spread / (1.0 - beta_two**STEP)) + adam_eps)
        + decay_factor * weight
    )
    return (moment, spread, change)


def dot(left, right):
    return jnp.dot(left, right, preferred_element_type=F32)


def dot_nt(left, right):
    return lax.dot_general(left, right, (((1,), (1,)), ((), ())), preferred_element_type=F32)


def dot_tn(left, right):
    return lax.dot_general(left, right, (((0,), (0,)), ((), ())), preferred_element_type=F32)


def paired(index, k):
    bit = 1
    while bit <= k:
        if k & bit:
            index = index + bit - 2 * bit * ((index // bit) % 2)
        bit *= 2
    return index


def remote(src, dst, send, recv, device):
    return pltpu.make_async_remote_copy(
        src_ref=src,
        dst_ref=dst,
        send_sem=send,
        recv_sem=recv,
        device_id=device,
        device_id_type=pl.DeviceIdType.MESH,
    )


def meet(peers):
    barrier = pltpu.get_barrier_semaphore()
    for peer in peers:
        pl.semaphore_signal(barrier, inc=1, device_id=peer, device_id_type=pl.DeviceIdType.MESH)
    pl.semaphore_wait(barrier, len(peers))


def start(moves):
    for move in moves:
        move.start()


def arrive(moves):
    for move in moves:
        move.wait_recv()


def sent(moves):
    for move in moves:
        move.wait_send()


class LineSum:

    def __init__(self, line, place, core, tp, value, send, got, send_sem, recv_sem):
        self.value, self.send, self.got = value, send, got
        self.slots, self.moves = [], []
        count, step = 0, 0
        while (1 << step) < line:
            size = line >> (step + 1)
            self.slots.append(list(range(count, count + size)))
            partner = (paired(place, 1 << step) * 2 + core, tp)
            self.moves.append(
                [
                    remote(send.at[i], got.at[i], send_sem.at[i], recv_sem.at[i], partner)
                    for i in self.slots[-1]
                ]
            )
            count, step = count + size, step + 1
        self.steps = step

    def held(self, r, step):
        total = self.value(r)
        for s in range(step):
            total = total + self.got[self.slots[s][r >> (s + 1)]].astype(F32)
        return total

    def begin(self, step):
        if step:
            arrive(self.moves[step - 1])
        for j, i in enumerate(self.slots[step]):
            self.send[i] = self.held((1 << step) | (j << (step + 1)), step).astype(BF16)
        start(self.moves[step])

    def total(self):
        arrive(self.moves[-1])
        return self.held(0, self.steps)

    def close(self):
        for moves in self.moves:
            sent(moves)


def row_moves(remote, rank, n_tp, low, got, send, recv):
    first = [
        [
            remote(low.at[m], got.at[m, k], send.at[m, k], recv.at[m, k], rank(k))
            for k in range(1, n_tp)
            if k != 3
        ]
        for m in range(MICRO)
    ]
    relay = [
        remote(got.at[m, 1 + m], got.at[m, 3], send.at[m, 3], recv.at[m, 3], rank(2 - m))
        for m in range(MICRO)
    ]
    return first, relay


def relay_rows(first, relay):
    for m in range(MICRO):
        first[m][m].wait_recv()
        relay[m].start()


def close_rows(first, relay):
    for m in range(MICRO):
        for i, move in enumerate(first[m]):
            if i != m:
                move.wait_recv()
            move.wait_send()
        relay[m].wait_recv()
        relay[m].wait_send()


def carried(n_tp, src, got, send, recv):
    dp, tp = lax.axis_index("dp"), lax.axis_index("tp")
    rows = got.shape[1]
    return [
        remote(
            src.at[pl.ds(k * rows, rows)],
            got.at[k],
            send.at[k],
            recv.at[k],
            (dp, paired(tp, k)),
        )
        for k in range(1, n_tp)
    ]


def carry_start(n_tp, *move):
    dp, tp = lax.axis_index("dp"), lax.axis_index("tp")
    meet([(dp, paired(tp, k)) for k in range(1, n_tp)])
    start(carried(n_tp, *move))


def carry_end(n_tp, *move):
    moves = carried(n_tp, *move)
    arrive(moves)
    sent(moves)


def gated_kernel(n_tp, last, steps, u_ref, g_ref, w_ref, *refs):
    refs = list(refs)
    move = None
    if n_tp:
        send, recv = refs[-2:]
        src, got = refs.pop(2), refs[6]
        move = (src, got, send, recv)
        refs = refs[:6] + refs[7:-2]
    if last:
        y_old, du_old = refs[:2]
        refs = refs[2:]
    hid_ref, dgu_ref, y_out, du_out, y_sum, du_sum, y_low, du_low, sem = refs
    step = pl.program_id(0)
    depth = w_ref.shape[0]
    sub = hid_ref.shape[1]
    cols = min(512, depth)

    @pl.when(step == 0)
    def _():
        if move:
            carry_start(n_tp, *move)
        y_sum[...] = jnp.zeros_like(y_sum)
        du_sum[...] = jnp.zeros_like(du_sum)
        if last:
            pltpu.make_async_copy(y_old, y_low, sem.at[0]).start()
            pltpu.make_async_copy(du_old, du_low, sem.at[1]).start()

    gate_proj = dot(u_ref[...], w_ref[:, :sub])
    up_proj = dot(u_ref[...], w_ref[:, sub : 2 * sub])
    sigmoid_gate = jax.nn.sigmoid(gate_proj)
    silu_gate = gate_proj * sigmoid_gate
    hid_ref[...] = (silu_gate * up_proj).astype(BF16)
    d_hidden = dot(g_ref[...], w_ref[:, 2 * sub :])
    d_gate = d_hidden * up_proj * sigmoid_gate * (1.0 + gate_proj * (1.0 - sigmoid_gate))
    dgu_ref[:, :sub] = d_gate.astype(BF16)
    dgu_ref[:, sub:] = (d_hidden * silu_gate).astype(BF16)
    for start in range(0, depth, cols):
        part = slice(start, start + cols)
        du_sum[:, part] += dot_nt(dgu_ref[...], w_ref[part, : 2 * sub])
        y_sum[:, part] += dot_nt(hid_ref[...], w_ref[part, 2 * sub :])

    @pl.when(step == steps - 1)
    def _():
        copy_y = pltpu.make_async_copy(y_low, y_out, sem.at[0])
        copy_du = pltpu.make_async_copy(du_low, du_out, sem.at[1])
        if last:
            pltpu.make_async_copy(y_old, y_low, sem.at[0]).wait()
            pltpu.make_async_copy(du_old, du_low, sem.at[1]).wait()
            du_low[...] = (du_sum[...] + du_low[...].astype(F32)).astype(BF16)
            copy_du.start()
            y_low[...] = (y_sum[...] + y_low[...].astype(F32)).astype(BF16)
        else:
            du_low[...] = du_sum[...].astype(BF16)
            copy_du.start()
            y_low[...] = y_sum[...].astype(BF16)
        copy_y.start()
        copy_du.wait()
        copy_y.wait()
        if move:
            carry_end(n_tp, *move)


def carrier_params(n_tp, collective_id):
    if not n_tp:
        return pltpu.CompilerParams(vmem_limit_bytes=VMEM_LIMIT)
    return pltpu.CompilerParams(
        collective_id=collective_id, has_side_effects=True, vmem_limit_bytes=VMEM_LIMIT
    )


def feed_forward(u, g, weights, sub, sums, n_tp=0, carry=None):
    rows, depth = u.shape
    steps = weights.shape[1] // (3 * sub)
    last = sums is not None
    whole = functools.partial(pl.BlockSpec, pipeline_mode=pl.Buffered(1))
    anywhere = pl.BlockSpec(memory_space=pl.ANY)
    return pl.pallas_call(
        functools.partial(gated_kernel, n_tp, last, steps),
        grid=(steps,),
        in_specs=[
            whole((rows, depth), lambda j: (0, 0)),
            whole((rows, depth), lambda j: (0, 0)),
            pl.BlockSpec((depth, 3 * sub), lambda j: (0, j)),
        ]
        + ([anywhere, anywhere] if last else [])
        + ([anywhere] if n_tp else []),
        out_specs=[
            pl.BlockSpec((rows, sub), lambda j: (0, j)),
            pl.BlockSpec((rows, 2 * sub), lambda j: (0, j)),
            anywhere,
            anywhere,
        ]
        + ([anywhere] if n_tp else []),
        out_shape=[
            jax.ShapeDtypeStruct((rows, steps * sub), BF16),
            jax.ShapeDtypeStruct((rows, 2 * steps * sub), BF16),
            jax.ShapeDtypeStruct((rows, depth), BF16),
            jax.ShapeDtypeStruct((rows, depth), BF16),
        ]
        + ([jax.ShapeDtypeStruct((n_tp, rows // n_tp, depth), BF16)] if n_tp else []),
        scratch_shapes=[
            pltpu.VMEM((rows, depth), F32),
            pltpu.VMEM((rows, depth), F32),
            pltpu.VMEM((rows, depth), BF16),
            pltpu.VMEM((rows, depth), BF16),
            pltpu.SemaphoreType.DMA((2,)),
        ]
        + ([pltpu.SemaphoreType.DMA((n_tp,))] * 2 if n_tp else []),
        compiler_params=carrier_params(n_tp, 3),
        cost_estimate=hint(
            flops=12 * rows * depth * steps * sub,
            bytes_accessed=2 * weights.size + 8 * rows * depth,
            transcendentals=0,
        ),
        name="feed_forward",
    )(u, g, weights, *(sums if last else ()), *([carry] if n_tp else []))


def outer_kernel(n_tp, batches, sub, steps, *refs):
    u_refs, g_refs = refs[:batches], refs[batches : 2 * batches]
    hid_refs, dgu_refs = refs[2 * batches : 3 * batches], refs[3 * batches : 4 * batches]
    refs = refs[4 * batches :]
    move = None
    if n_tp:
        src, out_ref, got, send, recv = refs
        move = (src, got, send, recv)

        @pl.when(pl.program_id(0) == 0)
        def _():
            carry_start(n_tp, *move)

    else:
        (out_ref,) = refs
    for j in range(steps):
        both = slice(2 * j * sub, 2 * (j + 1) * sub)
        one = slice(j * sub, (j + 1) * sub)
        total = dot_tn(u_refs[0][...], dgu_refs[0][:, both])
        for m in range(1, batches):
            total += dot_tn(u_refs[m][...], dgu_refs[m][:, both])
        out_ref[0, :, 3 * j * sub : 3 * j * sub + 2 * sub] = total.astype(BF16)
        total = dot_tn(g_refs[0][...], hid_refs[0][:, one])
        for m in range(1, batches):
            total += dot_tn(g_refs[m][...], hid_refs[m][:, one])
        out_ref[0, :, 3 * j * sub + 2 * sub : 3 * (j + 1) * sub] = total.astype(BF16)
    if n_tp:

        @pl.when(pl.program_id(0) == pl.num_programs(0) - 1)
        def _():
            carry_end(n_tp, *move)


def outer_products(us, gs, hids, dgus, own, sub, n_tp=0, carry=None):
    batches = len(us)
    rows, depth = us[0].shape
    n_dp = depth // own
    width = hids[0].shape[1]
    steps = width // sub
    whole = functools.partial(pl.BlockSpec, pipeline_mode=pl.Buffered(1))
    column = pl.BlockSpec((rows, own), lambda i: (0, i))
    anywhere = pl.BlockSpec(memory_space=pl.ANY)
    return pl.pallas_call(
        functools.partial(outer_kernel, n_tp, batches, sub, steps),
        grid=(n_dp,),
        in_specs=[column] * (2 * batches)
        + [whole((rows, width), lambda i: (0, 0))] * batches
        + [whole((rows, 2 * width), lambda i: (0, 0))] * batches
        + ([anywhere] if n_tp else []),
        out_specs=[pl.BlockSpec((1, own, 3 * width), lambda i: (i, 0, 0))]
        + ([anywhere] if n_tp else []),
        out_shape=[jax.ShapeDtypeStruct((n_dp, own, 3 * width), BF16)]
        + ([jax.ShapeDtypeStruct((n_tp, rows // n_tp, depth), BF16)] if n_tp else []),
        scratch_shapes=[pltpu.SemaphoreType.DMA((n_tp,))] * 2 if n_tp else [],
        compiler_params=carrier_params(n_tp, 4),
        cost_estimate=hint(
            flops=6 * rows * batches * depth * width,
            bytes_accessed=6 * depth * width,
            transcendentals=0,
        ),
        name="outer_products",
    )(*us, *gs, *hids, *dgus, *([carry] if n_tp else []))


def attn_grad_kernel(a_ref, m_ref, qkv_ref, att_ref, out_qkv, out_output):
    out_qkv[0] = dot_tn(a_ref[...], qkv_ref[...]).astype(BF16)
    out_output[0] = dot_tn(m_ref[...], att_ref[...]).astype(BF16)


def attn_weight_grads(attn_in, d_mid, d_qkv, attended, own):
    rows, depth = attn_in.shape
    column = pl.BlockSpec((rows, own), lambda i: (0, i))
    whole = functools.partial(pl.BlockSpec, pipeline_mode=pl.Buffered(1))
    widths = (d_qkv.shape[1], attended.shape[1])
    return pl.pallas_call(
        attn_grad_kernel,
        grid=(depth // own,),
        in_specs=[column, column] + [whole((rows, w), lambda i: (0, 0)) for w in widths],
        out_specs=[pl.BlockSpec((1, own, w), lambda i: (i, 0, 0)) for w in widths],
        out_shape=[jax.ShapeDtypeStruct((depth // own, own, w), BF16) for w in widths],
        compiler_params=pltpu.CompilerParams(vmem_limit_bytes=VMEM_LIMIT),
        cost_estimate=hint(
            flops=2 * rows * depth * sum(widths), bytes_accessed=4 * rows * depth, transcendentals=0
        ),
        name="attn_weight_grads",
    )(attn_in, d_mid, d_qkv, attended)


def small_steps_kernel(qkv_ref, out_ref, gain_ref, *refs):
    states, results = refs[:12], refs[12:]
    q_width = states[0].shape[1]
    gradients = (
        lambda: qkv_ref[0, :, :q_width].astype(F32),
        lambda: qkv_ref[0, :, q_width:].astype(F32),
        lambda: out_ref[...].T,
        lambda: gain_ref[...],
    )
    for i, read in enumerate(gradients):
        gradient = read()
        mean_ref, square_ref, weight_ref = states[3 * i : 3 * i + 3]
        decay = weight_decay if i < 3 else 0.0
        moment, spread, change = adam_update(
            gradient, mean_ref[...], square_ref[...], weight_ref[...].astype(F32), decay
        )
        for ref, value in zip(results[4 * i : 4 * i + 4], (gradient, moment, spread, change)):
            ref[...] = value


def small_steps(qkv_grad, out_grad, gain_grad, *states):
    vmem = pl.BlockSpec(memory_space=pltpu.VMEM)
    shapes = [jax.ShapeDtypeStruct(states[3 * i].shape, F32) for i in range(4)]
    return tuple(
        pl.pallas_call(
            small_steps_kernel,
            in_specs=[vmem] * 15,
            out_specs=[vmem] * 16,
            out_shape=[shape for shape in shapes for _ in range(4)],
            compiler_params=pltpu.CompilerParams(vmem_limit_bytes=VMEM_LIMIT),
            name="small_steps",
        )(qkv_grad, out_grad, gain_grad, *states)
    )


def step_kernel(turned, decay, steps, chunks, *refs):
    grads = refs[:chunks]
    mean_ref, square_ref, weight_ref, grad_ref, moment_ref, spread_ref, update_ref = refs[chunks:]
    place = pl.program_id(1)
    for c in range(chunks):

        @pl.when(place // steps == c)
        def _(c=c):
            gradient = grads[c][...].astype(F32)
            if turned:
                gradient = gradient.T
            gradient = gradient.reshape(grad_ref.shape)
            moment, spread, change = adam_update(
                gradient, mean_ref[...], square_ref[...], weight_ref[...].astype(F32), decay
            )
            grad_ref[...] = gradient
            moment_ref[...] = moment
            spread_ref[...] = spread
            update_ref[...] = change


def step_from_chunks(grads, old_mean, square, weight, sub, offset, turned, decay):
    chunks, own = len(grads), grads[0].shape[0]
    steps = grads[0].shape[1] // (3 * sub)

    def grad_spec(c):
        def index(i, p):
            j = jnp.clip(p - c * steps, 0, steps - 1)
            return (0, 3 * j + i + offset)

        return pl.BlockSpec((own, sub), index)

    if turned:
        lead, spec = 1, pl.BlockSpec((sub, own), lambda i, p: (p, 0))
    else:
        lead, spec = old_mean.shape[0], pl.BlockSpec((1, own, sub), lambda i, p: (i, 0, p))
    return tuple(
        pl.pallas_call(
            functools.partial(step_kernel, turned, decay, steps, chunks),
            grid=(lead, chunks * steps),
            in_specs=[grad_spec(c) for c in range(chunks)] + [spec] * 3,
            out_specs=[spec] * 4,
            out_shape=[jax.ShapeDtypeStruct(old_mean.shape, F32)] * 4,
            compiler_params=pltpu.CompilerParams(vmem_limit_bytes=VMEM_LIMIT),
            cost_estimate=hint(
                flops=20 * old_mean.size, bytes_accessed=28 * old_mean.size, transcendentals=0
            ),
            name="weight_step",
        )(*grads, old_mean, square, weight)
    )


def finish_kernel(
    n_dp,
    n_tp,
    tok_low,
    share_ref,
    gain_ref,
    tok_rows,
    grad_ref,
    gain_own,
    met,
    z_send,
    z_got,
    ranks_got,
    gain_sum,
    gain_got,
    local_sem,
    tok_s,
    tok_r,
    core_s,
    core_r,
    z_s,
    z_r,
    rank_s,
    rank_r,
    gain_s,
    gain_r,
):
    line = n_dp // 2
    own = share_ref.shape[1]
    dp, tp = lax.axis_index("dp"), lax.axis_index("tp")
    place, core = dp // 2, dp % 2

    def rank(k):
        return (dp, paired(tp, k))

    def columns(index):
        return pl.ds(pl.multiple_of(index * own, own), own)

    first, relay = row_moves(remote, rank, n_tp, tok_low, tok_rows, tok_s, tok_r)
    keep = [
        pltpu.make_async_copy(tok_low.at[m], tok_rows.at[m, 0], local_sem.at[m])
        for m in range(MICRO)
    ]
    core_moves = [
        remote(
            share_ref.at[z * 2 + 1 - core],
            met.at[z],
            core_s.at[z],
            core_r.at[z],
            (place * 2 + 1 - core, tp),
        )
        for z in range(line)
    ]
    sums = LineSum(
        line,
        place,
        core,
        tp,
        lambda r: share_ref[paired(place, r) * 2 + core].astype(F32)
        + met[paired(place, r)].astype(F32),
        z_send,
        z_got,
        z_s,
        z_r,
    )
    rank_moves = [
        remote(gain_ref, ranks_got.at[k], rank_s.at[k], rank_r.at[k], rank(k))
        for k in range(1, n_tp)
    ]
    gain_moves = [
        remote(
            gain_sum.at[:, columns(paired(dp, j))],
            gain_got.at[j],
            gain_s.at[j],
            gain_r.at[j],
            (paired(dp, j), tp),
        )
        for j in range(1, n_dp)
    ]

    meet([rank(k) for k in range(1, n_tp)] + [(paired(dp, j), tp) for j in range(1, n_dp)])
    start(core_moves)
    start(rank_moves)
    for moves in first:
        start(moves)
    start(keep)
    arrive(core_moves)
    sums.begin(0)
    arrive(rank_moves)
    total = gain_ref[...]
    for k in range(1, n_tp):
        total = total + ranks_got[k]
    gain_sum[...] = total
    start(gain_moves)
    for step in range(1, sums.steps):
        sums.begin(step)
    relay_rows(first, relay)
    arrive(gain_moves)
    total = gain_sum[:, columns(dp)]
    for j in range(1, n_dp):
        total = total + gain_got[j]
    gain_own[...] = total
    grad_ref[...] = sums.total()
    close_rows(first, relay)
    sums.close()
    for moves in (core_moves, rank_moves, gain_moves):
        sent(moves)
    for copy in keep:
        copy.wait()


def finish(n_dp, n_tp, tok_low, shares, gain_part):
    micro, rows, depth = tok_low.shape
    _, own, width = shares.shape
    line = n_dp // 2
    anywhere = pl.BlockSpec(memory_space=pl.ANY)
    vmem = pl.BlockSpec(memory_space=pltpu.VMEM)
    dma = pltpu.SemaphoreType.DMA
    return pl.pallas_call(
        functools.partial(finish_kernel, n_dp, n_tp),
        in_specs=[anywhere, vmem, vmem],
        out_specs=[anywhere, vmem, vmem],
        out_shape=[
            jax.ShapeDtypeStruct((micro, n_tp, rows, depth), BF16),
            jax.ShapeDtypeStruct((own, width), F32),
            jax.ShapeDtypeStruct((2, own), F32),
        ],
        scratch_shapes=[
            pltpu.VMEM((line, own, width), BF16),
            pltpu.VMEM((line, own, width), BF16),
            pltpu.VMEM((line, own, width), BF16),
            pltpu.VMEM((n_tp, 2, depth), F32),
            pltpu.VMEM((2, depth), F32),
            pltpu.VMEM((n_dp, 2, own), F32),
            dma((micro,)),
            dma((micro, n_tp)),
            dma((micro, n_tp)),
            dma((line,)),
            dma((line,)),
            dma((line,)),
            dma((line,)),
            dma((n_tp,)),
            dma((n_tp,)),
            dma((n_dp,)),
            dma((n_dp,)),
        ],
        compiler_params=pltpu.CompilerParams(
            collective_id=1, has_side_effects=True, vmem_limit_bytes=VMEM_LIMIT
        ),
        cost_estimate=hint(flops=10**10, bytes_accessed=10**8, transcendentals=0),
        name="finish",
    )(tok_low, shares, gain_part)


def tail_kernel(n_dp, n_tp, group, *refs):
    (
        du_refs,
        y_refs,
        du_ins,
        seed_ref,
        middle_ref,
        x_ref,
        gains_ref,
        out_refs,
        qkv_refs,
        q_ref,
        kv_ref,
        qpos_ref,
        kpos_ref,
        cos_ref,
        sin_ref,
        d_qkv_ref,
        mid_rows,
        out_rows,
        tok_low,
        gain_ref,
    ) = (refs[0:2], refs[2:4], refs[4:6]) + refs[6:10] + (refs[10:12], refs[12:14]) + refs[14:25]
    (
        weights,
        du_got,
        y_got,
        own_mid,
        mid_low,
        block_low,
        do_send,
        do_got,
        shares,
        met,
        z_send,
        z_got,
        heads_got,
        local_sem,
        block_s,
        block_r,
        y_s,
        y_r,
        mid_s,
        mid_r,
        do_s,
        do_r,
        core_s,
        core_r,
        z_s,
        z_r,
        heads_s,
        heads_r,
    ) = refs[25:]
    line = n_dp // 2
    batches = range(MICRO)
    others = range(1, n_tp)
    dp, tp = lax.axis_index("dp"), lax.axis_index("tp")
    place, core = dp // 2, dp % 2
    depth = middle_ref.shape[1]
    rows = mid_low.shape[1]
    seq_rows = q_ref.shape[2]
    q_width = q_ref.shape[3]
    kv_width = kv_ref.shape[4]
    width = q_width + kv_width
    half = depth // 2

    def rank(k):
        return (dp, paired(tp, k))

    def spot(k):
        return (paired(place, k) * 2 + core, tp)

    other_core = (place * 2 + 1 - core, tp)

    def block(k):
        return pl.ds(k * rows, rows)

    y_moves = [
        [
            remote(y_refs[m].at[block(k)], y_got.at[m, k], y_s.at[m, k], y_r.at[m, k], rank(k))
            for k in others
        ]
        for m in batches
    ]

    block_first, block_relay = row_moves(
        remote, rank, n_tp, block_low, out_rows, block_s, block_r
    )
    mid_first, mid_relay = row_moves(remote, rank, n_tp, mid_low, mid_rows, mid_s, mid_r)
    do_moves = [
        [
            remote(
                do_send.at[m, k], do_got.at[m, block(k)], do_s.at[m, k], do_r.at[m, k], rank(k)
            )
            for k in others
        ]
        for m in batches
    ]
    core_moves = [
        remote(shares.at[m, 1 - core], met.at[m], core_s.at[m], core_r.at[m], other_core)
        for m in batches
    ]
    key_sums = [
        LineSum(
            line,
            place,
            core,
            tp,
            lambda r, m=m: shares[m, core, paired(place, r)].astype(F32)
            + met[m, paired(place, r)].astype(F32),
            z_send.at[m],
            z_got.at[m],
            z_s.at[m],
            z_r.at[m],
        )
        for m in batches
    ]
    heads_moves = [
        [
            remote(
                d_qkv_ref.at[m, block(k)],
                heads_got.at[m, k],
                heads_s.at[m, k],
                heads_r.at[m, k],
                rank(k),
            )
            for k in others
        ]
        for m in batches
    ]

    own_copies = [
        pltpu.make_async_copy(ref.at[pl.ds(0, rows)], got.at[m, 0], local_sem.at[i, m])
        for i, (pair, got) in enumerate(((du_refs, du_got), (y_refs, y_got)))
        for m, ref in enumerate(pair)
    ]
    own_copies += [
        pltpu.make_async_copy(
            ref.at[pl.ds(1, n_tp - 1)], du_got.at[m, pl.ds(1, n_tp - 1)], local_sem.at[4, m]
        )
        for m, ref in enumerate(du_ins)
    ]
    keep_block = [
        pltpu.make_async_copy(block_low.at[m], out_rows.at[m, 0], local_sem.at[5, m])
        for m in batches
    ]
    load_out = [
        pltpu.make_async_copy(
            ref, weights.at[side, :, pl.ds(0, n_tp * q_width)], local_sem.at[6, side]
        )
        for side, ref in enumerate(out_refs)
    ]
    load_qkv = [
        pltpu.make_async_copy(ref, weights.at[side], local_sem.at[2, side])
        for side, ref in enumerate(qkv_refs)
    ]
    keep = [
        pltpu.make_async_copy(mid_low.at[m], mid_rows.at[m, 0], local_sem.at[3, m])
        for m in batches
    ]

    meet([rank(k) for k in others] + [other_core] + [spot(k) for k in range(1, line)])
    start(own_copies)
    start(load_out)
    gain_one = gains_ref[0:1, :].astype(F32)
    gain_two = gains_ref[1:2, :].astype(F32)
    gain_ref[...] = jnp.zeros_like(gain_ref)

    def total_of(got, m):
        total = got[m, 0].astype(F32)
        for k in others:
            total = total + got[m, k].astype(F32)
        return total

    for copy in own_copies:
        copy.wait()
    for m in batches:
        part = slice(m * rows, (m + 1) * rows)
        d_mixed = total_of(du_got, m)
        middle = middle_ref[part, :]
        scale = mean_square_scale(middle)
        normed = middle * scale
        gain_ref[1:2, :] += jnp.sum(d_mixed * normed, axis=0, keepdims=True)
        d_middle = seed_ref[part, :].astype(F32) + norm_back(d_mixed * gain_two, normed, scale)
        own_mid[m] = d_middle
        mid_low[m] = d_middle.astype(BF16)
        if m == 0:
            for copy in load_out:
                copy.wait()
        near_cols = pl.ds(pl.multiple_of(core * half, half), half)
        far_cols = pl.ds(pl.multiple_of((1 - core) * half, half), half)
        near, far = mid_low[m, :, near_cols], mid_low[m, :, far_cols]
        for k in range(n_tp):
            lanes = slice(k * q_width, (k + 1) * q_width)
            rows_out = (dot(near, weights[0, :, lanes]) + dot(far, weights[1, :, lanes])).astype(
                BF16
            )
            if k == 0:
                do_got[m, 0:rows, :] = rows_out
            else:
                do_send[m, k] = rows_out
        start(do_moves[m])
    start(load_qkv)
    for m in batches:
        start(y_moves[m])

    def attend_back_seq(m, s):
        seq = pl.ds(s * seq_rows, seq_rows)
        for h in range(kv_width // (2 * HD)):
            pair = slice(h * 2 * HD, (h + 1) * 2 * HD)
            keyvals = kv_ref[:, m, s, :, pair].reshape(-1, 2 * HD)
            grads = None
            for part in range(group // 2):
                lanes = slice((h * group + 2 * part) * HD, (h * group + 2 * part + 2) * HD)
                q_pad = stack_heads(q_ref[m, s, :, lanes], 2, False)
                do_pad = stack_heads(do_got[m, seq, lanes], 2, True)
                probs = scores_and_probs(q_pad, keyvals, qpos_ref[...], kpos_ref[...], 2)
                d_probs = dot_nt(do_pad, keyvals)
                d_scores = probs * (d_probs - jnp.sum(d_probs * probs, axis=-1, keepdims=True))
                ds_low = d_scores.astype(BF16) * HD ** (-0.5)
                dq = unstack_heads(dot(ds_low, keyvals), 2, False)
                cos_q, sin_q = cos_ref[:, 0 : 2 * HD], sin_ref[:, 0 : 2 * HD]
                dq = dq * cos_q + half_turn(dq * sin_q)
                d_qkv_ref[m, seq, lanes] = dq.astype(BF16)
                term = dot_tn(ds_low, q_pad) + dot_tn(probs.astype(BF16), do_pad)
                grads = term if grads is None else grads + term
            grads = grads.astype(BF16)
            for i in range(n_dp):
                shares[m, i % 2, i // 2, seq, pair] = grads[i * seq_rows : (i + 1) * seq_rows]

    def attend_back_range(m, low, high):
        @pl.loop(low, high)
        def _(s):
            attend_back_seq(m, s)

    def send_along(m):
        arrive([core_moves[m]])
        key_sums[m].begin(0)

    def advance(m):
        for step in range(1, key_sums[m].steps):
            key_sums[m].begin(step)

    def close_keys(m):
        total = key_sums[m].total()
        cos_k, sin_k = cos_ref[:, q_width:], sin_ref[:, q_width:]
        for s in range(SEQS):
            seq = slice(s * seq_rows, (s + 1) * seq_rows)
            grad = total[seq]
            d_qkv_ref[m, seq, q_width:] = (grad * cos_k + half_turn(grad * sin_k)).astype(BF16)
        start(heads_moves[m])

    def close_block(m):
        arrive(y_moves[m])
        part = slice(m * rows, (m + 1) * rows)
        block_low[m] = (middle_ref[part, :] + total_of(y_got, m)).astype(BF16)
        start(block_first[m])
        keep_block[m].start()

    def close_tokens(m):
        arrive(heads_moves[m])
        part = slice(m * rows, (m + 1) * rows)
        heads = [d_qkv_ref[m, 0:rows, :]] + [heads_got[m, k] for k in others]
        sides = []
        for side in range(2):
            total = dot_nt(heads[0], weights[side, :, 0:width])
            for k in others:
                total = total + dot_nt(heads[k], weights[side, :, k * width : (k + 1) * width])
            sides.append(total)
        d_act = jnp.where(
            core == 0,
            jnp.concatenate(sides, axis=1),
            jnp.concatenate(sides[::-1], axis=1),
        )
        x_part = x_ref[part, :].astype(F32)
        scale = mean_square_scale(x_part)
        normed = x_part * scale
        gain_ref[0:1, :] += jnp.sum(d_act * normed, axis=0, keepdims=True)
        tok_low[m] = (own_mid[m] + norm_back(d_act * gain_one, normed, scale)).astype(BF16)

    arrive(do_moves[0])
    attend_back_range(0, 0, SEQS)
    core_moves[0].start()
    for m in batches:
        start(mid_first[m])
        keep[m].start()
    arrive(do_moves[1])
    attend_back_range(1, 0, SEQS // 2)
    send_along(0)
    attend_back_range(1, SEQS // 2, SEQS)
    core_moves[1].start()
    advance(0)
    for copy in load_qkv:
        copy.wait()
    send_along(1)
    close_block(0)
    close_keys(0)
    advance(1)
    close_block(1)
    relay_rows(mid_first, mid_relay)
    close_tokens(0)
    close_keys(1)
    relay_rows(block_first, block_relay)
    close_tokens(1)
    close_rows(mid_first, mid_relay)
    close_rows(block_first, block_relay)
    for m in batches:
        key_sums[m].close()
        for moves in (y_moves[m], do_moves[m], [core_moves[m]], heads_moves[m]):
            sent(moves)
        keep[m].wait()
        keep_block[m].wait()


def tail(
    n_dp, n_tp, group, sums, arrived, seed, middle, x, gains, out_w, qkv_w, q, kv, qpos, kpos, cos, sin
):
    own_rows, depth = middle.shape
    rows = own_rows // MICRO
    batch_rows = n_tp * rows
    line = n_dp // 2
    q_width, kv_width = q.shape[3], kv.shape[4]
    width = q_width + kv_width
    anywhere = pl.BlockSpec(memory_space=pl.ANY)
    vmem = pl.BlockSpec(memory_space=pltpu.VMEM)
    dma = pltpu.SemaphoreType.DMA
    gathered = jax.ShapeDtypeStruct((MICRO, n_tp, rows, depth), BF16)
    return pl.pallas_call(
        functools.partial(tail_kernel, n_dp, n_tp, group),
        in_specs=[anywhere] * 6 + [vmem] * 4 + [anywhere] * 4 + [vmem] * 6,
        out_specs=[vmem, anywhere, anywhere, vmem, vmem],
        out_shape=[
            jax.ShapeDtypeStruct((MICRO, batch_rows, width), BF16),
            gathered,
            gathered,
            jax.ShapeDtypeStruct((MICRO, rows, depth), BF16),
            jax.ShapeDtypeStruct((2, depth), F32),
        ],
        scratch_shapes=[
            pltpu.VMEM((2, depth // 2, n_tp * width), BF16),
            pltpu.VMEM((MICRO, n_tp, rows, depth), BF16),
            pltpu.VMEM((MICRO, n_tp, rows, depth), BF16),
            pltpu.VMEM((MICRO, rows, depth), F32),
            pltpu.VMEM((MICRO, rows, depth), BF16),
            pltpu.VMEM((MICRO, rows, depth), BF16),
            pltpu.VMEM((MICRO, n_tp, rows, q_width), BF16),
            pltpu.VMEM((MICRO, batch_rows, q_width), BF16),
            pltpu.VMEM((MICRO, 2, line, batch_rows, kv_width), BF16),
            pltpu.VMEM((MICRO, line, batch_rows, kv_width), BF16),
            pltpu.VMEM((MICRO, line, batch_rows, kv_width), BF16),
            pltpu.VMEM((MICRO, line, batch_rows, kv_width), BF16),
            pltpu.VMEM((MICRO, n_tp, rows, width), BF16),
            dma((7, 2)),
        ]
        + [dma((MICRO, n_tp))] * 8
        + [dma((MICRO,))] * 2
        + [dma((MICRO, line))] * 2
        + [dma((MICRO, n_tp))] * 2,
        compiler_params=pltpu.CompilerParams(
            collective_id=0, has_side_effects=True, vmem_limit_bytes=VMEM_LIMIT
        ),
        cost_estimate=hint(
            flops=10**10,
            bytes_accessed=10**8,
            transcendentals=0,
        ),
        name="tail",
    )(
        sums[0][1],
        sums[1][1],
        sums[0][0],
        sums[1][0],
        *arrived,
        seed,
        middle,
        x,
        gains,
        *out_w,
        *qkv_w,
        q,
        kv,
        qpos,
        kpos,
        cos,
        sin,
    )


def spread_kernel(rank_ref, out_ref, tok_ref, block_ref, grad_ref):
    block_ref[...] = out_ref[...]
    grad_ref[...] = tok_ref[...].astype(F32)


def spread(rank, out_rows, tok_rows):
    micro, n_tp, rows, depth = out_rows.shape
    here = pl.BlockSpec((1, 1, rows, depth), lambda m, k, r: (m, k, 0, 0))
    there = pl.BlockSpec((1, 1, rows, depth), lambda m, k, r: (m, r[0] ^ k, 0, 0))
    return pl.pallas_call(
        spread_kernel,
        grid_spec=pltpu.PrefetchScalarGridSpec(
            num_scalar_prefetch=1,
            grid=(micro, n_tp),
            in_specs=[here, here],
            out_specs=[there, there],
        ),
        out_shape=[
            jax.ShapeDtypeStruct(out_rows.shape, BF16),
            jax.ShapeDtypeStruct(out_rows.shape, F32),
        ],
        compiler_params=pltpu.CompilerParams(vmem_limit_bytes=VMEM_LIMIT),
        name="spread",
    )(rank, out_rows, tok_rows)


def per_device(
    n_dp,
    n_tp,
    tokens,
    cotangent,
    span_order,
    w_query,
    w_keyval,
    w_output,
    w_gateup,
    w_down,
    norm_gains,
    mean_query,
    square_query,
    mean_keyval,
    square_keyval,
    mean_output,
    square_output,
    mean_gateup,
    square_gateup,
    mean_down,
    square_down,
    mean_gains,
    square_gains,
):
    depth = tokens.shape[1]
    span_rows = 2 * CH
    block_rows = SEQS * span_rows // n_tp
    parts = span_rows // min(span_rows, block_rows)
    q_width = w_query.shape[1]
    kv_width = w_keyval.shape[1]
    hidden_width = w_down.shape[0]
    own_depth = w_query.shape[0]
    group = q_width // HD // (kv_width // (2 * HD))
    device = lax.axis_index("dp")
    rank = lax.axis_index("tp")
    line = n_dp // 2
    place, core = device // 2, device % 2

    def swap(value, k):
        return lax.ppermute(value, "tp", [(i, i ^ k) for i in range(n_tp)])

    def reorder(value):
        return jnp.concatenate(
            [lax.dynamic_slice_in_dim(value, rank ^ k, 1, axis=1) for k in range(n_tp)], axis=1
        )

    def gather_blocks(own):
        half = own.shape[0] // 2
        got = [own, swap(own, 1), swap(own, 2)]
        got.append(jnp.concatenate([swap(got[1][:half], 2), swap(got[2][half:], 1)], axis=0))
        return got + [swap(own, k) for k in range(4, n_tp)]

    def exchange(blocks):
        return [blocks[0]] + [swap(blocks[k], k) for k in range(1, n_tp)]

    def total_of(parts):
        total = parts[0].astype(F32)
        for part in parts[1:]:
            total = total + part.astype(F32)
        return total

    def gather_pair(owns):
        got = [owns, [swap(own, 1) for own in owns], [swap(own, 2) for own in owns]]
        got.append([swap(got[1][0], 2)] + [swap(own, 1) for own in got[2][1:]])
        return got + [[swap(own, k) for own in owns] for k in range(4, n_tp)]

    def scatter_pair(blocks):
        first = swap(blocks[0][3], 1)
        seconds = [swap(blocks[m][3], 2) for m in range(1, MICRO)]
        to_two = total_of([blocks[0][2], first]).astype(BF16)
        to_one = [total_of([blocks[m][1], seconds[m - 1]]).astype(BF16) for m in range(1, MICRO)]
        yield [to_two] + to_one
        totals = []
        for m in range(MICRO):
            one = blocks[m][1] if m == 0 else to_one[m - 1]
            two = to_two if m == 0 else blocks[m][2]
            far = [swap(blocks[m][k], k) for k in range(4, n_tp)]
            totals.append(total_of([blocks[m][0], swap(one, 1), swap(two, 2)] + far))
        yield totals

    def line_sum(other, own):
        met = lax.ppermute(other, "dp", [(i, i ^ 1) for i in range(n_dp)])
        yield [met]

        def share(index):
            index = jnp.clip(index, 0, line - 1)
            return lax.dynamic_index_in_dim(own, index, 0, False).astype(
                F32
            ) + lax.dynamic_index_in_dim(met, index, 0, False).astype(F32)

        sends = []
        for far in range(1, line):
            for way in (far, -far):
                sends.append((way, share(place + way).astype(BF16)))
        yield [value for _, value in sends]
        total = share(place)
        for far in range(1, line):
            arrived = []
            for way, value in sends:
                if abs(way) == far:
                    pairs = [
                        (i, i + 2 * way) for i in range(n_dp) if 0 <= i + 2 * way < n_dp
                    ]
                    arrived.append(lax.ppermute(value, "dp", pairs))
            if far <= 3:
                yield arrived
            for value in arrived:
                total = total + value.astype(F32)
        yield [total]

    def my_half(value):
        return lax.dynamic_slice_in_dim(value, core * (depth // 2), depth // 2, axis=0)

    def swap_cores(value):
        return lax.ppermute(value, "dp", [(i, i ^ 1) for i in range(n_dp)])

    def both_halves(near, far):
        return jnp.where(
            core == 0,
            jnp.concatenate([near, far], axis=1),
            jnp.concatenate([far, near], axis=1),
        )

    def after(value, *earlier):
        return lax.optimization_barrier((value,) + earlier)[0]

    attn_full = lax.all_gather(
        jnp.concatenate([w_query, w_keyval, w_output.T], axis=1), "dp", axis=0, tiled=True
    )
    qkv_full = attn_full[:, : q_width + kv_width]
    out_t_full = attn_full[:, q_width + kv_width :]
    gains_full = lax.all_gather(norm_gains, "dp", axis=1, tiled=True)

    offsets = jnp.arange(CH, dtype=jnp.int32)
    all_pos = (span_order[:, None] * CH + offsets[None, :]).reshape(n_dp, parts, -1)
    all_pos = jnp.stack([all_pos[:, (rank % parts) ^ p] for p in range(parts)], axis=1)
    own_pos = lax.dynamic_slice_in_dim(all_pos, device, 1).reshape(-1)
    all_pos = all_pos.reshape(-1)
    qpos, kpos = own_pos[:, None], all_pos[None, :]
    kv_kinds = [True, False] * (kv_width // (2 * HD))
    cos_t, sin_t = lane_tables(own_pos, [True] * (q_width // HD) + kv_kinds)

    x = reorder(tokens.reshape(MICRO, n_tp, block_rows, depth))
    seed = reorder(cotangent.reshape(MICRO, n_tp, block_rows, depth))
    batch_rows = SEQS * span_rows
    rows = MICRO * batch_rows
    gain_one, gain_two = gains_full[0:1], gains_full[1:2]
    x_rows = x.reshape(rows, depth)
    cos_k, sin_k = cos_t[:, q_width:], sin_t[:, q_width:]
    (kv,) = project(x_rows, gain_one, attn_full, q_width // kv_width, cos_k, sin_k, 0)
    kv = kv.reshape(MICRO, SEQS, span_rows, kv_width)
    q, attn_in = project(
        after(x_rows, kv), gain_one, attn_full, 0, cos_t[:, :q_width], sin_t[:, :q_width], 1
    )
    q = q.reshape(MICRO, SEQS, span_rows, q_width)
    out_t_full = after(out_t_full, q)
    kv_all = lax.all_gather(kv, "dp", axis=0, tiled=False)

    sub = min(SUB, hidden_width // CHUNKS)
    chunk = hidden_width // CHUNKS
    w_down_t = w_down.T
    mlp_full = []
    for c in range(CHUNKS):
        pieces = []
        for start in range(c * chunk, (c + 1) * chunk, sub):
            cols = slice(start, start + sub)
            pieces += [w_gateup[0][:, cols], w_gateup[1][:, cols], w_down_t[:, cols]]
        shard = jnp.concatenate(pieces, axis=1)
        mlp_full.append(lax.all_gather(shard, "dp", axis=0, tiled=True))

    attended = attend(qpos, kpos, q, kv_all, group)
    attended_blocks = attended.reshape(MICRO, n_tp, block_rows, q_width)
    out_near = my_half(out_t_full)
    out_near = jnp.concatenate([out_near] + [swap(out_near, k) for k in range(1, n_tp)], axis=1)
    out_far = swap_cores(out_near)
    heads_in = exchange([attended_blocks[:, k] for k in range(n_tp)])
    own_rows = MICRO * block_rows
    x_own = x[:, 0].reshape(own_rows, depth).astype(F32)
    heads_cat = jnp.concatenate([v.reshape(own_rows, q_width) for v in heads_in], axis=1)
    middle = x_own + both_halves(dot_nt(heads_cat, out_near), dot_nt(heads_cat, out_far))
    scale_two = mean_square_scale(middle)
    normed_two = middle * scale_two
    u_own = (normed_two * gain_two.astype(F32)).astype(BF16)
    batches = range(MICRO)
    gathered = [g.reshape(MICRO, block_rows, depth) for g in gather_blocks(u_own)]
    u = [jnp.concatenate([gathered[k][m] for k in range(n_tp)], axis=0) for m in batches]
    g = [seed[m].reshape(batch_rows, depth) for m in batches]

    qkv_half = after(my_half(qkv_full), u[0])
    quarter = depth // 4
    qkv_width = q_width + kv_width
    qkv_near = jnp.zeros((depth // 2, n_tp * qkv_width), BF16)
    qkv_near = lax.dynamic_update_slice(qkv_near, qkv_half, (0, 0))
    qkv_moves = [(k, i) for i in range(2) for k in range(1, min(n_tp, 3))]
    qkv_moves = [qkv_moves[:2], qkv_moves[2:]] + [
        [(k, i) for k in range(3, n_tp)] for i in range(2)
    ]

    def move_qkv(buffer):
        for k, i in qkv_moves.pop(0) if qkv_moves else []:
            got = swap(qkv_half[i * quarter : (i + 1) * quarter], k)
            buffer = lax.dynamic_update_slice(buffer, got, (i * quarter, k * qkv_width))
        return buffer

    def blocks_of(value):
        return [value[k * block_rows : (k + 1) * block_rows] for k in range(n_tp)]

    def own_part(value, m):
        return value[m * block_rows : (m + 1) * block_rows]

    core_index = core.astype(jnp.int32).reshape(1)
    gain_two_f = gain_two.astype(F32)
    gain_one_f = gain_one.astype(F32)
    cos_q, sin_q = cos_t[:, : group * HD], sin_t[:, : group * HD]
    cos_k, sin_k = cos_t[:, q_width:], sin_t[:, q_width:]
    gain_grads = [0.0, 0.0]
    sums = [None] * MICRO

    arrived = []

    def expand(c, m, *earlier):
        carry = (n_tp, sums[m - 1][1]) if c == CHUNKS - 1 and m else ()
        hid, dgu, y_low, du_low, *got = feed_forward(
            after(u[m], *earlier), g[m], mlp_full[c], sub, sums[m], *carry
        )
        sums[m] = (y_low, du_low)
        arrived.extend(got)
        return hid, dgu

    def close(hids, dgus, last, *earlier):
        carry = (n_tp, sums[-1][1]) if last else ()
        grads, *got = outer_products(
            [after(u[0], *earlier)] + u[1:], g, hids, dgus, own_depth, sub, *carry
        )
        arrived.extend(got)
        return grads, lax.psum_scatter(grads, "dp", scatter_dimension=0, tiled=False)

    chunk_grads = []
    earlier = []
    for c in range(CHUNKS - 1):
        hids, dgus = [], []
        for m in batches:
            hid, dgu = expand(c, m, *earlier)
            qkv_near = move_qkv(qkv_near)
            earlier = [hid, qkv_near]
            hids.append(hid)
            dgus.append(dgu)
        grads, owned = close(hids, dgus, False, *earlier)
        qkv_near = move_qkv(qkv_near)
        earlier = [grads, qkv_near]
        chunk_grads.append(owned)

    d_middles, d_mid_lows, d_attends, all_rows = [], [], [], []
    hids, dgus = [], []
    for m in batches:
        hid, dgu = expand(CHUNKS - 1, m, *earlier)
        qkv_near = move_qkv(qkv_near)
        earlier = [hid, qkv_near]
        if m == 0:
            qkv_far = swap_cores(qkv_near)
        hids.append(hid)
        dgus.append(dgu)
    grads, owned = close(hids, dgus, True, *earlier, qkv_far)
    chunk_grads.append(owned)
    tail_sums = [after(sums[0], grads)] + sums[1:]
    d_qkv, mid_rows, out_rows, tok_low, gain_part = tail(
        n_dp,
        n_tp,
        group,
        tail_sums,
        arrived,
        seed[:, 0].reshape(own_rows, depth),
        middle,
        x[:, 0].reshape(own_rows, depth),
        gains_full,
        (out_near, out_far),
        (qkv_near, qkv_far),
        q,
        kv_all,
        qpos,
        kpos,
        cos_t,
        sin_t,
    )
    mlp_grads = [v.reshape(own_depth, -1) for v in chunk_grads]
    qkv_shares, out_shares = attn_weight_grads(
        attn_in,
        mid_rows.reshape(rows, depth),
        d_qkv.reshape(rows, q_width + kv_width),
        attended.reshape(rows, q_width),
        own_depth,
    )
    tok_rows, out_grad, gain_grad = finish(n_dp, n_tp, tok_low, out_shares, gain_part)
    qkv_shares = after(qkv_shares, out_grad, *chunk_grads)
    qkv_grad = lax.psum_scatter(qkv_shares, "dp", scatter_dimension=0, tiled=False)
    block_output, grad_tokens = spread(rank.astype(jnp.int32).reshape(1), out_rows, tok_rows)
    block_output = block_output.reshape(rows, depth)
    grad_tokens = grad_tokens.reshape(rows, depth)
    small = small_steps(
        qkv_grad.reshape(1, own_depth, q_width + kv_width),
        out_grad,
        gain_grad,
        mean_query,
        square_query,
        w_query,
        mean_keyval,
        square_keyval,
        w_keyval,
        mean_output,
        square_output,
        w_output,
        mean_gains,
        square_gains,
        norm_gains,
    )
    return (
        (block_output, grad_tokens)
        + small[:12]
        + step_from_chunks(
            mlp_grads, mean_gateup, square_gateup, w_gateup, sub, 0, False, weight_decay
        )
        + step_from_chunks(mlp_grads, mean_down, square_down, w_down, sub, 2, True, weight_decay)
        + small[12:]
    )


def solution(mesh):
    rows_first = P("dp", "tp")
    cols_last = P("tp", "dp")
    stacked = P(None, "dp", "tp")
    gains = P(None, "dp")
    token_rows = P("dp", None)
    placed = (
        (token_rows, token_rows, P())
        + (rows_first, rows_first, cols_last, stacked, cols_last, gains)
        + (rows_first,) * 4
        + (cols_last,) * 2
        + (stacked,) * 2
        + (cols_last,) * 2
        + (gains,) * 2
    )
    results = (
        (token_rows, token_rows)
        + (rows_first,) * 8
        + (cols_last,) * 4
        + (stacked,) * 4
        + (cols_last,) * 4
        + (gains,) * 4
    )
    return jax.shard_map(
        functools.partial(per_device, mesh.shape["dp"], mesh.shape["tp"]),
        mesh=mesh,
        in_specs=placed,
        out_specs=results,
        check_vma=False,
    )
```
